32 devices in a mesh: parts: 2 (over y), expert: 4 (over z), tensor: 4 (over x, core).
Axes of the slice: x: 2, y: 2, z: 4, core: 2. Of those that a mesh axis runs over, the one named last changes fastest.
Arguments:
- tokens: bfloat16 [1, 128, 7168], P(None, ('parts', 'expert', 'tensor')), parts along dimension 1, may hold values from -6 to 6
- routes: int32 [1, 128, 8], P(None, ('parts', 'expert', 'tensor')), parts along dimension 1, may hold values from 0 to 15, as said below
- numerators: int32 [1, 128, 8], P(None, ('parts', 'expert', 'tensor')), parts along dimension 1, may hold values from 1 to 256
- place: int32 [32], P('parts'), parts along dimension 0, may hold values from 0 to 15, as said below
- base_in: bfloat16 [4, 7168, 2, 1024], P('expert', None, None, 'tensor'), may hold values from -0.0625 to 0.0625
- base_down: bfloat16 [4, 1024, 7168], P('expert', 'tensor'), may hold values from -0.1875 to 0.1875
- delta_in: bfloat16 [16, 7168, 128], P(('expert', 'tensor')), may hold values from -0.0625 to 0.0625
- delta_mid: bfloat16 [4, 4, 128, 2, 1024], P('expert', None, None, None, 'tensor'), may hold values from -0.5 to 0.5
- delta_down: bfloat16 [4, 4, 1024, 128], P('expert', None, 'tensor'), may hold values from -0.1875 to 0.1875
- delta_back: bfloat16 [16, 128, 7168], P(('expert', 'tensor')), may hold values from -0.5 to 0.5
Outputs:
- mixed: bfloat16 [1, 128, 7168], P(None, ('parts', 'expert', 'tensor')), parts along dimension 1
The draws below stay inside these ranges and needn't reach their ends.
There are 2 independent parts, one for each index of `parts`. The reference program is written for one: setup_inputs(seed, part) draws one part's arguments, and reference() takes and returns one part's arrays. A program takes and returns all parts, laid end to end along the dimension named above; an argument that names none is the same for every part. Nothing has to cross between parts.
Inputs may be any that keep to these rules, and one draw needn't show every extreme that they name: `routes`: each token's entries name different experts, 4 in each of exactly 2 clusters (the cluster of expert e is place[e] // 4). Among the 4 tokens of one device in one step no cluster is named by more than 4 tokens; in each step one cluster, drawn from the seed, is named by exactly 4 tokens of every device. `place`: each position holds exactly one expert.
All inputs are finite; a program needn't handle non-finite values.
Results may differ from the reference program's by a relative error of at most 0.015.
Values may be sent and summed in bfloat16 or wider, within the bound.
No kernel may reach another device: no remote copies, remote signals or barrier semaphores. Data moves between devices by JAX's collectives and lax.ppermute only.
A program may use at most 128 MiB of HBM per device.

```python
import jax
import jax.numpy as jnp
from jax import lax

D = 7168
FF = 1024
RANK = 128
TOP = 8
STEPS = 1
TOK_DEV = 4
CLUSTERS = 4
SLOTS = 4
EXPERTS = 16
BLOCKS = 16
TOKENS = 64
CPT = 2
PER_CLUSTER = 4
CAP = 4


def shared_place(key):
    return jax.random.permutation(jax.random.fold_in(key, 7), EXPERTS).astype(jnp.int32)


def random_order(key, shape, count):
    scores = jax.random.randint(key, shape + (count,), 0, 1 << 20) * count + jnp.arange(count, dtype=jnp.int32)
    return jnp.argsort(scores, axis=-1).astype(jnp.int32)


def draw_place(key, part):
    return shared_place(key)


def draw_routes(key, part):
    placed = shared_place(key)
    key = jax.random.fold_in(key, 3)
    keys = jax.random.split(key, 5)
    inverse = jnp.argsort(placed).astype(jnp.int32)
    hottest = jax.random.randint(keys[0], (STEPS, 1, 1, 1), 0, CLUSTERS).astype(jnp.int32)
    others = random_order(keys[1], (STEPS, BLOCKS), CLUSTERS - 1)
    others = others + (others >= hottest[:, :, :, 0]).astype(jnp.int32)
    ranks = random_order(keys[2], (STEPS, BLOCKS), TOK_DEV)
    is_hot = ranks < CAP
    first = ranks * CPT - jnp.minimum(ranks, CAP)
    picks = jnp.arange(CPT, dtype=jnp.int32)
    index = (first[..., None] + picks - is_hot[..., None].astype(jnp.int32)) % (CLUSTERS - 1)
    spread = jnp.broadcast_to(others[:, :, None, :], (STEPS, BLOCKS, TOK_DEV, CLUSTERS - 1))
    chosen = jnp.take_along_axis(spread, index, axis=-1)
    chosen = jnp.where(is_hot[..., None] & (picks == 0), hottest, chosen)
    members = random_order(keys[3], (STEPS, BLOCKS, TOK_DEV, CPT), SLOTS)[..., :PER_CLUSTER]
    positions = (chosen[..., None] * SLOTS + members).reshape(STEPS, BLOCKS, TOK_DEV, TOP)
    experts = inverse[positions]
    shuffle = random_order(keys[4], (STEPS, BLOCKS, TOK_DEV), TOP)
    experts = jnp.take_along_axis(experts, shuffle, axis=-1)
    return experts.reshape(STEPS, TOKENS, TOP).astype(jnp.int32)


def plant(array, key, smallest, high):
    longest = array.shape.index(max(array.shape))
    spots = []
    for shift in (0, 1):
        where = [jax.random.randint(jax.random.fold_in(key, axis), (), 0, length) for axis, length in enumerate(array.shape)]
        where[longest] = (where[longest] + shift) % array.shape[longest]
        spots.append(tuple(where))
    return array.at[spots[0]].set(smallest).at[spots[1]].set(high)


def level_of(stream_key, shape, cuts, smallest, top_value):
    factor_of, own = 1.0, jax.random.fold_in(stream_key, 6)
    for dim, parts in cuts:
        heights = jnp.exp(jax.random.uniform(jax.random.fold_in(own, dim), (parts,), jnp.float32, smallest / len(cuts), top_value / len(cuts)))
        factor_of = factor_of * jnp.repeat(heights, shape[dim] // parts).reshape([-1 if axis == dim else 1 for axis in range(len(shape))])
    return factor_of


def gaussian(rng, dims, deviation, most, cuts=(), kind=jnp.bfloat16):
    values = deviation * jax.random.normal(rng, dims, jnp.float32)
    if cuts:
        values = values * level_of(rng, dims, cuts, -0.22, 0.18)
    return jnp.clip(values, -most, most).astype(kind)


def setup_inputs(seed: int = 0, part: int = 0) -> dict:
    key_of = jax.random.split(jax.random.key(seed), 11)
    part_keys = jax.random.split(jax.random.fold_in(key_of[10], part), 11)
    tokens = gaussian(part_keys[0], (STEPS, TOKENS, D), 1.0, 6.0, ((1, 16),))
    routes = draw_routes(jax.random.fold_in(jax.random.fold_in(key_of[10], part), 71), part)
    numerators = plant(jax.random.randint(part_keys[2], (STEPS, TOKENS, TOP), 1, 257), jax.random.fold_in(part_keys[2], 1), 1, 256).astype(jnp.int32)
    place = draw_place(jax.random.fold_in(jax.random.fold_in(key_of[10], part), 71), part)
    base_in = gaussian(key_of[4], (CLUSTERS, D, 2, FF), D ** -0.5, 0.0625, ((0, 4), (3, 4)))
    base_down = gaussian(key_of[5], (CLUSTERS, FF, D), FF ** -0.5, 0.1875, ((0, 4), (1, 4)))
    delta_in = gaussian(key_of[6], (EXPERTS, D, RANK), D ** -0.5, 0.0625, ((0, 16),))
    delta_mid = gaussian(key_of[7], (CLUSTERS, SLOTS, RANK, 2, FF), RANK ** -0.5, 0.5, ((0, 4), (4, 4)))
    delta_down = gaussian(key_of[8], (CLUSTERS, SLOTS, FF, RANK), FF ** -0.5, 0.1875, ((0, 4), (2, 4)))
    delta_back = gaussian(key_of[9], (EXPERTS, RANK, D), RANK ** -0.5, 0.5, ((0, 16),))
    return {"tokens": tokens, "routes": routes, "numerators": numerators, "place": place, "base_in": base_in, "base_down": base_down, "delta_in": delta_in, "delta_mid": delta_mid, "delta_down": delta_down, "delta_back": delta_back}


def cluster_block(rows, table_c, present_c, gate_up, down, lift_in, middle, lower, lift_back):
    group_rows = BLOCKS * CAP
    order = jnp.argsort(1 - present_c.astype(jnp.int32), stable=True)[:group_rows].astype(jnp.int32)
    valid = jnp.arange(group_rows, dtype=jnp.int32) < jnp.sum(present_c.astype(jnp.int32))
    picked = jnp.where(valid[:, None], rows[order], jnp.zeros((), rows.dtype))
    scale = jnp.where(valid[:, None], table_c[order], jnp.zeros((), table_c.dtype)).astype(jnp.float32)
    projected = jnp.dot(picked, gate_up.reshape(D, 2 * FF), preferred_element_type=jnp.float32).reshape(group_rows, 2, FF)
    codes = jnp.einsum('rd,sdk->srk', picked.astype(jnp.float32), lift_in.astype(jnp.float32)).astype(jnp.bfloat16)
    lifted = jnp.einsum('srk,skgf->srgf', codes.astype(jnp.float32), middle.astype(jnp.float32))
    hidden = jax.nn.silu(projected[None, :, 0] + lifted[:, :, 0]) * (projected[None, :, 1] + lifted[:, :, 1])
    hidden_sum = jnp.sum(scale.T[:, :, None] * hidden, axis=0).astype(jnp.bfloat16)
    hidden_low = lax.optimization_barrier(hidden.astype(jnp.bfloat16))
    lowrank = jnp.einsum('srf,sfk->srk', hidden_low.astype(jnp.float32), lower.astype(jnp.float32))
    scaled = (scale.T[:, :, None] * lowrank).astype(jnp.bfloat16)
    grouped = hidden_sum.astype(jnp.float32).reshape(group_rows, SLOTS, FF // SLOTS)
    terms = jnp.einsum('rsf,sfd->srd', grouped, down.astype(jnp.float32).reshape(SLOTS, FF // SLOTS, D))
    terms = terms + jnp.einsum('srk,skd->srd', scaled.astype(jnp.float32), lift_back.astype(jnp.float32))
    rounded = lax.optimization_barrier(terms.astype(jnp.bfloat16))
    result = jnp.sum(rounded.astype(jnp.float32), axis=0).astype(jnp.bfloat16)
    return result, order, valid


def reference(tokens, routes, numerators, place, base_in, base_down, delta_in, delta_mid, delta_down, delta_back):
    lift_in = delta_in.reshape(CLUSTERS, SLOTS, D, RANK)
    lift_back = delta_back.reshape(CLUSTERS, SLOTS, RANK, D)
    outputs = []
    for step in range(STEPS):
        rows = tokens[step]
        position = place[routes[step]]
        cluster_of = position // SLOTS
        slot_of = position % SLOTS
        numerator = numerators[step].astype(jnp.float32)
        weight = (2.5 * numerator / jnp.sum(numerator, axis=-1, keepdims=True)).astype(jnp.bfloat16)
        cluster_hit = (cluster_of[..., None] == jnp.arange(CLUSTERS, dtype=jnp.int32)).astype(jnp.float32)
        slot_hit = (slot_of[..., None] == jnp.arange(SLOTS, dtype=jnp.int32)).astype(jnp.float32)
        table = jnp.einsum('nk,nkc,nks->cns', weight.astype(jnp.float32), cluster_hit, slot_hit).astype(jnp.bfloat16)
        present = jnp.max(cluster_hit, axis=1).T > 0.5

        def one_cluster(items):
            return cluster_block(rows, *items)

        results, orders, valids = lax.map(one_cluster, (table, present, base_in, base_down, lift_in, delta_mid, delta_down, lift_back))
        values = jnp.where(valids[..., None], results.astype(jnp.float32), jnp.zeros((), jnp.float32))
        total = jnp.zeros((TOKENS, D), jnp.float32).at[orders.reshape(-1)].add(values.reshape(-1, D))
        outputs.append(total.astype(jnp.bfloat16))
    return jnp.stack(outputs)
```

```python
import jax
import jax.numpy as jnp
from jax import lax
from jax.sharding import PartitionSpec as P


def lookup(table, index):
    keys = jnp.arange(table.shape[0], dtype=jnp.int32)
    return jnp.sum(jnp.where(index[..., None] == keys, table, 0), axis=-1)


def from_ahead(value, steps):
    size = lax.axis_size("expert")
    return lax.ppermute(value, "expert", [((i + steps) % size, i) for i in range(size)])


def swap(value, mask):
    size = lax.axis_size("tensor")
    return lax.ppermute(value, "tensor", [(i, i ^ mask) for i in range(size)])


def local(
    tokens,
    routes,
    numerators,
    place,
    base_in,
    base_down,
    delta_in,
    delta_mid,
    delta_down,
    delta_back,
):
    clusters = lax.axis_size("expert")
    members = lax.axis_size("tensor")
    chips = members // 2
    me = lax.axis_index("tensor")
    cluster = lax.axis_index("expert")
    count, width = tokens.shape[1:]
    top = routes.shape[2]
    group = clusters * count

    side = jnp.concatenate([routes[0], numerators[0]], axis=1).astype(jnp.bfloat16)
    side = jnp.pad(side, ((0, 0), (0, 128 - 2 * top)))
    packed = jnp.concatenate([tokens[0], side], axis=1)

    held = jnp.concatenate([packed] + [from_ahead(packed, k) for k in range(1, clusters)])
    held = jnp.concatenate([held] + [swap(held, 2 * m) for m in range(1, chips)])
    held = jnp.concatenate([held, swap(held, 1)])
    rows = held[:, :width]
    all_routes = held[:, width : width + top].astype(jnp.int32)
    numerator = held[:, width + top : width + 2 * top].astype(jnp.float32)

    position = lookup(place, all_routes)
    weight = (2.5 * numerator / jnp.sum(numerator, axis=-1, keepdims=True)).astype(jnp.bfloat16)
    target = cluster * members + jnp.arange(members, dtype=jnp.int32)
    scale = jnp.sum(
        jnp.where(position[None] == target[:, None, None], weight[None].astype(jnp.float32), 0.0), axis=-1
    )

    codes = jnp.dot(rows, delta_in[0], preferred_element_type=jnp.float32).astype(jnp.bfloat16)

    def block_of(m):
        return (m % 2) * chips + m // 2

    def reorder(value, m):
        if m == 0:
            return value
        blocks = value.reshape(members, group, value.shape[-1])
        return jnp.concatenate([blocks[i ^ block_of(m)] for i in range(members)])

    shared = jnp.stack([reorder(codes if m == 0 else swap(codes, m), m) for m in range(members)])
    by_slot = jnp.stack([lax.dynamic_index_in_dim(shared, s ^ me, 0, keepdims=False) for s in range(members)])

    projected = jnp.einsum("nd,dgf->ngf", rows, base_in[0], preferred_element_type=jnp.float32)
    lifted = jnp.einsum("srk,skgf->srgf", by_slot, delta_mid[0], preferred_element_type=jnp.float32)
    hidden = jax.nn.silu(projected[None, :, 0] + lifted[:, :, 0]) * (
        projected[None, :, 1] + lifted[:, :, 1]
    )
    hidden_sum = jnp.sum(scale[:, :, None] * hidden, axis=0).astype(jnp.bfloat16)
    partial_codes = jnp.einsum(
        "srf,sfk->srk", hidden.astype(jnp.bfloat16), delta_down[0], preferred_element_type=jnp.float32
    ).astype(jnp.bfloat16)
    lowrank = lax.dynamic_index_in_dim(partial_codes, me, 0, keepdims=False).astype(jnp.float32)
    for m in range(1, members):
        part = swap(lax.dynamic_index_in_dim(partial_codes, me ^ m, 0, keepdims=False), m)
        lowrank = lowrank + reorder(part, m).astype(jnp.float32)
    own_scale = lax.dynamic_index_in_dim(scale, me, 0, keepdims=False)
    scaled = (own_scale[:, None] * lowrank).astype(jnp.bfloat16)

    term = jnp.dot(hidden_sum, base_down[0], preferred_element_type=jnp.float32)
    term = (term + jnp.dot(scaled, delta_back[0], preferred_element_type=jnp.float32)).astype(jnp.bfloat16)

    half = chips * group
    total = (term[:half].astype(jnp.float32) + swap(term[half:], 1).astype(jnp.float32)).astype(jnp.bfloat16)
    parts = total.reshape(chips, group, width)
    total = parts[0].astype(jnp.float32)
    for m in range(1, chips):
        total = total + swap(parts[m], 2 * m).astype(jnp.float32)
    parts = total.astype(jnp.bfloat16).reshape(clusters, count, width)
    mixed = parts[0].astype(jnp.float32)
    for k in range(1, clusters):
        mixed = mixed + from_ahead(parts[k], clusters - k).astype(jnp.float32)
    return mixed.astype(jnp.bfloat16)[None]


def solution(mesh):
    placed = (
        P(None, ("parts", "expert", "tensor"), None),
        P(None, ("parts", "expert", "tensor"), None),
        P(None, ("parts", "expert", "tensor"), None),
        P("parts"),
        P("expert", None, None, "tensor"),
        P("expert", "tensor", None),
        P(("expert", "tensor"), None, None),
        P("expert", None, None, None, "tensor"),
        P("expert", None, "tensor", None),
        P(("expert", "tensor"), None, None),
    )
    return jax.shard_map(
        local,
        mesh=mesh,
        in_specs=placed,
        out_specs=P(None, ("parts", "expert", "tensor"), None),
        check_vma=False,
    )
```

```python
import jax
import jax.numpy as jnp
from jax import lax
from jax.experimental.layout import Layout, with_layout_constraint
from jax.sharding import PartitionSpec as P

CHUNKS = 2


def by_rows(value):
    return with_layout_constraint(value, Layout((0, 1)))


def lookup(table, index):
    keys = jnp.arange(table.shape[0], dtype=jnp.int32)
    return jnp.sum(jnp.where(index[..., None] == keys, table, 0), axis=-1)


def from_ahead(value, steps):
    size = lax.axis_size("expert")
    return lax.ppermute(value, "expert", [((i + steps) % size, i) for i in range(size)])


def swap(value, mask):
    size = lax.axis_size("tensor")
    return lax.ppermute(value, "tensor", [(i, i ^ mask) for i in range(size)])


def local(
    tokens,
    routes,
    numerators,
    place,
    base_in,
    base_down,
    delta_in,
    delta_mid,
    delta_down,
    delta_back,
):
    clusters = lax.axis_size("expert")
    members = lax.axis_size("tensor")
    chips = members // 2
    me = lax.axis_index("tensor")
    cluster = lax.axis_index("expert")
    count, width = tokens.shape[1:]
    top = routes.shape[2]
    group = clusters * count

    chunk = width // CHUNKS
    side = jnp.concatenate([routes[0], numerators[0]], axis=1).astype(jnp.bfloat16)
    side = jnp.pad(side, ((0, 0), (0, 128 - 2 * top)))
    pieces = [tokens[0][:, c * chunk : (c + 1) * chunk] for c in range(CHUNKS)]
    pieces[0] = jnp.concatenate([pieces[0], side], axis=1)

    gathered = []
    for piece in pieces:
        held = jnp.concatenate([piece] + [from_ahead(piece, k) for k in range(1, clusters)])
        held = jnp.concatenate([held] + [swap(held, 2 * m) for m in range(1, chips)])
        gathered.append(by_rows(jnp.concatenate([held, swap(held, 1)])))
    side = by_rows(gathered[0][:, chunk:])
    rows = [held[:, :chunk] for held in gathered]
    all_routes = side[:, :top].astype(jnp.int32)
    numerator = side[:, top : 2 * top].astype(jnp.float32)

    position = lookup(place, all_routes)
    weight = (2.5 * numerator / jnp.sum(numerator, axis=-1, keepdims=True)).astype(jnp.bfloat16)
    target = cluster * members + jnp.arange(members, dtype=jnp.int32)
    scale = jnp.sum(
        jnp.where(position[None] == target[:, None, None], weight[None].astype(jnp.float32), 0.0), axis=-1
    )

    codes = sum(
        jnp.dot(rows[c], delta_in[0, c * chunk : (c + 1) * chunk], preferred_element_type=jnp.float32)
        for c in range(CHUNKS)
    ).astype(jnp.bfloat16)

    def block_of(m):
        return (m % 2) * chips + m // 2

    def reorder(value, m):
        if m == 0:
            return value
        blocks = value.reshape(members, group, value.shape[-1])
        return jnp.concatenate([blocks[i ^ block_of(m)] for i in range(members)])

    shared = jnp.stack([reorder(codes if m == 0 else swap(codes, m), m) for m in range(members)])
    by_slot = jnp.stack([lax.dynamic_index_in_dim(shared, s ^ me, 0, keepdims=False) for s in range(members)])

    projected = sum(
        jnp.einsum(
            "nd,dgf->ngf", rows[c], base_in[0, c * chunk : (c + 1) * chunk], preferred_element_type=jnp.float32
        )
        for c in range(CHUNKS)
    )
    lifted = jnp.einsum("srk,skgf->srgf", by_slot, delta_mid[0], preferred_element_type=jnp.float32)
    hidden = jax.nn.silu(projected[None, :, 0] + lifted[:, :, 0]) * (
        projected[None, :, 1] + lifted[:, :, 1]
    )
    hidden_sum = jnp.sum(scale[:, :, None] * hidden, axis=0).astype(jnp.bfloat16)
    partial_codes = jnp.einsum(
        "srf,sfk->srk", hidden.astype(jnp.bfloat16), delta_down[0], preferred_element_type=jnp.float32
    ).astype(jnp.bfloat16)
    lowrank = lax.dynamic_index_in_dim(partial_codes, me, 0, keepdims=False).astype(jnp.float32)
    for m in range(1, members):
        part = swap(lax.dynamic_index_in_dim(partial_codes, me ^ m, 0, keepdims=False), m)
        lowrank = lowrank + reorder(part, m).astype(jnp.float32)
    own_scale = lax.dynamic_index_in_dim(scale, me, 0, keepdims=False)
    scaled = (own_scale[:, None] * lowrank).astype(jnp.bfloat16)

    half = chips * group
    outputs = []
    for c in range(CHUNKS):
        columns = slice(c * chunk, (c + 1) * chunk)
        term = jnp.dot(hidden_sum, base_down[0, :, columns], preferred_element_type=jnp.float32)
        term = term + jnp.dot(scaled, delta_back[0, :, columns], preferred_element_type=jnp.float32)
        term = term.astype(jnp.bfloat16)
        total = (term[:half].astype(jnp.float32) + swap(term[half:], 1).astype(jnp.float32)).astype(jnp.bfloat16)
        parts = total.reshape(chips, group, chunk)
        total = parts[0].astype(jnp.float32)
        for m in range(1, chips):
            total = total + swap(parts[m], 2 * m).astype(jnp.float32)
        parts = total.astype(jnp.bfloat16).reshape(clusters, count, chunk)
        mixed = parts[0].astype(jnp.float32)
        for k in range(1, clusters):
            mixed = mixed + from_ahead(parts[k], clusters - k).astype(jnp.float32)
        outputs.append(mixed.astype(jnp.bfloat16))
    return jnp.concatenate(outputs, axis=1)[None]


def solution(mesh):
    placed = (
        P(None, ("parts", "expert", "tensor"), None),
        P(None, ("parts", "expert", "tensor"), None),
        P(None, ("parts", "expert", "tensor"), None),
        P("parts"),
        P("expert", None, None, "tensor"),
        P("expert", "tensor", None),
        P(("expert", "tensor"), None, None),
        P("expert", None, None, None, "tensor"),
        P("expert", None, "tensor", None),
        P(("expert", "tensor"), None, None),
    )
    return jax.shard_map(
        local,
        mesh=mesh,
        in_specs=placed,
        out_specs=P(None, ("parts", "expert", "tensor"), None),
        check_vma=False,
    )
```

```python
import functools

import jax
import jax.numpy as jnp
from jax import lax
from jax.experimental import pallas as pl
from jax.experimental.pallas import tpu as pltpu
from jax.experimental.layout import Layout, with_layout_constraint
from jax.sharding import PartitionSpec as P

VMEM = pl.BlockSpec(memory_space=pltpu.VMEM)


def by_rows(value):
    return with_layout_constraint(value, Layout((0, 1)))


def lookup(table, index):
    keys = jnp.arange(table.shape[0], dtype=jnp.int32)
    return jnp.sum(jnp.where(index[..., None] == keys, table, 0), axis=-1)


def trade(value, even, odd):
    members = lax.axis_size("tensor")
    pairs = []
    for e in range(lax.axis_size("expert")):
        for t in range(members):
            along, across = odd if t % 2 else even
            pairs.append((e * members + t, (e ^ along) * members + (t ^ across)))
    return lax.ppermute(value, ("expert", "tensor"), pairs)


def halves(size):
    masks = []
    while size > 1:
        size //= 2
        masks.append(size)
    return masks


def ordered(flip, first, second):
    return jnp.where(flip, second, first), jnp.where(flip, first, second)


def split_kernel(interleaved, split, wide):
    depth, _, columns = interleaved.shape
    step = 64
    flat = interleaved.reshape(2 * depth, columns)

    @pl.loop(0, depth // step)
    def _(i):
        rows = pl.ds(pl.multiple_of(step * i, step), step)
        both = pl.ds(pl.multiple_of(2 * step * i, 2 * step), 2 * step)
        for lane in range(0, columns, 128):
            tile = wide.at[lane // 128]
            tile[...] = flat[both, lane : lane + 128].astype(jnp.float32)
            for half in range(2):
                split[rows, half * columns + lane : half * columns + lane + 128] = tile[
                    pl.ds(half, step, stride=2), :
                ].astype(jnp.bfloat16)


def split_gate_up(base):
    depth, _, columns = base.shape
    block = 512
    return pl.pallas_call(
        split_kernel,
        grid=(depth // block,),
        out_shape=jax.ShapeDtypeStruct((depth, 2 * columns), jnp.bfloat16),
        in_specs=[pl.BlockSpec((block, 2, columns), lambda i: (i, 0, 0))],
        out_specs=pl.BlockSpec((block, 2 * columns), lambda i: (i, 0)),
        scratch_shapes=[pltpu.VMEM((columns // 128, 128, 128), jnp.float32)],
        compiler_params=pltpu.CompilerParams(vmem_limit_bytes=16 << 20),
        cost_estimate=pl.CostEstimate(flops=0, bytes_accessed=4 * base.size, transcendentals=0),
    )(base)


def product_kernel(other, x, weights, out):
    core = lax.axis_index("tensor") % 2
    start = (1 - core) if other else core
    depth = weights.shape[0] // 2
    rows = weights[pl.ds(pl.multiple_of(start * depth, depth), depth), :]
    out[...] = jnp.dot(x[:, :depth], rows, preferred_element_type=jnp.float32)


def half_product(x, weights, other):
    depth, columns = weights.shape
    return pl.pallas_call(
        functools.partial(product_kernel, other),
        out_shape=jax.ShapeDtypeStruct((x.shape[0], columns), jnp.float32),
        in_specs=[VMEM, VMEM],
        out_specs=VMEM,
        compiler_params=pltpu.CompilerParams(vmem_limit_bytes=16 << 20),
        cost_estimate=pl.CostEstimate(
            flops=x.shape[0] * depth * columns, bytes_accessed=weights.size, transcendentals=0
        ),
    )(x, weights)


def local(
    tokens,
    routes,
    numerators,
    place,
    base_in,
    base_down,
    delta_in,
    delta_mid,
    delta_down,
    delta_back,
):
    clusters = lax.axis_size("expert")
    members = lax.axis_size("tensor")
    me = lax.axis_index("tensor")
    cluster = lax.axis_index("expert")
    core = me % 2
    count, width = tokens.shape[1:]
    top = routes.shape[2]
    half = width // 2

    along, across = halves(clusters), halves(members // 2)
    shared, paired = along[: len(along) - len(across)], along[len(along) - len(across) :]

    side = jnp.concatenate([routes[0], numerators[0]], axis=1).astype(jnp.bfloat16)
    side = jnp.pad(side, ((0, 0), (0, 128 - 2 * top)))
    left, right = (jnp.concatenate([tokens[0, :, :half], side], axis=1), jnp.concatenate([tokens[0, :, half:], side], axis=1))
    mine, theirs = ordered(core == 1, left, right)

    held = jnp.concatenate(ordered(core == 1, mine, trade(theirs, (0, 1), (0, 1))))
    for mask in shared:
        held = jnp.concatenate([held, trade(held, (mask, 0), (mask, 0))])
    for z, x in zip(paired, across):
        size = held.shape[0]
        flag = (me // (2 * x)) % 2 == 1
        held = jnp.concatenate(ordered((core == 0) & flag, held, trade(held, (0, 2 * x), (z, 0))))
        low, high = ordered((core == 1) & flag, held, trade(held, (z, 0), (0, 2 * x)))
        inner = ordered(core == 1, low[size:], high[:size])
        held = jnp.concatenate([low[:size], *inner, high[size:]])
    held = by_rows(held)
    rest = by_rows(trade(held, (0, 1), (0, 1)))

    split = split_gate_up(base_in[0])
    projected = half_product(held, split, False) + half_product(rest, split, True)
    codes = (half_product(held, delta_in[0], False) + half_product(rest, delta_in[0], True)).astype(jnp.bfloat16)

    side = by_rows(held[:, half:])
    all_routes = side[:, :top].astype(jnp.int32)
    numerator = side[:, top : 2 * top].astype(jnp.float32)
    position = lookup(place, all_routes)
    weight = (2.5 * numerator / jnp.sum(numerator, axis=-1, keepdims=True)).astype(jnp.bfloat16)
    target = cluster * members + jnp.arange(members, dtype=jnp.int32)
    scale = jnp.sum(
        jnp.where(position[None] == target[:, None, None], weight[None].astype(jnp.float32), 0.0), axis=-1
    )

    codes = jnp.stack([codes if m == 0 else trade(codes, (0, m), (0, m)) for m in range(members)])
    by_slot = jnp.stack([lax.dynamic_index_in_dim(codes, s ^ me, 0, keepdims=False) for s in range(members)])

    lifted = jnp.einsum("srk,skgf->srgf", by_slot, delta_mid[0], preferred_element_type=jnp.float32)
    part = projected.shape[1] // 2
    hidden = jax.nn.silu(projected[None, :, :part] + lifted[:, :, 0]) * (
        projected[None, :, part:] + lifted[:, :, 1]
    )
    hidden_sum = jnp.sum(scale[:, :, None] * hidden, axis=0).astype(jnp.bfloat16)
    partial_codes = jnp.einsum(
        "srf,sfk->srk", hidden.astype(jnp.bfloat16), delta_down[0], preferred_element_type=jnp.float32
    ).astype(jnp.bfloat16)
    lowrank = lax.dynamic_index_in_dim(partial_codes, me, 0, keepdims=False).astype(jnp.float32)
    for m in range(1, members):
        sent = lax.dynamic_index_in_dim(partial_codes, me ^ m, 0, keepdims=False)
        lowrank = lowrank + trade(sent, (0, m), (0, m)).astype(jnp.float32)
    own_scale = lax.dynamic_index_in_dim(scale, me, 0, keepdims=False)
    scaled = (own_scale[:, None] * lowrank).astype(jnp.bfloat16)

    term = jnp.dot(hidden_sum, base_down[0], preferred_element_type=jnp.float32)
    term = (term + jnp.dot(scaled, delta_back[0], preferred_element_type=jnp.float32)).astype(jnp.bfloat16)

    def add(kept, received):
        return (kept.astype(jnp.float32) + received.astype(jnp.float32)).astype(jnp.bfloat16)

    sent = lax.dynamic_slice_in_dim(term, (1 - core) * half, half, axis=1)
    kept = lax.dynamic_slice_in_dim(term, core * half, half, axis=1)
    total = add(kept, trade(sent, (0, 1), (0, 1)))
    for z, x in reversed(list(zip(paired, across))):
        flag = (me // (2 * x)) % 2 == 1
        size = total.shape[0] // 4
        blocks = [total[i * size : (i + 1) * size] for i in range(4)]
        inner = ordered(core == 1, blocks[1], blocks[2])
        kept, sent = ordered(
            (core == 1) & flag,
            jnp.concatenate([blocks[0], inner[0]]),
            jnp.concatenate([inner[1], blocks[3]]),
        )
        total = add(kept, trade(sent, (z, 0), (0, 2 * x)))
        kept, sent = ordered((core == 0) & flag, total[:size], total[size:])
        total = add(kept, trade(sent, (0, 2 * x), (z, 0)))
    for mask in reversed(shared):
        size = total.shape[0] // 2
        total = add(total[:size], trade(total[size:], (mask, 0), (mask, 0)))
    kept, sent = ordered(core == 1, total[:count], total[count:])
    mixed = ordered(core == 1, kept, trade(sent, (0, 1), (0, 1)))
    return jnp.concatenate(mixed, axis=1)[None]


def solution(mesh):
    placed = (
        P(None, ("parts", "expert", "tensor"), None),
        P(None, ("parts", "expert", "tensor"), None),
        P(None, ("parts", "expert", "tensor"), None),
        P("parts"),
        P("expert", None, None, "tensor"),
        P("expert", "tensor", None),
        P(("expert", "tensor"), None, None),
        P("expert", None, None, None, "tensor"),
        P("expert", None, "tensor", None),
        P(("expert", "tensor"), None, None),
    )
    return jax.shard_map(
        local,
        mesh=mesh,
        in_specs=placed,
        out_specs=P(None, ("parts", "expert", "tensor"), None),
        check_vma=False,
    )
```

```python
import jax
import jax.numpy as jnp
from jax import lax
from jax.experimental import pallas as pl
from jax.experimental.pallas import tpu as pltpu
from jax.experimental.layout import Layout, with_layout_constraint
from jax.sharding import PartitionSpec as P

VMEM = pl.BlockSpec(memory_space=pltpu.VMEM)
HBM = pl.BlockSpec(memory_space=pltpu.HBM)


def by_rows(value):
    return with_layout_constraint(value, Layout((0, 1)))


def lookup(table, index):
    keys = jnp.arange(table.shape[0], dtype=jnp.int32)
    return jnp.sum(jnp.where(index[..., None] == keys, table, 0), axis=-1)


def trade(value, even, odd):
    members = lax.axis_size("tensor")
    pairs = []
    for e in range(lax.axis_size("expert")):
        for t in range(members):
            along, across = odd if t % 2 else even
            pairs.append((e * members + t, (e ^ along) * members + (t ^ across)))
    return lax.ppermute(value, ("expert", "tensor"), pairs)


def halves(size):
    masks = []
    while size > 1:
        size //= 2
        masks.append(size)
    return masks


def ordered(flip, first, second):
    return jnp.where(flip, second, first), jnp.where(flip, first, second)


def code_kernel(x, table, out, weights, sems):
    depth = weights.shape[0]
    step = depth // sems.shape[0]
    copies = [
        pltpu.make_async_copy(table.at[pl.ds(k, step)], weights.at[pl.ds(k, step)], sems.at[k // step])
        for k in range(0, depth, step)
    ]
    for copy in copies:
        copy.start()
    total = jnp.zeros(out.shape, jnp.float32)
    for k in range(0, depth, step):
        copies[k // step].wait()
        total += jnp.dot(x[:, k : k + step], weights[k : k + step, :], preferred_element_type=jnp.float32)
    out[...] = total.astype(out.dtype)


def code_product(x, table):
    depth, rank = table.shape
    return pl.pallas_call(
        code_kernel,
        out_shape=jax.ShapeDtypeStruct((x.shape[0], rank), jnp.bfloat16),
        in_specs=[VMEM, HBM],
        out_specs=VMEM,
        scratch_shapes=[pltpu.VMEM(table.shape, table.dtype), pltpu.SemaphoreType.DMA((4,))],
        compiler_params=pltpu.CompilerParams(vmem_limit_bytes=32 << 20),
        cost_estimate=pl.CostEstimate(
            flops=2 * x.shape[0] * depth * rank, bytes_accessed=2 * table.size, transcendentals=0
        ),
    )(x, table)


def gate_up_kernel(x, base, out, weights, sems):
    depth, _, columns = weights.shape
    step = depth // sems.shape[0]
    copies = [
        pltpu.make_async_copy(base.at[pl.ds(k, step)], weights.at[pl.ds(k, step)], sems.at[k // step])
        for k in range(0, depth, step)
    ]
    for copy in copies:
        copy.start()
    row = lax.broadcasted_iota(jnp.int32, (128, 512), 0)
    column = lax.broadcasted_iota(jnp.int32, (128, 512), 1)
    target = 2 * row + jnp.where(column < 256, 0, 257)
    spread = jnp.where(column == target, 1.0, 0.0).astype(jnp.bfloat16)
    flat = weights.reshape(2 * depth, columns)
    total = jnp.zeros(out.shape, jnp.float32)
    for k in range(0, depth, step):
        wide = [
            jnp.dot(x[:, i : i + 128], spread, preferred_element_type=jnp.float32).astype(jnp.bfloat16)
            for i in range(k, k + step, 128)
        ]
        even = jnp.concatenate([part[:, :256] for part in wide], axis=1)
        odd = jnp.concatenate([part[:, 256:] for part in wide], axis=1)
        copies[k // step].wait()
        total += jnp.dot(
            jnp.concatenate([even, odd]), flat[2 * k : 2 * (k + step), :], preferred_element_type=jnp.float32
        )
    out[...] = total


def gate_up_product(x, base):
    depth, _, columns = base.shape
    return pl.pallas_call(
        gate_up_kernel,
        out_shape=jax.ShapeDtypeStruct((2 * x.shape[0], columns), jnp.float32),
        in_specs=[VMEM, HBM],
        out_specs=VMEM,
        scratch_shapes=[pltpu.VMEM(base.shape, base.dtype), pltpu.SemaphoreType.DMA((depth // 512,))],
        compiler_params=pltpu.CompilerParams(vmem_limit_bytes=32 << 20),
        cost_estimate=pl.CostEstimate(
            flops=4 * x.shape[0] * depth * columns, bytes_accessed=2 * base.size, transcendentals=0
        ),
    )(x, base)


def local(
    tokens,
    routes,
    numerators,
    place,
    base_in,
    base_down,
    delta_in,
    delta_mid,
    delta_down,
    delta_back,
):
    clusters = lax.axis_size("expert")
    members = lax.axis_size("tensor")
    me = lax.axis_index("tensor")
    cluster = lax.axis_index("expert")
    core = me % 2
    count, width = tokens.shape[1:]
    top = routes.shape[2]

    along, across = halves(clusters), halves(members // 2)
    shared, paired = along[: len(along) - len(across)], along[len(along) - len(across) :]

    side = jnp.concatenate([routes[0], numerators[0]], axis=1).astype(jnp.bfloat16)
    held = jnp.concatenate([tokens[0], jnp.pad(side, ((0, 0), (0, 128 - 2 * top)))], axis=1)

    for mask in shared:
        held = jnp.concatenate([held, trade(held, (mask, 0), (mask, 0))])
    for z, x in zip(paired, across):
        size = held.shape[0]
        flag = (me // (2 * x)) % 2 == 1
        held = jnp.concatenate(ordered((core == 0) & flag, held, trade(held, (0, 2 * x), (z, 0))))
        low, high = ordered((core == 1) & flag, held, trade(held, (z, 0), (0, 2 * x)))
        inner = ordered(core == 1, low[size:], high[:size])
        held = jnp.concatenate([low[:size], *inner, high[size:]])
    held = by_rows(jnp.concatenate(ordered(core == 1, held, trade(held, (0, 1), (0, 1)))))

    codes = code_product(held, delta_in[0])
    projected = gate_up_product(held, base_in[0])

    side = by_rows(held[:, width:])
    all_routes = side[:, :top].astype(jnp.int32)
    numerator = side[:, top : 2 * top].astype(jnp.float32)
    position = lookup(place, all_routes)
    weight = (2.5 * numerator / jnp.sum(numerator, axis=-1, keepdims=True)).astype(jnp.bfloat16)
    target = cluster * members + jnp.arange(members, dtype=jnp.int32)
    scale = jnp.sum(
        jnp.where(position[None] == target[:, None, None], weight[None].astype(jnp.float32), 0.0), axis=-1
    )

    codes = jnp.stack([codes if m == 0 else trade(codes, (0, m), (0, m)) for m in range(members)])
    by_slot = jnp.stack([lax.dynamic_index_in_dim(codes, s ^ me, 0, keepdims=False) for s in range(members)])

    lifted = jnp.einsum("srk,skgf->srgf", by_slot, delta_mid[0], preferred_element_type=jnp.float32)
    total = held.shape[0]
    hidden = jax.nn.silu(projected[None, :total] + lifted[:, :, 0]) * (projected[None, total:] + lifted[:, :, 1])
    hidden_sum = jnp.sum(scale[:, :, None] * hidden, axis=0).astype(jnp.bfloat16)
    partial_codes = jnp.einsum(
        "srf,sfk->srk", hidden.astype(jnp.bfloat16), delta_down[0], preferred_element_type=jnp.float32
    ).astype(jnp.bfloat16)
    lowrank = lax.dynamic_index_in_dim(partial_codes, me, 0, keepdims=False).astype(jnp.float32)
    for m in range(1, members):
        sent = lax.dynamic_index_in_dim(partial_codes, me ^ m, 0, keepdims=False)
        lowrank = lowrank + trade(sent, (0, m), (0, m)).astype(jnp.float32)
    own_scale = lax.dynamic_index_in_dim(scale, me, 0, keepdims=False)
    scaled = (own_scale[:, None] * lowrank).astype(jnp.bfloat16)

    term = jnp.dot(hidden_sum, base_down[0], preferred_element_type=jnp.float32)
    term = (term + jnp.dot(scaled, delta_back[0], preferred_element_type=jnp.float32)).astype(jnp.bfloat16)

    def add(kept, received):
        return (kept.astype(jnp.float32) + received.astype(jnp.float32)).astype(jnp.bfloat16)

    kept, sent = ordered(core == 1, term[: total // 2], term[total // 2 :])
    total = add(kept, trade(sent, (0, 1), (0, 1)))
    for z, x in reversed(list(zip(paired, across))):
        flag = (me // (2 * x)) % 2 == 1
        size = total.shape[0] // 4
        blocks = [total[i * size : (i + 1) * size] for i in range(4)]
        inner = ordered(core == 1, blocks[1], blocks[2])
        kept, sent = ordered(
            (core == 1) & flag,
            jnp.concatenate([blocks[0], inner[0]]),
            jnp.concatenate([inner[1], blocks[3]]),
        )
        total = add(kept, trade(sent, (z, 0), (0, 2 * x)))
        kept, sent = ordered((core == 0) & flag, total[:size], total[size:])
        total = add(kept, trade(sent, (0, 2 * x), (z, 0)))
    for mask in reversed(shared):
        size = total.shape[0] // 2
        total = add(total[:size], trade(total[size:], (mask, 0), (mask, 0)))
    return total[None]


def solution(mesh):
    placed = (
        P(None, ("parts", "expert", "tensor"), None),
        P(None, ("parts", "expert", "tensor"), None),
        P(None, ("parts", "expert", "tensor"), None),
        P("parts"),
        P("expert", None, None, "tensor"),
        P("expert", "tensor", None),
        P(("expert", "tensor"), None, None),
        P("expert", None, None, None, "tensor"),
        P("expert", None, "tensor", None),
        P(("expert", "tensor"), None, None),
    )
    return jax.shard_map(
        local,
        mesh=mesh,
        in_specs=placed,
        out_specs=P(None, ("parts", "expert", "tensor"), None),
        check_vma=False,
    )
```

```python
import jax
import jax.numpy as jnp
from jax import lax
from jax.experimental import pallas as pl
from jax.experimental.pallas import tpu as pltpu
from jax.experimental.layout import Layout, with_layout_constraint
from jax.sharding import PartitionSpec as P

VMEM = pl.BlockSpec(memory_space=pltpu.VMEM)
HBM = pl.BlockSpec(memory_space=pltpu.HBM)


def in_hbm(value):
    return pltpu.with_memory_space_constraint(value, pltpu.HBM)


def by_rows(value):
    return with_layout_constraint(value, Layout((0, 1)))


def lookup(table, index):
    keys = jnp.arange(table.shape[0], dtype=jnp.int32)
    return jnp.sum(jnp.where(index[..., None] == keys, table, 0), axis=-1)


def trade(value, even, odd):
    members = lax.axis_size("tensor")
    pairs = []
    for e in range(lax.axis_size("expert")):
        for t in range(members):
            along, across = odd if t % 2 else even
            pairs.append((e * members + t, (e ^ along) * members + (t ^ across)))
    return lax.ppermute(value, ("expert", "tensor"), pairs)


def halves(size):
    masks = []
    while size > 1:
        size //= 2
        masks.append(size)
    return masks


def ordered(flip, first, second):
    return jnp.where(flip, second, first), jnp.where(flip, first, second)


def code_kernel(x, table, out, weights, sems):
    depth = weights.shape[0]
    step = depth // sems.shape[0]
    copies = [
        pltpu.make_async_copy(table.at[pl.ds(k, step)], weights.at[pl.ds(k, step)], sems.at[k // step])
        for k in range(0, depth, step)
    ]
    for copy in copies:
        copy.start()
    total = jnp.zeros(out.shape, jnp.float32)
    for k in range(0, depth, step):
        copies[k // step].wait()
        total += jnp.dot(x[:, k : k + step], weights[k : k + step, :], preferred_element_type=jnp.float32)
    out[...] = total.astype(out.dtype)


def code_product(x, table):
    depth, rank = table.shape
    return pl.pallas_call(
        code_kernel,
        out_shape=jax.ShapeDtypeStruct((x.shape[0], rank), jnp.bfloat16),
        in_specs=[VMEM, HBM],
        out_specs=VMEM,
        scratch_shapes=[pltpu.VMEM(table.shape, table.dtype), pltpu.SemaphoreType.DMA((4,))],
        compiler_params=pltpu.CompilerParams(vmem_limit_bytes=32 << 20),
        cost_estimate=pl.CostEstimate(
            flops=2 * x.shape[0] * depth * rank, bytes_accessed=2 * table.size, transcendentals=0
        ),
    )(x, in_hbm(table))


def gate_up_kernel(x, base, out, weights, sems):
    depth, _, columns = weights.shape
    step = depth // sems.shape[0]
    copies = [
        pltpu.make_async_copy(base.at[pl.ds(k, step)], weights.at[pl.ds(k, step)], sems.at[k // step])
        for k in range(0, depth, step)
    ]
    for copy in copies:
        copy.start()
    row = lax.broadcasted_iota(jnp.int32, (128, 512), 0)
    column = lax.broadcasted_iota(jnp.int32, (128, 512), 1)
    target = 2 * row + jnp.where(column < 256, 0, 257)
    spread = jnp.where(column == target, 1.0, 0.0).astype(jnp.bfloat16)
    flat = weights.reshape(2 * depth, columns)
    total = jnp.zeros(out.shape, jnp.float32)
    for k in range(0, depth, step):
        wide = [
            jnp.dot(x[:, i : i + 128], spread, preferred_element_type=jnp.float32).astype(jnp.bfloat16)
            for i in range(k, k + step, 128)
        ]
        even = jnp.concatenate([part[:, :256] for part in wide], axis=1)
        odd = jnp.concatenate([part[:, 256:] for part in wide], axis=1)
        copies[k // step].wait()
        total += jnp.dot(
            jnp.concatenate([even, odd]), flat[2 * k : 2 * (k + step), :], preferred_element_type=jnp.float32
        )
    out[...] = total


def gate_up_product(x, base):
    depth, _, columns = base.shape
    return pl.pallas_call(
        gate_up_kernel,
        out_shape=jax.ShapeDtypeStruct((2 * x.shape[0], columns), jnp.float32),
        in_specs=[VMEM, HBM],
        out_specs=VMEM,
        scratch_shapes=[pltpu.VMEM(base.shape, base.dtype), pltpu.SemaphoreType.DMA((depth // 512,))],
        compiler_params=pltpu.CompilerParams(vmem_limit_bytes=32 << 20),
        cost_estimate=pl.CostEstimate(
            flops=4 * x.shape[0] * depth * columns, bytes_accessed=2 * base.size, transcendentals=0
        ),
    )(x, in_hbm(base))


def local(
    tokens,
    routes,
    numerators,
    place,
    base_in,
    base_down,
    delta_in,
    delta_mid,
    delta_down,
    delta_back,
):
    clusters = lax.axis_size("expert")
    members = lax.axis_size("tensor")
    me = lax.axis_index("tensor")
    cluster = lax.axis_index("expert")
    core = me % 2
    count, width = tokens.shape[1:]
    top = routes.shape[2]

    along, across = halves(clusters), halves(members // 2)
    shared, paired = along[: len(along) - len(across)], along[len(along) - len(across) :]

    side = jnp.concatenate([routes[0], numerators[0]], axis=1).astype(jnp.bfloat16)
    side = jnp.pad(side, ((0, 0), (0, 128 - 2 * top)))
    held = lax.optimization_barrier(jnp.concatenate([tokens[0], side], axis=1))

    for i, mask in enumerate(shared):
        if i == 0:
            pieces = [trade(piece, (mask, 0), (mask, 0)) for piece in (tokens[0], side)]
            received = jnp.concatenate(pieces, axis=1)
        else:
            received = trade(held, (mask, 0), (mask, 0))
        held = jnp.concatenate([held, received])
    for z, x in zip(paired, across):
        size = held.shape[0]
        flag = (me // (2 * x)) % 2 == 1
        held = jnp.concatenate(ordered((core == 0) & flag, held, trade(held, (0, 2 * x), (z, 0))))
        low, high = ordered((core == 1) & flag, held, trade(held, (z, 0), (0, 2 * x)))
        inner = ordered(core == 1, low[size:], high[:size])
        held = jnp.concatenate([low[:size], *inner, high[size:]])
    held = by_rows(jnp.concatenate(ordered(core == 1, held, trade(held, (0, 1), (0, 1)))))

    codes = code_product(held, delta_in[0])
    projected = gate_up_product(held, base_in[0])

    side = by_rows(held[:, width:])
    all_routes = side[:, :top].astype(jnp.int32)
    numerator = side[:, top : 2 * top].astype(jnp.float32)
    position = lookup(place, all_routes)
    weight = (2.5 * numerator / jnp.sum(numerator, axis=-1, keepdims=True)).astype(jnp.bfloat16)
    target = cluster * members + jnp.arange(members, dtype=jnp.int32)
    scale = jnp.sum(
        jnp.where(position[None] == target[:, None, None], weight[None].astype(jnp.float32), 0.0), axis=-1
    )

    codes = jnp.stack([codes if m == 0 else trade(codes, (0, m), (0, m)) for m in range(members)])
    by_slot = jnp.stack([lax.dynamic_index_in_dim(codes, s ^ me, 0, keepdims=False) for s in range(members)])

    lifted = jnp.einsum("srk,skgf->srgf", by_slot, delta_mid[0], preferred_element_type=jnp.float32)
    total = held.shape[0]
    hidden = jax.nn.silu(projected[None, :total] + lifted[:, :, 0]) * (projected[None, total:] + lifted[:, :, 1])
    hidden_sum = jnp.sum(scale[:, :, None] * hidden, axis=0).astype(jnp.bfloat16)
    partial_codes = jnp.einsum(
        "srf,sfk->srk", hidden.astype(jnp.bfloat16), delta_down[0], preferred_element_type=jnp.float32
    ).astype(jnp.bfloat16)
    lowrank = lax.dynamic_index_in_dim(partial_codes, me, 0, keepdims=False).astype(jnp.float32)
    for m in range(1, members):
        sent = lax.dynamic_index_in_dim(partial_codes, me ^ m, 0, keepdims=False)
        lowrank = lowrank + trade(sent, (0, m), (0, m)).astype(jnp.float32)
    own_scale = lax.dynamic_index_in_dim(scale, me, 0, keepdims=False)
    scaled = (own_scale[:, None] * lowrank).astype(jnp.bfloat16)

    term = jnp.dot(hidden_sum, base_down[0], preferred_element_type=jnp.float32)
    term = (term + jnp.dot(scaled, delta_back[0], preferred_element_type=jnp.float32)).astype(jnp.bfloat16)

    def add(kept, received):
        return (kept.astype(jnp.float32) + received.astype(jnp.float32)).astype(jnp.bfloat16)

    kept, sent = ordered(core == 1, term[: total // 2], term[total // 2 :])
    total = add(kept, trade(sent, (0, 1), (0, 1)))
    for z, x in reversed(list(zip(paired, across))):
        flag = (me // (2 * x)) % 2 == 1
        size = total.shape[0] // 4
        blocks = [total[i * size : (i + 1) * size] for i in range(4)]
        inner = ordered(core == 1, blocks[1], blocks[2])
        kept, sent = ordered(
            (core == 1) & flag,
            jnp.concatenate([blocks[0], inner[0]]),
            jnp.concatenate([inner[1], blocks[3]]),
        )
        total = add(kept, trade(sent, (z, 0), (0, 2 * x)))
        kept, sent = ordered((core == 0) & flag, total[:size], total[size:])
        total = add(kept, trade(sent, (0, 2 * x), (z, 0)))
    for mask in reversed(shared):
        size = total.shape[0] // 2
        total = add(total[:size], trade(total[size:], (mask, 0), (mask, 0)))
    return total[None]


def solution(mesh):
    placed = (
        P(None, ("parts", "expert", "tensor"), None),
        P(None, ("parts", "expert", "tensor"), None),
        P(None, ("parts", "expert", "tensor"), None),
        P("parts"),
        P("expert", None, None, "tensor"),
        P("expert", "tensor", None),
        P(("expert", "tensor"), None, None),
        P("expert", None, None, None, "tensor"),
        P("expert", None, "tensor", None),
        P(("expert", "tensor"), None, None),
    )
    return jax.shard_map(
        local,
        mesh=mesh,
        in_specs=placed,
        out_specs=P(None, ("parts", "expert", "tensor"), None),
        check_vma=False,
    )
```

```python
import jax
import jax.numpy as jnp
from jax import lax
from jax.experimental import pallas as pl
from jax.experimental.pallas import tpu as pltpu
from jax.experimental.layout import Layout, with_layout_constraint
from jax.sharding import PartitionSpec as P

VMEM = pl.BlockSpec(memory_space=pltpu.VMEM)
HBM = pl.BlockSpec(memory_space=pltpu.HBM)


def in_hbm(value):
    return pltpu.with_memory_space_constraint(value, pltpu.HBM)


def by_rows(value):
    return with_layout_constraint(value, Layout((0, 1)))


def lookup(table, index):
    keys = jnp.arange(table.shape[0], dtype=jnp.int32)
    return jnp.sum(jnp.where(index[..., None] == keys, table, 0), axis=-1)


def trade(value, even, odd):
    members = lax.axis_size("tensor")
    pairs = []
    for e in range(lax.axis_size("expert")):
        for t in range(members):
            along, across = odd if t % 2 else even
            pairs.append((e * members + t, (e ^ along) * members + (t ^ across)))
    return lax.ppermute(value, ("expert", "tensor"), pairs)


def halves(size):
    masks = []
    while size > 1:
        size //= 2
        masks.append(size)
    return masks


def ordered(flip, first, second):
    return jnp.where(flip, second, first), jnp.where(flip, first, second)


def split_kernel(first, base, table, split, codes_in, rows, sems):
    depth, _, columns = rows.shape
    step = depth // (sems.shape[0] - 1)
    copies = [
        pltpu.make_async_copy(base.at[pl.ds(first + k, step)], rows.at[pl.ds(k, step)], sems.at[k // step])
        for k in range(0, depth, step)
    ]
    whole = pltpu.make_async_copy(table, codes_in, sems.at[sems.shape[0] - 1])
    for copy in copies:
        copy.start()
    whole.start()
    row = lax.broadcasted_iota(jnp.int32, (256, 256), 0)
    column = lax.broadcasted_iota(jnp.int32, (256, 256), 1)
    source = 2 * row - jnp.where(row < 128, 0, 255)
    order = jnp.where(column == source, 1.0, 0.0).astype(jnp.bfloat16)
    flat = rows.reshape(2 * depth, columns)
    for k in range(0, depth, 128):
        if k % step == 0:
            copies[k // step].wait()
        sorted_rows = jnp.dot(order, flat[2 * k : 2 * k + 256, :], preferred_element_type=jnp.float32)
        sorted_rows = sorted_rows.astype(jnp.bfloat16)
        split[k : k + 128, :columns] = sorted_rows[:128]
        split[k : k + 128, columns:] = sorted_rows[128:]
    whole.wait()


def split_gate_up(base, table, part, parts):
    depth, _, columns = base.shape
    block = depth // parts
    return pl.pallas_call(
        lambda base, table, *rest: split_kernel(
            part * block, base, table.at[pl.ds(part * block, block)], *rest
        ),
        out_shape=(
            pltpu.VMEM((block, 2 * columns), base.dtype),
            pltpu.VMEM((block, table.shape[1]), table.dtype),
        ),
        in_specs=[HBM, HBM],
        out_specs=(VMEM, VMEM),
        scratch_shapes=[pltpu.VMEM((block, 2, columns), base.dtype), pltpu.SemaphoreType.DMA((block // 512 + 1,))],
        compiler_params=pltpu.CompilerParams(vmem_limit_bytes=24 << 20),
        cost_estimate=pl.CostEstimate(flops=512 * block * columns, bytes_accessed=4 * block * columns, transcendentals=0),
    )(in_hbm(base), in_hbm(table))


def product_kernel(x, *refs):
    *tables, out = refs
    total = jnp.zeros(out.shape, jnp.float32)
    start = 0
    for table in tables:
        depth = table.shape[0]
        total += jnp.dot(x[:, start : start + depth], table[...], preferred_element_type=jnp.float32)
        start += depth
    out[...] = total.astype(out.dtype)


def product(x, tables, dtype):
    columns = tables[0].shape[1]
    size = sum(table.size for table in tables)
    return pl.pallas_call(
        product_kernel,
        out_shape=jax.ShapeDtypeStruct((x.shape[0], columns), dtype),
        in_specs=[VMEM] * (1 + len(tables)),
        out_specs=VMEM,
        compiler_params=pltpu.CompilerParams(vmem_limit_bytes=16 << 20),
        cost_estimate=pl.CostEstimate(flops=2 * x.shape[0] * size, bytes_accessed=2 * size, transcendentals=0),
    )(x, *(pltpu.with_memory_space_constraint(table, pltpu.VMEM) for table in tables))


def local(
    tokens,
    routes,
    numerators,
    place,
    base_in,
    base_down,
    delta_in,
    delta_mid,
    delta_down,
    delta_back,
):
    clusters = lax.axis_size("expert")
    members = lax.axis_size("tensor")
    me = lax.axis_index("tensor")
    cluster = lax.axis_index("expert")
    core = me % 2
    count, width = tokens.shape[1:]
    top = routes.shape[2]

    along, across = halves(clusters), halves(members // 2)
    shared, paired = along[: len(along) - len(across)], along[len(along) - len(across) :]

    def pack(rows, routes, numerators):
        side = jnp.concatenate([routes, numerators], axis=1).astype(jnp.bfloat16)
        return jnp.concatenate([rows, jnp.pad(side, ((0, 0), (0, 128 - 2 * top)))], axis=1)

    own = (tokens[0], routes[0], numerators[0])
    held = lax.optimization_barrier(pack(*own))

    for i, mask in enumerate(shared):
        if i == 0:
            received = pack(*(trade(piece, (mask, 0), (mask, 0)) for piece in own))
        else:
            received = trade(held, (mask, 0), (mask, 0))
        held = jnp.concatenate([held, received])
        if i == 0:
            parts = [split_gate_up(base_in[0], delta_in[0], 0, 2)]
            held, parts[0], *later = lax.optimization_barrier((held, parts[0], base_in, delta_in))
    for z, x in zip(paired, across):
        size = held.shape[0]
        flag = (me // (2 * x)) % 2 == 1
        held = jnp.concatenate(ordered((core == 0) & flag, held, trade(held, (0, 2 * x), (z, 0))))
        if len(parts) == 1:
            parts.append(split_gate_up(later[0][0], later[1][0], 1, 2))
            held, parts[1] = lax.optimization_barrier((held, parts[1]))
        low, high = ordered((core == 1) & flag, held, trade(held, (z, 0), (0, 2 * x)))
        inner = ordered(core == 1, low[size:], high[:size])
        held = jnp.concatenate([low[:size], *inner, high[size:]])
    held = by_rows(jnp.concatenate(ordered(core == 1, held, trade(held, (0, 1), (0, 1)))))

    codes = product(held, [part[1] for part in parts], jnp.bfloat16)
    projected = product(held, [part[0] for part in parts], jnp.float32)

    side = by_rows(held[:, width:])
    all_routes = side[:, :top].astype(jnp.int32)
    numerator = side[:, top : 2 * top].astype(jnp.float32)
    position = lookup(place, all_routes)
    weight = (2.5 * numerator / jnp.sum(numerator, axis=-1, keepdims=True)).astype(jnp.bfloat16)
    target = cluster * members + jnp.arange(members, dtype=jnp.int32)
    scale = jnp.sum(
        jnp.where(position[None] == target[:, None, None], weight[None].astype(jnp.float32), 0.0), axis=-1
    )

    codes = jnp.stack([codes if m == 0 else trade(codes, (0, m), (0, m)) for m in range(members)])
    by_slot = jnp.stack([lax.dynamic_index_in_dim(codes, s ^ me, 0, keepdims=False) for s in range(members)])

    lifted = jnp.einsum("srk,skgf->srgf", by_slot, delta_mid[0], preferred_element_type=jnp.float32)
    part = projected.shape[1] // 2
    hidden = jax.nn.silu(projected[None, :, :part] + lifted[:, :, 0]) * (
        projected[None, :, part:] + lifted[:, :, 1]
    )
    hidden_sum = jnp.sum(scale[:, :, None] * hidden, axis=0).astype(jnp.bfloat16)
    partial_codes = jnp.einsum(
        "srf,sfk->srk", hidden.astype(jnp.bfloat16), delta_down[0], preferred_element_type=jnp.float32
    ).astype(jnp.bfloat16)
    lowrank = lax.dynamic_index_in_dim(partial_codes, me, 0, keepdims=False).astype(jnp.float32)
    for m in range(1, members):
        sent = lax.dynamic_index_in_dim(partial_codes, me ^ m, 0, keepdims=False)
        lowrank = lowrank + trade(sent, (0, m), (0, m)).astype(jnp.float32)
    own_scale = lax.dynamic_index_in_dim(scale, me, 0, keepdims=False)
    scaled = (own_scale[:, None] * lowrank).astype(jnp.bfloat16)

    term = jnp.dot(hidden_sum, base_down[0], preferred_element_type=jnp.float32)
    term = (term + jnp.dot(scaled, delta_back[0], preferred_element_type=jnp.float32)).astype(jnp.bfloat16)

    def add(kept, received):
        return (kept.astype(jnp.float32) + received.astype(jnp.float32)).astype(jnp.bfloat16)

    size = term.shape[0] // 2
    kept, sent = ordered(core == 1, term[:size], term[size:])
    total = add(kept, trade(sent, (0, 1), (0, 1)))
    for z, x in reversed(list(zip(paired, across))):
        flag = (me // (2 * x)) % 2 == 1
        size = total.shape[0] // 4
        blocks = [total[i * size : (i + 1) * size] for i in range(4)]
        inner = ordered(core == 1, blocks[1], blocks[2])
        kept, sent = ordered(
            (core == 1) & flag,
            jnp.concatenate([blocks[0], inner[0]]),
            jnp.concatenate([inner[1], blocks[3]]),
        )
        total = add(kept, trade(sent, (z, 0), (0, 2 * x)))
        kept, sent = ordered((core == 0) & flag, total[:size], total[size:])
        total = add(kept, trade(sent, (0, 2 * x), (z, 0)))
    for mask in reversed(shared):
        size = total.shape[0] // 2
        total = add(total[:size], trade(total[size:], (mask, 0), (mask, 0)))
    return total[None]


def solution(mesh):
    placed = (
        P(None, ("parts", "expert", "tensor"), None),
        P(None, ("parts", "expert", "tensor"), None),
        P(None, ("parts", "expert", "tensor"), None),
        P("parts"),
        P("expert", None, None, "tensor"),
        P("expert", "tensor", None),
        P(("expert", "tensor"), None, None),
        P("expert", None, None, None, "tensor"),
        P("expert", None, "tensor", None),
        P(("expert", "tensor"), None, None),
    )
    return jax.shard_map(
        local,
        mesh=mesh,
        in_specs=placed,
        out_specs=P(None, ("parts", "expert", "tensor"), None),
        check_vma=False,
    )
```

```python
import jax
import jax.numpy as jnp
from jax import lax
from jax.experimental import pallas as pl
from jax.experimental.pallas import tpu as pltpu
from jax.experimental.layout import Layout, with_layout_constraint
from jax.sharding import PartitionSpec as P

VMEM = pl.BlockSpec(memory_space=pltpu.VMEM)
HBM = pl.BlockSpec(memory_space=pltpu.HBM)


def in_hbm(value):
    return pltpu.with_memory_space_constraint(value, pltpu.HBM)


def by_rows(value):
    return with_layout_constraint(value, Layout((0, 1)))


def lookup(table, index):
    keys = jnp.arange(table.shape[0], dtype=jnp.int32)
    return jnp.sum(jnp.where(index[..., None] == keys, table, 0), axis=-1)


def trade(value, even, odd):
    members = lax.axis_size("tensor")
    pairs = []
    for e in range(lax.axis_size("expert")):
        for t in range(members):
            along, across = odd if t % 2 else even
            pairs.append((e * members + t, (e ^ along) * members + (t ^ across)))
    return lax.ppermute(value, ("expert", "tensor"), pairs)


def halves(size):
    masks = []
    while size > 1:
        size //= 2
        masks.append(size)
    return masks


def ordered(flip, first, second):
    return jnp.where(flip, second, first), jnp.where(flip, first, second)


def code_kernel(x, table, out, weights, sems):
    depth = weights.shape[0]
    step = depth // sems.shape[0]
    copies = [
        pltpu.make_async_copy(table.at[pl.ds(k, step)], weights.at[pl.ds(k, step)], sems.at[k // step])
        for k in range(0, depth, step)
    ]
    for i, copy in enumerate(copies):
        copy.start(priority=i % 2)
    total = jnp.zeros(out.shape, jnp.float32)
    for k in range(0, depth, step):
        copies[k // step].wait()
        total += jnp.dot(x[:, k : k + step], weights[k : k + step, :], preferred_element_type=jnp.float32)
    out[...] = total.astype(out.dtype)


def code_product(x, table):
    depth, rank = table.shape
    return pl.pallas_call(
        code_kernel,
        out_shape=jax.ShapeDtypeStruct((x.shape[0], rank), jnp.bfloat16),
        in_specs=[VMEM, HBM],
        out_specs=VMEM,
        scratch_shapes=[pltpu.VMEM(table.shape, table.dtype), pltpu.SemaphoreType.DMA((4,))],
        compiler_params=pltpu.CompilerParams(vmem_limit_bytes=32 << 20),
        cost_estimate=pl.CostEstimate(
            flops=2 * x.shape[0] * depth * rank, bytes_accessed=2 * table.size, transcendentals=0
        ),
    )(x, in_hbm(table))


def gate_up_kernel(x, base, out, weights, sems):
    depth, _, columns = weights.shape
    step = depth // sems.shape[0]
    copies = [
        pltpu.make_async_copy(base.at[pl.ds(k, step)], weights.at[pl.ds(k, step)], sems.at[k // step])
        for k in range(0, depth, step)
    ]
    for i, copy in enumerate(copies):
        copy.start(priority=i % 2)
    row = lax.broadcasted_iota(jnp.int32, (128, 512), 0)
    column = lax.broadcasted_iota(jnp.int32, (128, 512), 1)
    target = 2 * row + jnp.where(column < 256, 0, 257)
    spread = jnp.where(column == target, 1.0, 0.0).astype(jnp.bfloat16)
    flat = weights.reshape(2 * depth, columns)
    total = jnp.zeros(out.shape, jnp.float32)
    for k in range(0, depth, step):
        wide = [
            jnp.dot(x[:, i : i + 128], spread, preferred_element_type=jnp.float32).astype(jnp.bfloat16)
            for i in range(k, k + step, 128)
        ]
        even = jnp.concatenate([part[:, :256] for part in wide], axis=1)
        odd = jnp.concatenate([part[:, 256:] for part in wide], axis=1)
        copies[k // step].wait()
        total += jnp.dot(
            jnp.concatenate([even, odd]), flat[2 * k : 2 * (k + step), :], preferred_element_type=jnp.float32
        )
    out[...] = total


def gate_up_product(x, base):
    depth, _, columns = base.shape
    return pl.pallas_call(
        gate_up_kernel,
        out_shape=jax.ShapeDtypeStruct((2 * x.shape[0], columns), jnp.float32),
        in_specs=[VMEM, HBM],
        out_specs=VMEM,
        scratch_shapes=[pltpu.VMEM(base.shape, base.dtype), pltpu.SemaphoreType.DMA((depth // 512,))],
        compiler_params=pltpu.CompilerParams(vmem_limit_bytes=32 << 20),
        cost_estimate=pl.CostEstimate(
            flops=4 * x.shape[0] * depth * columns, bytes_accessed=2 * base.size, transcendentals=0
        ),
    )(x, in_hbm(base))


def local(
    tokens,
    routes,
    numerators,
    place,
    base_in,
    base_down,
    delta_in,
    delta_mid,
    delta_down,
    delta_back,
):
    clusters = lax.axis_size("expert")
    members = lax.axis_size("tensor")
    me = lax.axis_index("tensor")
    cluster = lax.axis_index("expert")
    core = me % 2
    count, width = tokens.shape[1:]
    top = routes.shape[2]

    along, across = halves(clusters), halves(members // 2)
    shared, paired = along[: len(along) - len(across)], along[len(along) - len(across) :]

    side = jnp.concatenate([routes[0], numerators[0]], axis=1).astype(jnp.bfloat16)
    side = jnp.pad(side, ((0, 0), (0, 128 - 2 * top)))
    held = lax.optimization_barrier(jnp.concatenate([tokens[0], side], axis=1))

    for i, mask in enumerate(shared):
        if i == 0:
            pieces = [trade(piece, (mask, 0), (mask, 0)) for piece in (tokens[0], side)]
            received = jnp.concatenate(pieces, axis=1)
        else:
            received = trade(held, (mask, 0), (mask, 0))
        held = jnp.concatenate([held, received])
    for z, x in zip(paired, across):
        size = held.shape[0]
        flag = (me // (2 * x)) % 2 == 1
        held = jnp.concatenate(ordered((core == 0) & flag, held, trade(held, (0, 2 * x), (z, 0))))
        low, high = ordered((core == 1) & flag, held, trade(held, (z, 0), (0, 2 * x)))
        inner = ordered(core == 1, low[size:], high[:size])
        held = jnp.concatenate([low[:size], *inner, high[size:]])
    held = by_rows(jnp.concatenate(ordered(core == 1, held, trade(held, (0, 1), (0, 1)))))

    codes = code_product(held, delta_in[0])
    projected = gate_up_product(held, base_in[0])

    side = by_rows(held[:, width:])
    all_routes = side[:, :top].astype(jnp.int32)
    numerator = side[:, top : 2 * top].astype(jnp.float32)
    position = lookup(place, all_routes)
    weight = (2.5 * numerator / jnp.sum(numerator, axis=-1, keepdims=True)).astype(jnp.bfloat16)
    target = cluster * members + jnp.arange(members, dtype=jnp.int32)
    scale = jnp.sum(
        jnp.where(position[None] == target[:, None, None], weight[None].astype(jnp.float32), 0.0), axis=-1
    )

    codes = jnp.stack([codes if m == 0 else trade(codes, (0, m), (0, m)) for m in range(members)])
    by_slot = jnp.stack([lax.dynamic_index_in_dim(codes, s ^ me, 0, keepdims=False) for s in range(members)])

    lifted = jnp.einsum("srk,skgf->srgf", by_slot, delta_mid[0], preferred_element_type=jnp.float32)
    total = held.shape[0]
    hidden = jax.nn.silu(projected[None, :total] + lifted[:, :, 0]) * (projected[None, total:] + lifted[:, :, 1])
    hidden_sum = jnp.sum(scale[:, :, None] * hidden, axis=0).astype(jnp.bfloat16)
    partial_codes = jnp.einsum(
        "srf,sfk->srk", hidden.astype(jnp.bfloat16), delta_down[0], preferred_element_type=jnp.float32
    ).astype(jnp.bfloat16)
    lowrank = lax.all_to_all(partial_codes, "tensor", split_axis=0, concat_axis=0, tiled=True)
    lowrank = jnp.sum(lowrank.astype(jnp.float32), axis=0)
    own_scale = lax.dynamic_index_in_dim(scale, me, 0, keepdims=False)
    scaled = (own_scale[:, None] * lowrank).astype(jnp.bfloat16)

    term = jnp.dot(hidden_sum, base_down[0], preferred_element_type=jnp.float32)
    term = (term + jnp.dot(scaled, delta_back[0], preferred_element_type=jnp.float32)).astype(jnp.bfloat16)

    def add(kept, received):
        return (kept.astype(jnp.float32) + received.astype(jnp.float32)).astype(jnp.bfloat16)

    kept, sent = ordered(core == 1, term[: total // 2], term[total // 2 :])
    total = add(kept, trade(sent, (0, 1), (0, 1)))
    for z, x in reversed(list(zip(paired, across))):
        flag = (me // (2 * x)) % 2 == 1
        size = total.shape[0] // 4
        blocks = [total[i * size : (i + 1) * size] for i in range(4)]
        inner = ordered(core == 1, blocks[1], blocks[2])
        kept, sent = ordered(
            (core == 1) & flag,
            jnp.concatenate([blocks[0], inner[0]]),
            jnp.concatenate([inner[1], blocks[3]]),
        )
        total = add(kept, trade(sent, (z, 0), (0, 2 * x)))
        kept, sent = ordered((core == 0) & flag, total[:size], total[size:])
        total = add(kept, trade(sent, (0, 2 * x), (z, 0)))
    for mask in reversed(shared):
        size = total.shape[0] // 2
        total = add(total[:size], trade(total[size:], (mask, 0), (mask, 0)))
    return total[None]


def solution(mesh):
    placed = (
        P(None, ("parts", "expert", "tensor"), None),
        P(None, ("parts", "expert", "tensor"), None),
        P(None, ("parts", "expert", "tensor"), None),
        P("parts"),
        P("expert", None, None, "tensor"),
        P("expert", "tensor", None),
        P(("expert", "tensor"), None, None),
        P("expert", None, None, None, "tensor"),
        P("expert", None, "tensor", None),
        P(("expert", "tensor"), None, None),
    )
    return jax.shard_map(
        local,
        mesh=mesh,
        in_specs=placed,
        out_specs=P(None, ("parts", "expert", "tensor"), None),
        check_vma=False,
    )
```

```python
import functools

import jax
import jax.numpy as jnp
from jax import lax
from jax.experimental import pallas as pl
from jax.experimental.pallas import tpu as pltpu
from jax.experimental.layout import Layout, with_layout_constraint
from jax.sharding import PartitionSpec as P

VMEM = pl.BlockSpec(memory_space=pltpu.VMEM)
HBM = pl.BlockSpec(memory_space=pltpu.HBM)


def in_hbm(value):
    return pltpu.with_memory_space_constraint(value, pltpu.HBM)


def by_rows(value):
    return with_layout_constraint(value, Layout((0, 1)))


def lookup(table, index):
    keys = jnp.arange(table.shape[0], dtype=jnp.int32)
    return jnp.sum(jnp.where(index[..., None] == keys, table, 0), axis=-1)


def trade(value, even, odd):
    members = lax.axis_size("tensor")
    pairs = []
    for e in range(lax.axis_size("expert")):
        for t in range(members):
            along, across = odd if t % 2 else even
            pairs.append((e * members + t, (e ^ along) * members + (t ^ across)))
    return lax.ppermute(value, ("expert", "tensor"), pairs)


def halves(size):
    masks = []
    while size > 1:
        size //= 2
        masks.append(size)
    return masks


def ordered(flip, first, second):
    return jnp.where(flip, second, first), jnp.where(flip, first, second)


def split_kernel(first, base, split, rows, split_rows, in_sems, out_sems):
    depth, _, columns = rows.shape
    step = 512
    count = depth // step
    arrive = [
        pltpu.make_async_copy(base.at[pl.ds(first + i * step, step)], rows.at[pl.ds(i * step, step)], in_sems.at[i])
        for i in range(count)
    ]
    leave = [
        pltpu.make_async_copy(split_rows.at[pl.ds(i * step, step)], split.at[pl.ds(i * step, step)], out_sems.at[i])
        for i in range(count)
    ]
    for copy in arrive:
        copy.start()
    row = lax.broadcasted_iota(jnp.int32, (256, 256), 0)
    column = lax.broadcasted_iota(jnp.int32, (256, 256), 1)
    source = 2 * row - jnp.where(row < 128, 0, 255)
    order = jnp.where(column == source, 1.0, 0.0).astype(jnp.bfloat16)
    flat = rows.reshape(2 * depth, columns)
    for i in range(count):
        arrive[i].wait()
        blocks = range(i * step, (i + 1) * step, 128)
        wide = jnp.concatenate([flat[2 * k : 2 * k + 256, :] for k in blocks], axis=1)
        wide = jnp.dot(order, wide, preferred_element_type=jnp.float32).astype(jnp.bfloat16)
        for j, k in enumerate(blocks):
            split_rows[k : k + 128, :columns] = wide[:128, j * columns : (j + 1) * columns]
            split_rows[k : k + 128, columns:] = wide[128:, j * columns : (j + 1) * columns]
        leave[i].start()
    for copy in leave:
        copy.wait()


def split_gate_up(base, part, parts):
    depth, _, columns = base.shape
    block = depth // parts
    return pl.pallas_call(
        functools.partial(split_kernel, part * block),
        out_shape=pltpu.HBM((block, 2 * columns), base.dtype),
        in_specs=[HBM],
        out_specs=HBM,
        scratch_shapes=[
            pltpu.VMEM((block, 2, columns), base.dtype),
            pltpu.VMEM((block, 2 * columns), base.dtype),
            pltpu.SemaphoreType.DMA((block // 512,)),
            pltpu.SemaphoreType.DMA((block // 512,)),
        ],
        compiler_params=pltpu.CompilerParams(vmem_limit_bytes=24 << 20),
        cost_estimate=pl.CostEstimate(flops=512 * block * columns, bytes_accessed=8 * block * columns, transcendentals=0),
    )(in_hbm(base))


def split_beside(held, parts, weights):
    held, parts, weights = lax.optimization_barrier((held, parts, weights))
    if len(parts) < 2:
        parts = [*parts, split_gate_up(weights[0], len(parts), 2)]
    return held, parts, weights


def local(
    tokens,
    routes,
    numerators,
    place,
    base_in,
    base_down,
    delta_in,
    delta_mid,
    delta_down,
    delta_back,
):
    clusters = lax.axis_size("expert")
    members = lax.axis_size("tensor")
    me = lax.axis_index("tensor")
    cluster = lax.axis_index("expert")
    core = me % 2
    count, width = tokens.shape[1:]
    top = routes.shape[2]

    along, across = halves(clusters), halves(members // 2)
    shared, paired = along[: len(along) - len(across)], along[len(along) - len(across) :]

    side = jnp.concatenate([routes[0], numerators[0]], axis=1).astype(jnp.bfloat16)
    side = jnp.pad(side, ((0, 0), (0, 128 - 2 * top)))
    held = lax.optimization_barrier(jnp.concatenate([tokens[0], side], axis=1))

    for i, mask in enumerate(shared):
        if i == 0:
            pieces = [trade(piece, (mask, 0), (mask, 0)) for piece in (tokens[0], side)]
            received = jnp.concatenate(pieces, axis=1)
        else:
            received = trade(held, (mask, 0), (mask, 0))
        held = jnp.concatenate([held, received])
    parts, weights = [], base_in
    for z, x in zip(paired, across):
        size = held.shape[0]
        flag = (me // (2 * x)) % 2 == 1
        held, parts, weights = split_beside(held, parts, weights)
        held = jnp.concatenate(ordered((core == 0) & flag, held, trade(held, (0, 2 * x), (z, 0))))
        held, parts, weights = split_beside(held, parts, weights)
        low, high = ordered((core == 1) & flag, held, trade(held, (z, 0), (0, 2 * x)))
        inner = ordered(core == 1, low[size:], high[:size])
        held = jnp.concatenate([low[:size], *inner, high[size:]])
    held, parts = lax.optimization_barrier((held, parts))
    held = by_rows(jnp.concatenate(ordered(core == 1, held, trade(held, (0, 1), (0, 1)))))

    rows = held[:, :width]
    codes = jnp.dot(rows, delta_in[0], preferred_element_type=jnp.float32).astype(jnp.bfloat16)
    block = parts[0].shape[0]
    projected = sum(
        jnp.dot(rows[:, i * block : (i + 1) * block], part, preferred_element_type=jnp.float32)
        for i, part in enumerate(parts)
    )

    side = by_rows(held[:, width:])
    all_routes = side[:, :top].astype(jnp.int32)
    numerator = side[:, top : 2 * top].astype(jnp.float32)
    position = lookup(place, all_routes)
    weight = (2.5 * numerator / jnp.sum(numerator, axis=-1, keepdims=True)).astype(jnp.bfloat16)
    target = cluster * members + jnp.arange(members, dtype=jnp.int32)
    scale = jnp.sum(
        jnp.where(position[None] == target[:, None, None], weight[None].astype(jnp.float32), 0.0), axis=-1
    )

    codes = jnp.stack([codes if m == 0 else trade(codes, (0, m), (0, m)) for m in range(members)])
    by_slot = jnp.stack([lax.dynamic_index_in_dim(codes, s ^ me, 0, keepdims=False) for s in range(members)])

    lifted = jnp.einsum("srk,skgf->srgf", by_slot, delta_mid[0], preferred_element_type=jnp.float32)
    part = projected.shape[1] // 2
    hidden = jax.nn.silu(projected[None, :, :part] + lifted[:, :, 0]) * (
        projected[None, :, part:] + lifted[:, :, 1]
    )
    hidden_sum = jnp.sum(scale[:, :, None] * hidden, axis=0).astype(jnp.bfloat16)
    partial_codes = jnp.einsum(
        "srf,sfk->srk", hidden.astype(jnp.bfloat16), delta_down[0], preferred_element_type=jnp.float32
    ).astype(jnp.bfloat16)
    lowrank = lax.dynamic_index_in_dim(partial_codes, me, 0, keepdims=False).astype(jnp.float32)
    for m in range(1, members):
        sent = lax.dynamic_index_in_dim(partial_codes, me ^ m, 0, keepdims=False)
        lowrank = lowrank + trade(sent, (0, m), (0, m)).astype(jnp.float32)
    own_scale = lax.dynamic_index_in_dim(scale, me, 0, keepdims=False)
    scaled = (own_scale[:, None] * lowrank).astype(jnp.bfloat16)

    term = jnp.dot(hidden_sum, base_down[0], preferred_element_type=jnp.float32)
    term = (term + jnp.dot(scaled, delta_back[0], preferred_element_type=jnp.float32)).astype(jnp.bfloat16)

    def add(kept, received):
        return (kept.astype(jnp.float32) + received.astype(jnp.float32)).astype(jnp.bfloat16)

    size = term.shape[0] // 2
    kept, sent = ordered(core == 1, term[:size], term[size:])
    total = add(kept, trade(sent, (0, 1), (0, 1)))
    for z, x in reversed(list(zip(paired, across))):
        flag = (me // (2 * x)) % 2 == 1
        size = total.shape[0] // 4
        blocks = [total[i * size : (i + 1) * size] for i in range(4)]
        inner = ordered(core == 1, blocks[1], blocks[2])
        kept, sent = ordered(
            (core == 1) & flag,
            jnp.concatenate([blocks[0], inner[0]]),
            jnp.concatenate([inner[1], blocks[3]]),
        )
        total = add(kept, trade(sent, (z, 0), (0, 2 * x)))
        kept, sent = ordered((core == 0) & flag, total[:size], total[size:])
        total = add(kept, trade(sent, (0, 2 * x), (z, 0)))
    for mask in reversed(shared):
        size = total.shape[0] // 2
        total = add(total[:size], trade(total[size:], (mask, 0), (mask, 0)))
    return total[None]


def solution(mesh):
    placed = (
        P(None, ("parts", "expert", "tensor"), None),
        P(None, ("parts", "expert", "tensor"), None),
        P(None, ("parts", "expert", "tensor"), None),
        P("parts"),
        P("expert", None, None, "tensor"),
        P("expert", "tensor", None),
        P(("expert", "tensor"), None, None),
        P("expert", None, None, None, "tensor"),
        P("expert", None, "tensor", None),
        P(("expert", "tensor"), None, None),
    )
    return jax.shard_map(
        local,
        mesh=mesh,
        in_specs=placed,
        out_specs=P(None, ("parts", "expert", "tensor"), None),
        check_vma=False,
    )
```

```python
import jax
import jax.numpy as jnp
from jax import lax
from jax.experimental import pallas as pl
from jax.experimental.pallas import tpu as pltpu
from jax.experimental.layout import Layout, with_layout_constraint
from jax.sharding import PartitionSpec as P

VMEM = pl.BlockSpec(memory_space=pltpu.VMEM)
HBM = pl.BlockSpec(memory_space=pltpu.HBM)


def in_hbm(value):
    return pltpu.with_memory_space_constraint(value, pltpu.HBM)


def by_rows(value):
    return with_layout_constraint(value, Layout((0, 1)))


def lookup(table, index):
    keys = jnp.arange(table.shape[0], dtype=jnp.int32)
    return jnp.sum(jnp.where(index[..., None] == keys, table, 0), axis=-1)


def trade(value, even, odd):
    members = lax.axis_size("tensor")
    pairs = []
    for e in range(lax.axis_size("expert")):
        for t in range(members):
            along, across = odd if t % 2 else even
            pairs.append((e * members + t, (e ^ along) * members + (t ^ across)))
    return lax.ppermute(value, ("expert", "tensor"), pairs)


def halves(size):
    masks = []
    while size > 1:
        size //= 2
        masks.append(size)
    return masks


def ordered(flip, first, second):
    return jnp.where(flip, second, first), jnp.where(flip, first, second)


def pack_kernel(tokens, routes, numerators, packed, routes_in, numerators_in, sems):
    width, top = tokens.shape[1], routes.shape[1]
    copies = [
        pltpu.make_async_copy(tokens, packed.at[:, pl.ds(0, width)], sems.at[0]),
        pltpu.make_async_copy(routes, routes_in, sems.at[1]),
        pltpu.make_async_copy(numerators, numerators_in, sems.at[2]),
    ]
    for copy in copies:
        copy.start()
    packed[:, width:] = jnp.zeros((packed.shape[0], packed.shape[1] - width), packed.dtype)
    for copy in copies[1:]:
        copy.wait()
    packed[:, width : width + top] = routes_in[...].astype(jnp.float32).astype(packed.dtype)
    packed[:, width + top : width + 2 * top] = numerators_in[...].astype(jnp.float32).astype(packed.dtype)
    copies[0].wait()


def pack(tokens, routes, numerators):
    count, width = tokens.shape
    return pl.pallas_call(
        pack_kernel,
        out_shape=jax.ShapeDtypeStruct((count, width + 128), tokens.dtype),
        in_specs=[HBM] * 3,
        out_specs=VMEM,
        scratch_shapes=[
            pltpu.VMEM(routes.shape, routes.dtype),
            pltpu.VMEM(numerators.shape, numerators.dtype),
            pltpu.SemaphoreType.DMA((3,)),
        ],
        compiler_params=pltpu.CompilerParams(vmem_limit_bytes=4 << 20),
        cost_estimate=pl.CostEstimate(flops=0, bytes_accessed=4 * tokens.size, transcendentals=0),
    )(in_hbm(tokens), in_hbm(routes), in_hbm(numerators))


def gate_up_kernel(x, base, out, weights, sems):
    depth, _, columns = weights.shape
    step = depth // sems.shape[0]
    copies = [
        pltpu.make_async_copy(base.at[pl.ds(k, step)], weights.at[pl.ds(k, step)], sems.at[k // step])
        for k in range(0, depth, step)
    ]
    for copy in copies:
        copy.start()
    row = lax.broadcasted_iota(jnp.int32, (128, 256), 0)
    column = lax.broadcasted_iota(jnp.int32, (128, 256), 1)
    spread = jnp.where(column // 2 == row, 1.0, 0.0).astype(jnp.bfloat16)
    is_odd = (lax.broadcasted_iota(jnp.int32, (1, 2 * step), 1) % 2).astype(jnp.float32)
    odd_mask, even_mask = is_odd.astype(jnp.bfloat16), (1.0 - is_odd).astype(jnp.bfloat16)
    count = x.shape[0]
    flat = weights.reshape(2 * depth, columns)
    total = jnp.zeros(out.shape, jnp.float32)
    for k in range(0, depth, step):
        stacked = jnp.concatenate([x[:, i : i + 128] for i in range(k, k + step, 128)])
        wide = jnp.dot(stacked, spread, preferred_element_type=jnp.float32).astype(jnp.bfloat16)
        wide = jnp.concatenate([wide[i : i + count] for i in range(0, stacked.shape[0], count)], axis=1)
        copies[k // step].wait()
        total += jnp.dot(
            jnp.concatenate([wide * even_mask, wide * odd_mask]), flat[2 * k : 2 * (k + step), :], preferred_element_type=jnp.float32
        )
    out[...] = total


def gate_up_product(x, base):
    depth, _, columns = base.shape
    return pl.pallas_call(
        gate_up_kernel,
        out_shape=jax.ShapeDtypeStruct((2 * x.shape[0], columns), jnp.float32),
        in_specs=[VMEM, HBM],
        out_specs=VMEM,
        scratch_shapes=[pltpu.VMEM(base.shape, base.dtype), pltpu.SemaphoreType.DMA((depth // 512,))],
        compiler_params=pltpu.CompilerParams(vmem_limit_bytes=32 << 20),
        cost_estimate=pl.CostEstimate(
            flops=4 * x.shape[0] * depth * columns, bytes_accessed=2 * base.size, transcendentals=0
        ),
    )(x, in_hbm(base))


def local(
    tokens,
    routes,
    numerators,
    place,
    base_in,
    base_down,
    delta_in,
    delta_mid,
    delta_down,
    delta_back,
):
    clusters = lax.axis_size("expert")
    members = lax.axis_size("tensor")
    me = lax.axis_index("tensor")
    cluster = lax.axis_index("expert")
    core = me % 2
    count, width = tokens.shape[1:]
    top = routes.shape[2]

    along, across = halves(clusters), halves(members // 2)
    shared, paired = along[: len(along) - len(across)], along[len(along) - len(across) :]

    packed = pack(tokens[0], routes[0], numerators[0])
    chips = members // 2
    pieces = {(0, 0): packed}
    for z in range(clusters - 1, 0, -1):
        pieces[0, z] = trade(packed, (z, 0), (z, 0))
    for x in range(1, chips):
        pieces[x, 0] = trade(packed, (0, 2 * x), (0, 2 * x))
    rest = jnp.concatenate([pieces[0, z] for z in range(1, clusters)])
    for x in range(1, chips):
        received = trade(rest, (0, 2 * x), (0, 2 * x))
        for z in range(1, clusters):
            pieces[x, z] = received[(z - 1) * count : z * count]

    for bit in across:
        for x in range(chips):
            if not x & bit:
                for z in range(clusters):
                    flag = (me // (2 * bit)) % 2 == 1
                    pieces[x, z], pieces[x | bit, z] = ordered(flag, pieces[x, z], pieces[x | bit, z])
    places = [(0, 0)]
    for mask in shared:
        places += [(x, z | mask) for x, z in places]
    for zbit, xbit in zip(paired, across):
        places += [(x | xbit, z) for x, z in places]
        places += [(x, z | zbit) for x, z in places]
    held = by_rows(jnp.concatenate([pieces[place] for place in places]))
    held = by_rows(jnp.concatenate(ordered(core == 1, held, trade(held, (0, 1), (0, 1)))))

    codes = jnp.dot(held[:, :width], delta_in[0], preferred_element_type=jnp.float32).astype(jnp.bfloat16)
    projected = gate_up_product(held, base_in[0])

    side = by_rows(held[:, width:])
    all_routes = side[:, :top].astype(jnp.int32)
    numerator = side[:, top : 2 * top].astype(jnp.float32)
    position = lookup(place, all_routes)
    weight = (2.5 * numerator / jnp.sum(numerator, axis=-1, keepdims=True)).astype(jnp.bfloat16)
    target = cluster * members + jnp.arange(members, dtype=jnp.int32)
    scale = jnp.sum(
        jnp.where(position[None] == target[:, None, None], weight[None].astype(jnp.float32), 0.0), axis=-1
    )

    codes = jnp.stack([codes if m == 0 else trade(codes, (0, m), (0, m)) for m in range(members)])
    by_slot = jnp.stack([lax.dynamic_index_in_dim(codes, s ^ me, 0, keepdims=False) for s in range(members)])

    lifted = jnp.einsum("srk,skgf->srgf", by_slot, delta_mid[0], preferred_element_type=jnp.float32)
    total = held.shape[0]
    hidden = jax.nn.silu(projected[None, :total] + lifted[:, :, 0]) * (projected[None, total:] + lifted[:, :, 1])
    hidden_sum = jnp.sum(scale[:, :, None] * hidden, axis=0).astype(jnp.bfloat16)
    partial_codes = jnp.einsum(
        "srf,sfk->srk", hidden.astype(jnp.bfloat16), delta_down[0], preferred_element_type=jnp.float32
    ).astype(jnp.bfloat16)
    lowrank = lax.dynamic_index_in_dim(partial_codes, me, 0, keepdims=False).astype(jnp.float32)
    for m in range(1, members):
        sent = lax.dynamic_index_in_dim(partial_codes, me ^ m, 0, keepdims=False)
        lowrank = lowrank + trade(sent, (0, m), (0, m)).astype(jnp.float32)
    own_scale = lax.dynamic_index_in_dim(scale, me, 0, keepdims=False)
    scaled = (own_scale[:, None] * lowrank).astype(jnp.bfloat16)

    term = jnp.dot(hidden_sum, base_down[0], preferred_element_type=jnp.float32)
    term = (term + jnp.dot(scaled, delta_back[0], preferred_element_type=jnp.float32)).astype(jnp.bfloat16)

    def add(kept, received):
        return (kept.astype(jnp.float32) + received.astype(jnp.float32)).astype(jnp.bfloat16)

    size = term.shape[0] // 2
    kept, sent = ordered(core == 1, term[:size], term[size:])
    total = add(kept, trade(sent, (0, 1), (0, 1)))
    for z, x in reversed(list(zip(paired, across))):
        flag = (me // (2 * x)) % 2 == 1
        size = total.shape[0] // 4
        blocks = [total[i * size : (i + 1) * size] for i in range(4)]
        inner = ordered(core == 1, blocks[1], blocks[2])
        kept, sent = ordered(
            (core == 1) & flag,
            jnp.concatenate([blocks[0], inner[0]]),
            jnp.concatenate([inner[1], blocks[3]]),
        )
        total = add(kept, trade(sent, (z, 0), (0, 2 * x)))
        kept, sent = ordered((core == 0) & flag, total[:size], total[size:])
        total = add(kept, trade(sent, (0, 2 * x), (z, 0)))
    for mask in reversed(shared):
        size = total.shape[0] // 2
        total = add(total[:size], trade(total[size:], (mask, 0), (mask, 0)))
    return total[None]


def solution(mesh):
    placed = (
        P(None, ("parts", "expert", "tensor"), None),
        P(None, ("parts", "expert", "tensor"), None),
        P(None, ("parts", "expert", "tensor"), None),
        P("parts"),
        P("expert", None, None, "tensor"),
        P("expert", "tensor", None),
        P(("expert", "tensor"), None, None),
        P("expert", None, None, None, "tensor"),
        P("expert", None, "tensor", None),
        P(("expert", "tensor"), None, None),
    )
    return jax.shard_map(
        local,
        mesh=mesh,
        in_specs=placed,
        out_specs=P(None, ("parts", "expert", "tensor"), None),
        check_vma=False,
    )
```

```python
import jax
import jax.numpy as jnp
from jax import lax
from jax.experimental import pallas as pl
from jax.experimental.pallas import tpu as pltpu
from jax.experimental.layout import Layout, with_layout_constraint
from jax.sharding import PartitionSpec as P

VMEM = pl.BlockSpec(memory_space=pltpu.VMEM)
HBM = pl.BlockSpec(memory_space=pltpu.HBM)


def in_hbm(value):
    return pltpu.with_memory_space_constraint(value, pltpu.HBM)


def by_rows(value):
    return with_layout_constraint(value, Layout((0, 1)))


def lookup(table, index):
    keys = jnp.arange(table.shape[0], dtype=jnp.int32)
    return jnp.sum(jnp.where(index[..., None] == keys, table, 0), axis=-1)


def trade(value, even, odd):
    members = lax.axis_size("tensor")
    pairs = []
    for e in range(lax.axis_size("expert")):
        for t in range(members):
            along, across = odd if t % 2 else even
            pairs.append((e * members + t, (e ^ along) * members + (t ^ across)))
    return lax.ppermute(value, ("expert", "tensor"), pairs)


def halves(size):
    masks = []
    while size > 1:
        size //= 2
        masks.append(size)
    return masks


def ordered(flip, first, second):
    return jnp.where(flip, second, first), jnp.where(flip, first, second)


def pack_kernel(tokens, routes, numerators, packed, routes_in, numerators_in, sems):
    width, top = tokens.shape[1], routes.shape[1]
    copies = [
        pltpu.make_async_copy(tokens, packed.at[:, pl.ds(0, width)], sems.at[0]),
        pltpu.make_async_copy(routes, routes_in, sems.at[1]),
        pltpu.make_async_copy(numerators, numerators_in, sems.at[2]),
    ]
    for copy in copies:
        copy.start()
    packed[:, width:] = jnp.zeros((packed.shape[0], packed.shape[1] - width), packed.dtype)
    for copy in copies[1:]:
        copy.wait()
    packed[:, width : width + top] = routes_in[...].astype(jnp.float32).astype(packed.dtype)
    packed[:, width + top : width + 2 * top] = numerators_in[...].astype(jnp.float32).astype(packed.dtype)
    copies[0].wait()


def pack(tokens, routes, numerators):
    count, width = tokens.shape
    return pl.pallas_call(
        pack_kernel,
        out_shape=jax.ShapeDtypeStruct((count, width + 128), tokens.dtype),
        in_specs=[HBM] * 3,
        out_specs=VMEM,
        scratch_shapes=[
            pltpu.VMEM(routes.shape, routes.dtype),
            pltpu.VMEM(numerators.shape, numerators.dtype),
            pltpu.SemaphoreType.DMA((3,)),
        ],
        compiler_params=pltpu.CompilerParams(vmem_limit_bytes=4 << 20),
        cost_estimate=pl.CostEstimate(flops=0, bytes_accessed=4 * tokens.size, transcendentals=0),
    )(in_hbm(tokens), in_hbm(routes), in_hbm(numerators))


def gate_up_kernel(x, base, out, weights, sems):
    depth, _, columns = weights.shape
    step = depth // sems.shape[0]
    copies = [
        pltpu.make_async_copy(base.at[pl.ds(k, step)], weights.at[pl.ds(k, step)], sems.at[k // step])
        for k in range(0, depth, step)
    ]
    for copy in copies:
        copy.start()
    row = lax.broadcasted_iota(jnp.int32, (256, 512), 0)
    column = lax.broadcasted_iota(jnp.int32, (256, 512), 1)
    spread = jnp.where(column // 2 == row, 1.0, 0.0).astype(jnp.bfloat16)
    is_up = (lax.broadcasted_iota(jnp.int32, (2 * step, columns), 0) % 2).astype(jnp.float32)
    gate_rows, up_rows = (1.0 - is_up).astype(jnp.bfloat16), is_up.astype(jnp.bfloat16)
    flat = weights.reshape(2 * depth, columns)
    total = jnp.zeros(out.shape, jnp.float32)
    for k in range(0, depth, step):
        wide = [
            jnp.dot(x[:, i : i + 256], spread, preferred_element_type=jnp.float32).astype(jnp.bfloat16)
            for i in range(k, k + step, 256)
        ]
        copies[k // step].wait()
        table = flat[2 * k : 2 * (k + step), :]
        total += jnp.dot(
            jnp.concatenate(wide, axis=1),
            jnp.concatenate([table * gate_rows, table * up_rows], axis=1),
            preferred_element_type=jnp.float32,
        )
    out[...] = total


def gate_up_product(x, base):
    depth, _, columns = base.shape
    return pl.pallas_call(
        gate_up_kernel,
        out_shape=jax.ShapeDtypeStruct((x.shape[0], 2 * columns), jnp.float32),
        in_specs=[VMEM, HBM],
        out_specs=VMEM,
        scratch_shapes=[pltpu.VMEM(base.shape, base.dtype), pltpu.SemaphoreType.DMA((depth // 512,))],
        compiler_params=pltpu.CompilerParams(vmem_limit_bytes=32 << 20),
        cost_estimate=pl.CostEstimate(
            flops=4 * x.shape[0] * depth * columns, bytes_accessed=2 * base.size, transcendentals=0
        ),
    )(x, in_hbm(base))


def local(
    tokens,
    routes,
    numerators,
    place,
    base_in,
    base_down,
    delta_in,
    delta_mid,
    delta_down,
    delta_back,
):
    clusters = lax.axis_size("expert")
    members = lax.axis_size("tensor")
    me = lax.axis_index("tensor")
    cluster = lax.axis_index("expert")
    core = me % 2
    count, width = tokens.shape[1:]
    top = routes.shape[2]

    along, across = halves(clusters), halves(members // 2)
    shared, paired = along[: len(along) - len(across)], along[len(along) - len(across) :]

    other_back = trade(delta_back[0], (0, 1), (0, 1))

    packed = pack(tokens[0], routes[0], numerators[0])
    chips = members // 2
    pieces = {(0, 0): packed}
    for z in range(clusters - 1, 0, -1):
        pieces[0, z] = trade(packed, (z, 0), (z, 0))
    for x in range(1, chips):
        pieces[x, 0] = trade(packed, (0, 2 * x), (0, 2 * x))
    rest = jnp.concatenate([pieces[0, z] for z in range(1, clusters)])
    for x in range(1, chips):
        received = trade(rest, (0, 2 * x), (0, 2 * x))
        for z in range(1, clusters):
            pieces[x, z] = received[(z - 1) * count : z * count]

    for bit in across:
        for x in range(chips):
            if not x & bit:
                for z in range(clusters):
                    flag = (me // (2 * bit)) % 2 == 1
                    pieces[x, z], pieces[x | bit, z] = ordered(flag, pieces[x, z], pieces[x | bit, z])
    places = [(0, 0)]
    for mask in shared:
        places += [(x, z | mask) for x, z in places]
    for zbit, xbit in zip(paired, across):
        places += [(x | xbit, z) for x, z in places]
        places += [(x, z | zbit) for x, z in places]
    held = by_rows(jnp.concatenate([pieces[place] for place in places]))
    held, other_back = lax.optimization_barrier((held, other_back))
    half = held.shape[0]
    held = by_rows(jnp.concatenate(ordered(core == 1, held, trade(held, (0, 1), (0, 1)))))

    codes = jnp.dot(held[:, :width], delta_in[0], preferred_element_type=jnp.float32).astype(jnp.bfloat16)
    rank = codes.shape[1]
    codes = jnp.stack([codes if m == 0 else trade(codes, (0, m), (0, m)) for m in range(members)])
    by_slot = jnp.stack([lax.dynamic_index_in_dim(codes, s ^ me, 0, keepdims=False) for s in range(members)])
    projected = gate_up_product(held, base_in[0])

    side = by_rows(held[:, width:])
    all_routes = side[:, :top].astype(jnp.int32)
    numerator = side[:, top : 2 * top].astype(jnp.float32)
    position = lookup(place, all_routes)
    weight = (2.5 * numerator / jnp.sum(numerator, axis=-1, keepdims=True)).astype(jnp.bfloat16)
    target = cluster * members + jnp.arange(members, dtype=jnp.int32)
    scale = jnp.sum(
        jnp.where(position[None] == target[:, None, None], weight[None].astype(jnp.float32), 0.0), axis=-1
    )

    lifted = jnp.einsum("srk,skgf->srgf", by_slot, delta_mid[0], preferred_element_type=jnp.float32)
    part = projected.shape[1] // 2
    hidden = jax.nn.silu(projected[None, :, :part] + lifted[:, :, 0]) * (
        projected[None, :, part:] + lifted[:, :, 1]
    )
    hidden_sum = jnp.sum(scale[:, :, None] * hidden, axis=0).astype(jnp.bfloat16)
    partial_codes = jnp.einsum(
        "srf,sfk->srk", hidden.astype(jnp.bfloat16), delta_down[0], preferred_element_type=jnp.float32
    ).astype(jnp.bfloat16)
    partial_codes = partial_codes.reshape(chips, 2, 2, half, rank).transpose(0, 2, 1, 3, 4)
    partial_codes = partial_codes.reshape(members, 2, half, rank)
    lowrank = lax.dynamic_index_in_dim(partial_codes, me, 0, keepdims=False).astype(jnp.float32)
    for m in range(1, members):
        sent = lax.dynamic_index_in_dim(partial_codes, me ^ m, 0, keepdims=False)
        lowrank = lowrank + trade(sent, (0, m), (0, m)).astype(jnp.float32)
    kept_scale = scale.reshape(chips, 2, 2, half).transpose(0, 2, 1, 3).reshape(members, 2, half)
    kept_scale = lax.dynamic_index_in_dim(kept_scale, me, 0, keepdims=False)
    scaled = (kept_scale[:, :, None] * lowrank).astype(jnp.bfloat16)
    scaled = ordered(core == 1, scaled[0], scaled[1])

    base = jnp.dot(hidden_sum, base_down[0], preferred_element_type=jnp.float32)
    kept, sent = ordered(core == 1, base[:half], base[half:])
    total = kept + trade(sent.astype(jnp.bfloat16), (0, 1), (0, 1)).astype(jnp.float32)
    for rows, table in zip(scaled, (delta_back[0], other_back)):
        total = total + jnp.dot(rows, table, preferred_element_type=jnp.float32)
    total = total.astype(jnp.bfloat16)

    def add(kept, received):
        return (kept.astype(jnp.float32) + received.astype(jnp.float32)).astype(jnp.bfloat16)

    for z, x in reversed(list(zip(paired, across))):
        flag = (me // (2 * x)) % 2 == 1
        size = total.shape[0] // 4
        blocks = [total[i * size : (i + 1) * size] for i in range(4)]
        inner = ordered(core == 1, blocks[1], blocks[2])
        kept, sent = ordered(
            (core == 1) & flag,
            jnp.concatenate([blocks[0], inner[0]]),
            jnp.concatenate([inner[1], blocks[3]]),
        )
        total = add(kept, trade(sent, (z, 0), (0, 2 * x)))
        kept, sent = ordered((core == 0) & flag, total[:size], total[size:])
        total = add(kept, trade(sent, (0, 2 * x), (z, 0)))
    for mask in reversed(shared):
        size = total.shape[0] // 2
        total = add(total[:size], trade(total[size:], (mask, 0), (mask, 0)))
    return total[None]


def solution(mesh):
    placed = (
        P(None, ("parts", "expert", "tensor"), None),
        P(None, ("parts", "expert", "tensor"), None),
        P(None, ("parts", "expert", "tensor"), None),
        P("parts"),
        P("expert", None, None, "tensor"),
        P("expert", "tensor", None),
        P(("expert", "tensor"), None, None),
        P("expert", None, None, None, "tensor"),
        P("expert", None, "tensor", None),
        P(("expert", "tensor"), None, None),
    )
    return jax.shard_map(
        local,
        mesh=mesh,
        in_specs=placed,
        out_specs=P(None, ("parts", "expert", "tensor"), None),
        check_vma=False,
    )
```

```python
import jax
import jax.numpy as jnp
from jax import lax
from jax.experimental import pallas as pl
from jax.experimental.pallas import tpu as pltpu
from jax.experimental.layout import Layout, with_layout_constraint
from jax.sharding import PartitionSpec as P

VMEM = pl.BlockSpec(memory_space=pltpu.VMEM)
HBM = pl.BlockSpec(memory_space=pltpu.HBM)


def in_hbm(value):
    return pltpu.with_memory_space_constraint(value, pltpu.HBM)


def by_rows(value):
    return with_layout_constraint(value, Layout((0, 1)))


def lookup(table, index):
    keys = jnp.arange(table.shape[0], dtype=jnp.int32)
    return jnp.sum(jnp.where(index[..., None] == keys, table, 0), axis=-1)


def trade(value, even, odd):
    members = lax.axis_size("tensor")
    pairs = []
    for e in range(lax.axis_size("expert")):
        for t in range(members):
            along, across = odd if t % 2 else even
            pairs.append((e * members + t, (e ^ along) * members + (t ^ across)))
    return lax.ppermute(value, ("expert", "tensor"), pairs)


def halves(size):
    masks = []
    while size > 1:
        size //= 2
        masks.append(size)
    return masks


def ordered(flip, first, second):
    return jnp.where(flip, second, first), jnp.where(flip, first, second)


def pack_kernel(tokens, routes, numerators, packed, routes_in, numerators_in, sems):
    width, top = tokens.shape[1], routes.shape[1]
    copies = [
        pltpu.make_async_copy(tokens, packed.at[:, pl.ds(0, width)], sems.at[0]),
        pltpu.make_async_copy(routes, routes_in, sems.at[1]),
        pltpu.make_async_copy(numerators, numerators_in, sems.at[2]),
    ]
    for copy in copies:
        copy.start()
    packed[:, width:] = jnp.zeros((packed.shape[0], packed.shape[1] - width), packed.dtype)
    for copy in copies[1:]:
        copy.wait()
    packed[:, width : width + top] = routes_in[...].astype(jnp.float32).astype(packed.dtype)
    packed[:, width + top : width + 2 * top] = numerators_in[...].astype(jnp.float32).astype(packed.dtype)
    copies[0].wait()


def pack(tokens, routes, numerators):
    count, width = tokens.shape
    return pl.pallas_call(
        pack_kernel,
        out_shape=jax.ShapeDtypeStruct((count, width + 128), tokens.dtype),
        in_specs=[HBM] * 3,
        out_specs=VMEM,
        scratch_shapes=[
            pltpu.VMEM(routes.shape, routes.dtype),
            pltpu.VMEM(numerators.shape, numerators.dtype),
            pltpu.SemaphoreType.DMA((3,)),
        ],
        compiler_params=pltpu.CompilerParams(vmem_limit_bytes=4 << 20),
        cost_estimate=pl.CostEstimate(flops=20 * 10**9, bytes_accessed=4 * tokens.size, transcendentals=0),
    )(in_hbm(tokens), in_hbm(routes), in_hbm(numerators))


def gate_up_kernel(x, base, out):
    depth, _, columns = base.shape
    step = 512
    row = lax.broadcasted_iota(jnp.int32, (128, 256), 0)
    column = lax.broadcasted_iota(jnp.int32, (128, 256), 1)
    spread = jnp.where(column // 2 == row, 1.0, 0.0).astype(jnp.bfloat16)
    is_odd = (lax.broadcasted_iota(jnp.int32, (1, 2 * step), 1) % 2).astype(jnp.float32)
    odd_mask, even_mask = is_odd.astype(jnp.bfloat16), (1.0 - is_odd).astype(jnp.bfloat16)
    count = x.shape[0]
    flat = base.reshape(2 * depth, columns)
    total = jnp.zeros(out.shape, jnp.float32)
    for k in range(0, depth, step):
        stacked = jnp.concatenate([x[:, i : i + 128] for i in range(k, k + step, 128)])
        wide = jnp.dot(stacked, spread, preferred_element_type=jnp.float32).astype(jnp.bfloat16)
        wide = jnp.concatenate([wide[i : i + count] for i in range(0, stacked.shape[0], count)], axis=1)
        total += jnp.dot(
            jnp.concatenate([wide * even_mask, wide * odd_mask]),
            flat[2 * k : 2 * (k + step), :],
            preferred_element_type=jnp.float32,
        )
    out[...] = total


def gate_up_product(x, base):
    depth, _, columns = base.shape
    return pl.pallas_call(
        gate_up_kernel,
        out_shape=jax.ShapeDtypeStruct((2 * x.shape[0], columns), jnp.float32),
        in_specs=[VMEM, VMEM],
        out_specs=VMEM,
        compiler_params=pltpu.CompilerParams(vmem_limit_bytes=16 << 20),
        cost_estimate=pl.CostEstimate(
            flops=4 * x.shape[0] * depth * columns, bytes_accessed=2 * base.size, transcendentals=0
        ),
    )(x, base)


def local(
    tokens,
    routes,
    numerators,
    place,
    base_in,
    base_down,
    delta_in,
    delta_mid,
    delta_down,
    delta_back,
):
    clusters = lax.axis_size("expert")
    members = lax.axis_size("tensor")
    me = lax.axis_index("tensor")
    cluster = lax.axis_index("expert")
    core = me % 2
    count, width = tokens.shape[1:]
    top = routes.shape[2]

    along, across = halves(clusters), halves(members // 2)
    shared, paired = along[: len(along) - len(across)], along[len(along) - len(across) :]

    other_back = trade(delta_back[0], (0, 1), (0, 1))

    packed = pack(tokens[0], routes[0], numerators[0])
    chips = members // 2
    pieces = {(0, 0): packed}
    for z in range(clusters - 1, 0, -1):
        pieces[0, z] = trade(packed, (z, 0), (z, 0))
    for x in range(1, chips):
        pieces[x, 0] = trade(packed, (0, 2 * x), (0, 2 * x))
    rest = jnp.concatenate([pieces[0, z] for z in range(1, clusters)])
    for x in range(1, chips):
        received = trade(rest, (0, 2 * x), (0, 2 * x))
        for z in range(1, clusters):
            pieces[x, z] = received[(z - 1) * count : z * count]

    for bit in across:
        for x in range(chips):
            if not x & bit:
                for z in range(clusters):
                    flag = (me // (2 * bit)) % 2 == 1
                    pieces[x, z], pieces[x | bit, z] = ordered(flag, pieces[x, z], pieces[x | bit, z])
    places = [(0, 0)]
    for mask in shared:
        places += [(x, z | mask) for x, z in places]
    for zbit, xbit in zip(paired, across):
        places += [(x | xbit, z) for x, z in places]
        places += [(x, z | zbit) for x, z in places]
    held = by_rows(jnp.concatenate([pieces[place] for place in places]))
    held, other_back = lax.optimization_barrier((held, other_back))
    half = held.shape[0]
    held = by_rows(jnp.concatenate(ordered(core == 1, held, trade(held, (0, 1), (0, 1)))))

    codes = jnp.dot(held[:, :width], delta_in[0], preferred_element_type=jnp.float32).astype(jnp.bfloat16)
    rank = codes.shape[1]
    codes = jnp.stack([codes if m == 0 else trade(codes, (0, m), (0, m)) for m in range(members)])
    by_slot = jnp.stack([lax.dynamic_index_in_dim(codes, s ^ me, 0, keepdims=False) for s in range(members)])
    projected = gate_up_product(held, base_in[0])

    side = by_rows(held[:, width:])
    all_routes = side[:, :top].astype(jnp.int32)
    numerator = side[:, top : 2 * top].astype(jnp.float32)
    position = lookup(place, all_routes)
    weight = (2.5 * numerator / jnp.sum(numerator, axis=-1, keepdims=True)).astype(jnp.bfloat16)
    target = cluster * members + jnp.arange(members, dtype=jnp.int32)
    scale = jnp.sum(
        jnp.where(position[None] == target[:, None, None], weight[None].astype(jnp.float32), 0.0), axis=-1
    )

    lifted = jnp.einsum("srk,skgf->srgf", by_slot, delta_mid[0], preferred_element_type=jnp.float32)
    total = held.shape[0]
    hidden = jax.nn.silu(projected[None, :total] + lifted[:, :, 0]) * (projected[None, total:] + lifted[:, :, 1])
    hidden_sum = jnp.sum(scale[:, :, None] * hidden, axis=0).astype(jnp.bfloat16)
    partial_codes = jnp.einsum(
        "srf,sfk->srk", hidden.astype(jnp.bfloat16), delta_down[0], preferred_element_type=jnp.float32
    ).astype(jnp.bfloat16)
    partial_codes = partial_codes.reshape(chips, 2, 2, half, rank).transpose(0, 2, 1, 3, 4)
    partial_codes = partial_codes.reshape(members, 2, half, rank)
    lowrank = lax.dynamic_index_in_dim(partial_codes, me, 0, keepdims=False).astype(jnp.float32)
    for m in range(1, members):
        sent = lax.dynamic_index_in_dim(partial_codes, me ^ m, 0, keepdims=False)
        lowrank = lowrank + trade(sent, (0, m), (0, m)).astype(jnp.float32)
    kept_scale = scale.reshape(chips, 2, 2, half).transpose(0, 2, 1, 3).reshape(members, 2, half)
    kept_scale = lax.dynamic_index_in_dim(kept_scale, me, 0, keepdims=False)
    scaled = (kept_scale[:, :, None] * lowrank).astype(jnp.bfloat16)
    scaled = ordered(core == 1, scaled[0], scaled[1])

    base = jnp.dot(hidden_sum, base_down[0], preferred_element_type=jnp.float32)
    kept, sent = ordered(core == 1, base[:half], base[half:])
    total = kept + trade(sent.astype(jnp.bfloat16), (0, 1), (0, 1)).astype(jnp.float32)
    for rows, table in zip(scaled, (delta_back[0], other_back)):
        total = total + jnp.dot(rows, table, preferred_element_type=jnp.float32)
    total = total.astype(jnp.bfloat16)

    def add(kept, received):
        return (kept.astype(jnp.float32) + received.astype(jnp.float32)).astype(jnp.bfloat16)

    for z, x in reversed(list(zip(paired, across))):
        flag = (me // (2 * x)) % 2 == 1
        size = total.shape[0] // 4
        blocks = [total[i * size : (i + 1) * size] for i in range(4)]
        inner = ordered(core == 1, blocks[1], blocks[2])
        kept, sent = ordered(
            (core == 1) & flag,
            jnp.concatenate([blocks[0], inner[0]]),
            jnp.concatenate([inner[1], blocks[3]]),
        )
        total = add(kept, trade(sent, (z, 0), (0, 2 * x)))
        kept, sent = ordered((core == 0) & flag, total[:size], total[size:])
        total = add(kept, trade(sent, (0, 2 * x), (z, 0)))
    for mask in reversed(shared):
        size = total.shape[0] // 2
        total = add(total[:size], trade(total[size:], (mask, 0), (mask, 0)))
    return total[None]


def solution(mesh):
    placed = (
        P(None, ("parts", "expert", "tensor"), None),
        P(None, ("parts", "expert", "tensor"), None),
        P(None, ("parts", "expert", "tensor"), None),
        P("parts"),
        P("expert", None, None, "tensor"),
        P("expert", "tensor", None),
        P(("expert", "tensor"), None, None),
        P("expert", None, None, None, "tensor"),
        P("expert", None, "tensor", None),
        P(("expert", "tensor"), None, None),
    )
    return jax.shard_map(
        local,
        mesh=mesh,
        in_specs=placed,
        out_specs=P(None, ("parts", "expert", "tensor"), None),
        check_vma=False,
    )
```

```python
import jax
import jax.numpy as jnp
from jax import lax
from jax.experimental import pallas as pl
from jax.experimental.pallas import tpu as pltpu
from jax.experimental.layout import Layout, with_layout_constraint
from jax.sharding import PartitionSpec as P

CHUNKS = 2
VMEM = pl.BlockSpec(memory_space=pltpu.VMEM)
HBM = pl.BlockSpec(memory_space=pltpu.HBM)


def in_hbm(value):
    return pltpu.with_memory_space_constraint(value, pltpu.HBM)


def by_rows(value):
    return with_layout_constraint(value, Layout((0, 1)))


def lookup(table, index):
    keys = jnp.arange(table.shape[0], dtype=jnp.int32)
    return jnp.sum(jnp.where(index[..., None] == keys, table, 0), axis=-1)


def trade(value, even, odd):
    members = lax.axis_size("tensor")
    pairs = []
    for e in range(lax.axis_size("expert")):
        for t in range(members):
            along, across = odd if t % 2 else even
            pairs.append((e * members + t, (e ^ along) * members + (t ^ across)))
    return lax.ppermute(value, ("expert", "tensor"), pairs)


def halves(size):
    masks = []
    while size > 1:
        size //= 2
        masks.append(size)
    return masks


def ordered(flip, first, second):
    return jnp.where(flip, second, first), jnp.where(flip, first, second)


def pack_kernel(tokens, routes, numerators, packed, routes_in, numerators_in, sems):
    width, top = tokens.shape[1], routes.shape[1]
    copies = [
        pltpu.make_async_copy(tokens, packed.at[:, pl.ds(0, width)], sems.at[0]),
        pltpu.make_async_copy(routes, routes_in, sems.at[1]),
        pltpu.make_async_copy(numerators, numerators_in, sems.at[2]),
    ]
    for copy in copies:
        copy.start()
    packed[:, width:] = jnp.zeros((packed.shape[0], packed.shape[1] - width), packed.dtype)
    for copy in copies[1:]:
        copy.wait()
    packed[:, width : width + top] = routes_in[...].astype(jnp.float32).astype(packed.dtype)
    packed[:, width + top : width + 2 * top] = numerators_in[...].astype(jnp.float32).astype(packed.dtype)
    copies[0].wait()


def pack(tokens, routes, numerators):
    count, width = tokens.shape
    return pl.pallas_call(
        pack_kernel,
        out_shape=jax.ShapeDtypeStruct((count, width + 128), tokens.dtype),
        in_specs=[HBM] * 3,
        out_specs=VMEM,
        scratch_shapes=[
            pltpu.VMEM(routes.shape, routes.dtype),
            pltpu.VMEM(numerators.shape, numerators.dtype),
            pltpu.SemaphoreType.DMA((3,)),
        ],
        compiler_params=pltpu.CompilerParams(vmem_limit_bytes=4 << 20),
        cost_estimate=pl.CostEstimate(flops=20 * 10**9, bytes_accessed=4 * tokens.size, transcendentals=0),
    )(in_hbm(tokens), in_hbm(routes), in_hbm(numerators))


def gate_up_kernel(x, base, out):
    depth, _, columns = base.shape
    step = 512
    row = lax.broadcasted_iota(jnp.int32, (128, 256), 0)
    column = lax.broadcasted_iota(jnp.int32, (128, 256), 1)
    spread = jnp.where(column // 2 == row, 1.0, 0.0).astype(jnp.bfloat16)
    is_odd = (lax.broadcasted_iota(jnp.int32, (1, 2 * step), 1) % 2).astype(jnp.float32)
    odd_mask, even_mask = is_odd.astype(jnp.bfloat16), (1.0 - is_odd).astype(jnp.bfloat16)
    count = x.shape[0]
    flat = base.reshape(2 * depth, columns)
    total = jnp.zeros(out.shape, jnp.float32)
    for k in range(0, depth, step):
        stacked = jnp.concatenate([x[:, i : i + 128] for i in range(k, k + step, 128)])
        wide = jnp.dot(stacked, spread, preferred_element_type=jnp.float32).astype(jnp.bfloat16)
        wide = jnp.concatenate([wide[i : i + count] for i in range(0, stacked.shape[0], count)], axis=1)
        total += jnp.dot(
            jnp.concatenate([wide * even_mask, wide * odd_mask]),
            flat[2 * k : 2 * (k + step), :],
            preferred_element_type=jnp.float32,
        )
    out[...] = total


def gate_up_product(x, base):
    depth, _, columns = base.shape
    return pl.pallas_call(
        gate_up_kernel,
        out_shape=jax.ShapeDtypeStruct((2 * x.shape[0], columns), jnp.float32),
        in_specs=[VMEM, VMEM],
        out_specs=VMEM,
        compiler_params=pltpu.CompilerParams(vmem_limit_bytes=16 << 20),
        cost_estimate=pl.CostEstimate(
            flops=4 * x.shape[0] * depth * columns, bytes_accessed=2 * base.size, transcendentals=0
        ),
    )(x, base)


def in_vmem(value):
    return pltpu.with_memory_space_constraint(value, pltpu.VMEM)


def down_kernel(hidden, base, sent, kept):
    half, width = kept.shape
    core = lax.axis_index("tensor") % 2
    first = pl.ds(pl.multiple_of((1 - core) * half, half), half)
    second = pl.ds(pl.multiple_of(core * half, half), half)
    rows = jnp.concatenate([hidden[first, :], hidden[second, :]])
    for k in range(0, width, 1024):
        total = jnp.dot(rows, base[:, k : k + 1024], preferred_element_type=jnp.float32)
        sent[:, k : k + 1024] = total[:half].astype(sent.dtype)
        kept[:, k : k + 1024] = total[half:]


def down_product(hidden, base):
    rows, width = hidden.shape[0], base.shape[1]
    return pl.pallas_call(
        down_kernel,
        out_shape=(
            jax.ShapeDtypeStruct((rows // 2, width), jnp.bfloat16),
            jax.ShapeDtypeStruct((rows // 2, width), jnp.float32),
        ),
        in_specs=[VMEM, VMEM],
        out_specs=(VMEM, VMEM),
        compiler_params=pltpu.CompilerParams(vmem_limit_bytes=16 << 20),
        cost_estimate=pl.CostEstimate(flops=2 * rows * base.size, bytes_accessed=2 * base.size, transcendentals=0),
    )(hidden, in_vmem(base))


def finish_kernel(kept, received, own, other, own_back, other_back, *outs):
    scaled = jnp.concatenate([own[...], other[...]], axis=1)
    step = outs[0].shape[1]
    for i, out in enumerate(outs):
        columns = slice(i * step, (i + 1) * step)
        back = jnp.concatenate([own_back[:, columns], other_back[:, columns]])
        total = kept[:, columns] + received[:, columns].astype(jnp.float32)
        total += jnp.dot(scaled, back, preferred_element_type=jnp.float32)
        out[...] = total.astype(out.dtype)


def finish(kept, received, scaled, backs):
    rows, width = kept.shape
    return pl.pallas_call(
        finish_kernel,
        out_shape=[jax.ShapeDtypeStruct((rows, width // CHUNKS), jnp.bfloat16)] * CHUNKS,
        in_specs=[VMEM] * 6,
        out_specs=[VMEM] * CHUNKS,
        compiler_params=pltpu.CompilerParams(vmem_limit_bytes=16 << 20),
        cost_estimate=pl.CostEstimate(
            flops=4 * rows * backs[0].size, bytes_accessed=4 * backs[0].size, transcendentals=0
        ),
    )(kept, received, *scaled, *map(in_vmem, backs))


def local(
    tokens,
    routes,
    numerators,
    place,
    base_in,
    base_down,
    delta_in,
    delta_mid,
    delta_down,
    delta_back,
):
    clusters = lax.axis_size("expert")
    members = lax.axis_size("tensor")
    me = lax.axis_index("tensor")
    cluster = lax.axis_index("expert")
    core = me % 2
    count, width = tokens.shape[1:]
    top = routes.shape[2]

    along, across = halves(clusters), halves(members // 2)
    shared, paired = along[: len(along) - len(across)], along[len(along) - len(across) :]

    other_back = trade(delta_back[0], (0, 1), (0, 1))

    packed = pack(tokens[0], routes[0], numerators[0])
    chips = members // 2
    pieces = {(0, 0): packed}
    for z in range(clusters - 1, 0, -1):
        pieces[0, z] = trade(packed, (z, 0), (z, 0))
    for x in range(1, chips):
        pieces[x, 0] = trade(packed, (0, 2 * x), (0, 2 * x))
    rest = jnp.concatenate([pieces[0, z] for z in range(1, clusters)])
    for x in range(1, chips):
        received = trade(rest, (0, 2 * x), (0, 2 * x))
        for z in range(1, clusters):
            pieces[x, z] = received[(z - 1) * count : z * count]

    for bit in across:
        for x in range(chips):
            if not x & bit:
                for z in range(clusters):
                    flag = (me // (2 * bit)) % 2 == 1
                    pieces[x, z], pieces[x | bit, z] = ordered(flag, pieces[x, z], pieces[x | bit, z])
    places = [(0, 0)]
    for mask in shared:
        places += [(x, z | mask) for x, z in places]
    for zbit, xbit in zip(paired, across):
        places += [(x | xbit, z) for x, z in places]
        places += [(x, z | zbit) for x, z in places]
    held = by_rows(jnp.concatenate([pieces[place] for place in places]))
    held, other_back = lax.optimization_barrier((held, other_back))
    half = held.shape[0]
    held = by_rows(jnp.concatenate(ordered(core == 1, held, trade(held, (0, 1), (0, 1)))))

    codes = jnp.dot(held[:, :width], delta_in[0], preferred_element_type=jnp.float32).astype(jnp.bfloat16)
    rank = codes.shape[1]
    codes = jnp.stack([codes if m == 0 else trade(codes, (0, m), (0, m)) for m in range(members)])
    by_slot = jnp.stack([lax.dynamic_index_in_dim(codes, s ^ me, 0, keepdims=False) for s in range(members)])
    projected = gate_up_product(held, base_in[0])

    side = by_rows(held[:, width:])
    all_routes = side[:, :top].astype(jnp.int32)
    numerator = side[:, top : 2 * top].astype(jnp.float32)
    position = lookup(place, all_routes)
    weight = (2.5 * numerator / jnp.sum(numerator, axis=-1, keepdims=True)).astype(jnp.bfloat16)
    target = cluster * members + jnp.arange(members, dtype=jnp.int32)
    scale = jnp.sum(
        jnp.where(position[None] == target[:, None, None], weight[None].astype(jnp.float32), 0.0), axis=-1
    )

    lifted = jnp.einsum("srk,skgf->srgf", by_slot, delta_mid[0], preferred_element_type=jnp.float32)
    total = held.shape[0]
    hidden = jax.nn.silu(projected[None, :total] + lifted[:, :, 0]) * (projected[None, total:] + lifted[:, :, 1])
    hidden_sum = jnp.sum(scale[:, :, None] * hidden, axis=0).astype(jnp.bfloat16)
    partial_codes = jnp.einsum(
        "srf,sfk->srk", hidden.astype(jnp.bfloat16), delta_down[0], preferred_element_type=jnp.float32
    ).astype(jnp.bfloat16)
    partial_codes = partial_codes.reshape(chips, 2, 2, half, rank).transpose(0, 2, 1, 3, 4)
    partial_codes = partial_codes.reshape(members, 2, half, rank)
    lowrank = lax.dynamic_index_in_dim(partial_codes, me, 0, keepdims=False).astype(jnp.float32)
    for m in range(1, members):
        sent = lax.dynamic_index_in_dim(partial_codes, me ^ m, 0, keepdims=False)
        lowrank = lowrank + trade(sent, (0, m), (0, m)).astype(jnp.float32)
    kept_scale = scale.reshape(chips, 2, 2, half).transpose(0, 2, 1, 3).reshape(members, 2, half)
    kept_scale = lax.dynamic_index_in_dim(kept_scale, me, 0, keepdims=False)
    scaled = (kept_scale[:, :, None] * lowrank).astype(jnp.bfloat16)
    scaled = ordered(core == 1, scaled[0], scaled[1])

    sent, kept = down_product(hidden_sum, base_down[0])
    totals = finish(kept, trade(sent, (0, 1), (0, 1)), scaled, (delta_back[0], other_back))

    def add(kept, received):
        return (kept.astype(jnp.float32) + received.astype(jnp.float32)).astype(jnp.bfloat16)

    outputs = []
    for total in totals:
        for z, x in reversed(list(zip(paired, across))):
            flag = (me // (2 * x)) % 2 == 1
            size = total.shape[0] // 4
            blocks = [total[i * size : (i + 1) * size] for i in range(4)]
            inner = ordered(core == 1, blocks[1], blocks[2])
            kept, sent = ordered(
                (core == 1) & flag,
                jnp.concatenate([blocks[0], inner[0]]),
                jnp.concatenate([inner[1], blocks[3]]),
            )
            total = add(kept, trade(sent, (z, 0), (0, 2 * x)))
            kept, sent = ordered((core == 0) & flag, total[:size], total[size:])
            total = add(kept, trade(sent, (0, 2 * x), (z, 0)))
        for mask in reversed(shared):
            size = total.shape[0] // 2
            total = add(total[:size], trade(total[size:], (mask, 0), (mask, 0)))
        outputs.append(total)
    return jnp.concatenate(outputs, axis=1)[None]


def solution(mesh):
    placed = (
        P(None, ("parts", "expert", "tensor"), None),
        P(None, ("parts", "expert", "tensor"), None),
        P(None, ("parts", "expert", "tensor"), None),
        P("parts"),
        P("expert", None, None, "tensor"),
        P("expert", "tensor", None),
        P(("expert", "tensor"), None, None),
        P("expert", None, None, None, "tensor"),
        P("expert", None, "tensor", None),
        P(("expert", "tensor"), None, None),
    )
    return jax.shard_map(
        local,
        mesh=mesh,
        in_specs=placed,
        out_specs=P(None, ("parts", "expert", "tensor"), None),
        check_vma=False,
    )
```

```python
import jax
import jax.numpy as jnp
from jax import lax
from jax.experimental import pallas as pl
from jax.experimental.pallas import tpu as pltpu
from jax.experimental.layout import Layout, with_layout_constraint
from jax.sharding import PartitionSpec as P

CHUNKS = 2
VMEM = pl.BlockSpec(memory_space=pltpu.VMEM)
HBM = pl.BlockSpec(memory_space=pltpu.HBM)


def in_vmem(value):
    return pltpu.with_memory_space_constraint(value, pltpu.VMEM)


def in_hbm(value):
    return pltpu.with_memory_space_constraint(value, pltpu.HBM)


def by_rows(value):
    return with_layout_constraint(value, Layout((0, 1)))


def lookup(table, index):
    keys = jnp.arange(table.shape[0], dtype=jnp.int32)
    return jnp.sum(jnp.where(index[..., None] == keys, table, 0), axis=-1)


def trade(value, even, odd):
    members = lax.axis_size("tensor")
    pairs = []
    for e in range(lax.axis_size("expert")):
        for t in range(members):
            along, across = odd if t % 2 else even
            pairs.append((e * members + t, (e ^ along) * members + (t ^ across)))
    return lax.ppermute(value, ("expert", "tensor"), pairs)


def halves(size):
    masks = []
    while size > 1:
        size //= 2
        masks.append(size)
    return masks


def ordered(flip, first, second):
    return jnp.where(flip, second, first), jnp.where(flip, first, second)


def pack_kernel(tokens, routes, numerators, packed, routes_in, numerators_in, sems):
    width, top = tokens.shape[1], routes.shape[1]
    copies = [
        pltpu.make_async_copy(tokens, packed.at[:, pl.ds(0, width)], sems.at[0]),
        pltpu.make_async_copy(routes, routes_in, sems.at[1]),
        pltpu.make_async_copy(numerators, numerators_in, sems.at[2]),
    ]
    for copy in copies:
        copy.start()
    packed[:, width:] = jnp.zeros((packed.shape[0], packed.shape[1] - width), packed.dtype)
    for copy in copies[1:]:
        copy.wait()
    packed[:, width : width + top] = routes_in[...].astype(jnp.float32).astype(packed.dtype)
    packed[:, width + top : width + 2 * top] = numerators_in[...].astype(jnp.float32).astype(packed.dtype)
    copies[0].wait()


def pack(tokens, routes, numerators):
    count, width = tokens.shape
    return pl.pallas_call(
        pack_kernel,
        out_shape=jax.ShapeDtypeStruct((count, width + 128), tokens.dtype),
        in_specs=[HBM] * 3,
        out_specs=VMEM,
        scratch_shapes=[
            pltpu.VMEM(routes.shape, routes.dtype),
            pltpu.VMEM(numerators.shape, numerators.dtype),
            pltpu.SemaphoreType.DMA((3,)),
        ],
        compiler_params=pltpu.CompilerParams(vmem_limit_bytes=4 << 20),
        cost_estimate=pl.CostEstimate(flops=20 * 10**9, bytes_accessed=4 * tokens.size, transcendentals=0),
    )(in_hbm(tokens), in_hbm(routes), in_hbm(numerators))


def gate_up_kernel(x, base, out):
    depth, _, columns = base.shape
    step = 512
    row = lax.broadcasted_iota(jnp.int32, (128, 256), 0)
    column = lax.broadcasted_iota(jnp.int32, (128, 256), 1)
    spread = jnp.where(column // 2 == row, 1.0, 0.0).astype(jnp.bfloat16)
    is_odd = (lax.broadcasted_iota(jnp.int32, (1, 2 * step), 1) % 2).astype(jnp.float32)
    odd_mask, even_mask = is_odd.astype(jnp.bfloat16), (1.0 - is_odd).astype(jnp.bfloat16)
    count = x.shape[0]
    flat = base.reshape(2 * depth, columns)
    total = jnp.zeros(out.shape, jnp.float32)
    for k in range(0, depth, step):
        stacked = jnp.concatenate([x[:, i : i + 128] for i in range(k, k + step, 128)])
        wide = jnp.dot(stacked, spread, preferred_element_type=jnp.float32).astype(jnp.bfloat16)
        wide = jnp.concatenate([wide[i : i + count] for i in range(0, stacked.shape[0], count)], axis=1)
        total += jnp.dot(
            jnp.concatenate([wide * even_mask, wide * odd_mask]),
            flat[2 * k : 2 * (k + step), :],
            preferred_element_type=jnp.float32,
        )
    out[...] = total


def gate_up_product(x, base):
    depth, _, columns = base.shape
    return pl.pallas_call(
        gate_up_kernel,
        out_shape=jax.ShapeDtypeStruct((2 * x.shape[0], columns), jnp.float32),
        in_specs=[VMEM, VMEM],
        out_specs=VMEM,
        compiler_params=pltpu.CompilerParams(vmem_limit_bytes=16 << 20),
        cost_estimate=pl.CostEstimate(flops=10**10, bytes_accessed=2 * base.size, transcendentals=0),
    )(x, in_vmem(base))


def join_kernel(own, received, joined):
    half = own.shape[0]
    core = lax.axis_index("tensor") % 2
    joined[pl.ds(pl.multiple_of(core * half, half), half), :] = own[...]
    joined[pl.ds(pl.multiple_of((1 - core) * half, half), half), :] = received[...]


def join(own, received):
    rows, width = own.shape
    return pl.pallas_call(
        join_kernel,
        out_shape=jax.ShapeDtypeStruct((2 * rows, width), own.dtype),
        in_specs=[VMEM, VMEM],
        out_specs=VMEM,
        compiler_params=pltpu.CompilerParams(vmem_limit_bytes=16 << 20),
        cost_estimate=pl.CostEstimate(flops=10**10, bytes_accessed=6 * own.size, transcendentals=0),
    )(own, received)


def down_kernel(hidden, base, sent, kept):
    half, width = kept.shape
    core = lax.axis_index("tensor") % 2
    first = pl.ds(pl.multiple_of((1 - core) * half, half), half)
    second = pl.ds(pl.multiple_of(core * half, half), half)
    rows = jnp.concatenate([hidden[first, :], hidden[second, :]])
    for k in range(0, width, 1024):
        total = jnp.dot(rows, base[:, k : k + 1024], preferred_element_type=jnp.float32)
        sent[:, k : k + 1024] = total[:half].astype(sent.dtype)
        kept[:, k : k + 1024] = total[half:]


def down_product(hidden, base):
    rows, width = hidden.shape[0], base.shape[1]
    return pl.pallas_call(
        down_kernel,
        out_shape=(
            jax.ShapeDtypeStruct((rows // 2, width), jnp.bfloat16),
            jax.ShapeDtypeStruct((rows // 2, width), jnp.float32),
        ),
        in_specs=[VMEM, VMEM],
        out_specs=(VMEM, VMEM),
        compiler_params=pltpu.CompilerParams(vmem_limit_bytes=16 << 20),
        cost_estimate=pl.CostEstimate(flops=2 * rows * base.size, bytes_accessed=2 * base.size, transcendentals=0),
    )(hidden, in_vmem(base))


def finish_kernel(kept, received, own, other, own_back, other_back, *outs):
    size, step = outs[0].shape[1], 512
    for i, out in enumerate(outs):
        for k in range(0, size, step):
            columns = slice(i * size + k, i * size + k + step)
            total = kept[:, columns] + received[:, columns].astype(jnp.float32)
            total += jnp.dot(own[...], own_back[:, columns], preferred_element_type=jnp.float32)
            total += jnp.dot(other[...], other_back[:, columns], preferred_element_type=jnp.float32)
            out[:, k : k + step] = total.astype(out.dtype)


def finish(kept, received, scaled, backs):
    rows, width = kept.shape
    return pl.pallas_call(
        finish_kernel,
        out_shape=[jax.ShapeDtypeStruct((rows, width // CHUNKS), jnp.bfloat16)] * CHUNKS,
        in_specs=[VMEM] * 6,
        out_specs=[VMEM] * CHUNKS,
        compiler_params=pltpu.CompilerParams(vmem_limit_bytes=16 << 20),
        cost_estimate=pl.CostEstimate(
            flops=4 * rows * backs[0].size, bytes_accessed=4 * backs[0].size, transcendentals=0
        ),
    )(kept, received, *scaled, *map(in_vmem, backs))


def local(
    tokens,
    routes,
    numerators,
    place,
    base_in,
    base_down,
    delta_in,
    delta_mid,
    delta_down,
    delta_back,
):
    clusters = lax.axis_size("expert")
    members = lax.axis_size("tensor")
    me = lax.axis_index("tensor")
    cluster = lax.axis_index("expert")
    core = me % 2
    count, width = tokens.shape[1:]
    top = routes.shape[2]

    along, across = halves(clusters), halves(members // 2)
    shared, paired = along[: len(along) - len(across)], along[len(along) - len(across) :]

    other_back = trade(delta_back[0], (0, 1), (0, 1))

    packed = pack(tokens[0], routes[0], numerators[0])
    chips = members // 2
    pieces = {(0, 0): packed}
    for z in range(clusters - 1, 0, -1):
        pieces[0, z] = trade(packed, (z, 0), (z, 0))
    for x in range(1, chips):
        pieces[x, 0] = trade(packed, (0, 2 * x), (0, 2 * x))
    rest = jnp.concatenate([pieces[0, z] for z in range(1, clusters)])
    for x in range(1, chips):
        received = trade(rest, (0, 2 * x), (0, 2 * x))
        for z in range(1, clusters):
            pieces[x, z] = received[(z - 1) * count : z * count]

    for bit in across:
        for x in range(chips):
            if not x & bit:
                for z in range(clusters):
                    flag = (me // (2 * bit)) % 2 == 1
                    pieces[x, z], pieces[x | bit, z] = ordered(flag, pieces[x, z], pieces[x | bit, z])
    places = [(0, 0)]
    for mask in shared:
        places += [(x, z | mask) for x, z in places]
    for zbit, xbit in zip(paired, across):
        places += [(x | xbit, z) for x, z in places]
        places += [(x, z | zbit) for x, z in places]
    held = by_rows(jnp.concatenate([pieces[place] for place in places]))
    held, other_back = lax.optimization_barrier((held, other_back))
    half = held.shape[0]
    held = join(held, trade(held, (0, 1), (0, 1)))

    codes = jnp.dot(held[:, :width], delta_in[0], preferred_element_type=jnp.float32).astype(jnp.bfloat16)
    rank = codes.shape[1]
    codes = jnp.stack([codes if m == 0 else trade(codes, (0, m), (0, m)) for m in range(members)])
    by_slot = jnp.stack([lax.dynamic_index_in_dim(codes, s ^ me, 0, keepdims=False) for s in range(members)])
    projected = gate_up_product(held, base_in[0])

    side = by_rows(held[:, width:])
    all_routes = side[:, :top].astype(jnp.int32)
    numerator = side[:, top : 2 * top].astype(jnp.float32)
    position = lookup(place, all_routes)
    weight = (2.5 * numerator / jnp.sum(numerator, axis=-1, keepdims=True)).astype(jnp.bfloat16)
    target = cluster * members + jnp.arange(members, dtype=jnp.int32)
    scale = jnp.sum(
        jnp.where(position[None] == target[:, None, None], weight[None].astype(jnp.float32), 0.0), axis=-1
    )

    lifted = jnp.einsum("srk,skgf->srgf", by_slot, delta_mid[0], preferred_element_type=jnp.float32)
    total = held.shape[0]
    hidden = jax.nn.silu(projected[None, :total] + lifted[:, :, 0]) * (projected[None, total:] + lifted[:, :, 1])
    hidden_sum = jnp.sum(scale[:, :, None] * hidden, axis=0).astype(jnp.bfloat16)
    partial_codes = jnp.einsum(
        "srf,sfk->srk", hidden.astype(jnp.bfloat16), delta_down[0], preferred_element_type=jnp.float32
    ).astype(jnp.bfloat16)
    partial_codes = partial_codes.reshape(chips, 2, 2, half, rank).transpose(0, 2, 1, 3, 4)
    partial_codes = partial_codes.reshape(members, 2, half, rank)
    lowrank = lax.dynamic_index_in_dim(partial_codes, me, 0, keepdims=False).astype(jnp.float32)
    for m in range(1, members):
        sent = lax.dynamic_index_in_dim(partial_codes, me ^ m, 0, keepdims=False)
        lowrank = lowrank + trade(sent, (0, m), (0, m)).astype(jnp.float32)
    kept_scale = scale.reshape(chips, 2, 2, half).transpose(0, 2, 1, 3).reshape(members, 2, half)
    kept_scale = lax.dynamic_index_in_dim(kept_scale, me, 0, keepdims=False)
    scaled = (kept_scale[:, :, None] * lowrank).astype(jnp.bfloat16)
    scaled = ordered(core == 1, scaled[0], scaled[1])

    sent, kept = down_product(hidden_sum, base_down[0])
    totals = finish(kept, trade(sent, (0, 1), (0, 1)), scaled, (delta_back[0], other_back))

    def add(kept, received):
        return (kept.astype(jnp.float32) + received.astype(jnp.float32)).astype(jnp.bfloat16)

    outputs = []
    for total in totals:
        for z, x in reversed(list(zip(paired, across))):
            flag = (me // (2 * x)) % 2 == 1
            size = total.shape[0] // 4
            blocks = [total[i * size : (i + 1) * size] for i in range(4)]
            inner = ordered(core == 1, blocks[1], blocks[2])
            kept, sent = ordered(
                (core == 1) & flag,
                jnp.concatenate([blocks[0], inner[0]]),
                jnp.concatenate([inner[1], blocks[3]]),
            )
            total = add(kept, trade(sent, (z, 0), (0, 2 * x)))
            kept, sent = ordered((core == 0) & flag, total[:size], total[size:])
            total = add(kept, trade(sent, (0, 2 * x), (z, 0)))
        for mask in reversed(shared):
            size = total.shape[0] // 2
            total = add(total[:size], trade(total[size:], (mask, 0), (mask, 0)))
        outputs.append(total)
    return jnp.concatenate(outputs, axis=1)[None]


def solution(mesh):
    placed = (
        P(None, ("parts", "expert", "tensor"), None),
        P(None, ("parts", "expert", "tensor"), None),
        P(None, ("parts", "expert", "tensor"), None),
        P("parts"),
        P("expert", None, None, "tensor"),
        P("expert", "tensor", None),
        P(("expert", "tensor"), None, None),
        P("expert", None, None, None, "tensor"),
        P("expert", None, "tensor", None),
        P(("expert", "tensor"), None, None),
    )
    return jax.shard_map(
        local,
        mesh=mesh,
        in_specs=placed,
        out_specs=P(None, ("parts", "expert", "tensor"), None),
        check_vma=False,
    )
```

```python
import jax
import jax.numpy as jnp
from jax import lax
from jax.experimental import pallas as pl
from jax.experimental.pallas import tpu as pltpu
from jax.experimental.layout import Layout, with_layout_constraint
from jax.sharding import PartitionSpec as P

CHUNKS = 2
VMEM = pl.BlockSpec(memory_space=pltpu.VMEM)
HBM = pl.BlockSpec(memory_space=pltpu.HBM)


def in_hbm(value):
    return pltpu.with_memory_space_constraint(value, pltpu.HBM)


def by_rows(value):
    return with_layout_constraint(value, Layout((0, 1)))


def lookup(table, index):
    keys = jnp.arange(table.shape[0], dtype=jnp.int32)
    return jnp.sum(jnp.where(index[..., None] == keys, table, 0), axis=-1)


def trade(value, even, odd):
    members = lax.axis_size("tensor")
    pairs = []
    for e in range(lax.axis_size("expert")):
        for t in range(members):
            along, across = odd if t % 2 else even
            pairs.append((e * members + t, (e ^ along) * members + (t ^ across)))
    return lax.ppermute(value, ("expert", "tensor"), pairs)


def halves(size):
    masks = []
    while size > 1:
        size //= 2
        masks.append(size)
    return masks


def ordered(flip, first, second):
    return jnp.where(flip, second, first), jnp.where(flip, first, second)


def pack_kernel(tokens, routes, numerators, packed, routes_in, numerators_in, sems):
    width, top = tokens.shape[1], routes.shape[1]
    copies = [
        pltpu.make_async_copy(tokens, packed.at[:, pl.ds(0, width)], sems.at[0]),
        pltpu.make_async_copy(routes, routes_in, sems.at[1]),
        pltpu.make_async_copy(numerators, numerators_in, sems.at[2]),
    ]
    for copy in copies:
        copy.start()
    packed[:, width:] = jnp.zeros((packed.shape[0], packed.shape[1] - width), packed.dtype)
    for copy in copies[1:]:
        copy.wait()
    packed[:, width : width + top] = routes_in[...].astype(jnp.float32).astype(packed.dtype)
    packed[:, width + top : width + 2 * top] = numerators_in[...].astype(jnp.float32).astype(packed.dtype)
    copies[0].wait()


def pack(tokens, routes, numerators):
    count, width = tokens.shape
    return pl.pallas_call(
        pack_kernel,
        out_shape=jax.ShapeDtypeStruct((count, width + 128), tokens.dtype),
        in_specs=[HBM] * 3,
        out_specs=VMEM,
        scratch_shapes=[
            pltpu.VMEM(routes.shape, routes.dtype),
            pltpu.VMEM(numerators.shape, numerators.dtype),
            pltpu.SemaphoreType.DMA((3,)),
        ],
        compiler_params=pltpu.CompilerParams(vmem_limit_bytes=4 << 20),
        cost_estimate=pl.CostEstimate(flops=0, bytes_accessed=4 * tokens.size, transcendentals=0),
    )(in_hbm(tokens), in_hbm(routes), in_hbm(numerators))


def gate_up_kernel(x, base, out):
    depth, _, columns = base.shape
    step = 512
    row = lax.broadcasted_iota(jnp.int32, (128, 256), 0)
    column = lax.broadcasted_iota(jnp.int32, (128, 256), 1)
    spread = jnp.where(column // 2 == row, 1.0, 0.0).astype(jnp.bfloat16)
    is_odd = (lax.broadcasted_iota(jnp.int32, (1, 2 * step), 1) % 2).astype(jnp.float32)
    odd_mask, even_mask = is_odd.astype(jnp.bfloat16), (1.0 - is_odd).astype(jnp.bfloat16)
    count = x.shape[0]
    flat = base.reshape(2 * depth, columns)
    total = jnp.zeros(out.shape, jnp.float32)
    for k in range(0, depth, step):
        stacked = jnp.concatenate([x[:, i : i + 128] for i in range(k, k + step, 128)])
        wide = jnp.dot(stacked, spread, preferred_element_type=jnp.float32).astype(jnp.bfloat16)
        wide = jnp.concatenate([wide[i : i + count] for i in range(0, stacked.shape[0], count)], axis=1)
        total += jnp.dot(
            jnp.concatenate([wide * even_mask, wide * odd_mask]),
            flat[2 * k : 2 * (k + step), :],
            preferred_element_type=jnp.float32,
        )
    out[...] = total


def gate_up_product(x, base):
    depth, _, columns = base.shape
    return pl.pallas_call(
        gate_up_kernel,
        out_shape=jax.ShapeDtypeStruct((2 * x.shape[0], columns), jnp.float32),
        in_specs=[VMEM, VMEM],
        out_specs=VMEM,
        compiler_params=pltpu.CompilerParams(vmem_limit_bytes=16 << 20),
        cost_estimate=pl.CostEstimate(
            flops=4 * x.shape[0] * depth * columns, bytes_accessed=2 * base.size, transcendentals=0
        ),
    )(x, base)


def local(
    tokens,
    routes,
    numerators,
    place,
    base_in,
    base_down,
    delta_in,
    delta_mid,
    delta_down,
    delta_back,
):
    clusters = lax.axis_size("expert")
    members = lax.axis_size("tensor")
    me = lax.axis_index("tensor")
    cluster = lax.axis_index("expert")
    core = me % 2
    count, width = tokens.shape[1:]
    top = routes.shape[2]

    along, across = halves(clusters), halves(members // 2)
    shared, paired = along[: len(along) - len(across)], along[len(along) - len(across) :]

    packed = pack(tokens[0], routes[0], numerators[0])
    chips = members // 2
    pieces = {(0, 0): packed}
    for z in range(clusters - 1, 0, -1):
        pieces[0, z] = trade(packed, (z, 0), (z, 0))
    for x in range(1, chips):
        pieces[x, 0] = trade(packed, (0, 2 * x), (0, 2 * x))
    rest = jnp.concatenate([pieces[0, z] for z in range(1, clusters)])
    for x in range(1, chips):
        received = trade(rest, (0, 2 * x), (0, 2 * x))
        for z in range(1, clusters):
            pieces[x, z] = received[(z - 1) * count : z * count]

    for bit in across:
        for x in range(chips):
            if not x & bit:
                for z in range(clusters):
                    flag = (me // (2 * bit)) % 2 == 1
                    pieces[x, z], pieces[x | bit, z] = ordered(flag, pieces[x, z], pieces[x | bit, z])
    places = [(0, 0)]
    for mask in shared:
        places += [(x, z | mask) for x, z in places]
    for zbit, xbit in zip(paired, across):
        places += [(x | xbit, z) for x, z in places]
        places += [(x, z | zbit) for x, z in places]
    held = by_rows(jnp.concatenate([pieces[place] for place in places]))
    held = by_rows(jnp.concatenate(ordered(core == 1, held, trade(held, (0, 1), (0, 1)))))

    codes = jnp.dot(held[:, :width], delta_in[0], preferred_element_type=jnp.float32).astype(jnp.bfloat16)
    projected = gate_up_product(held, base_in[0])

    side = by_rows(held[:, width:])
    all_routes = side[:, :top].astype(jnp.int32)
    numerator = side[:, top : 2 * top].astype(jnp.float32)
    position = lookup(place, all_routes)
    weight = (2.5 * numerator / jnp.sum(numerator, axis=-1, keepdims=True)).astype(jnp.bfloat16)
    target = cluster * members + jnp.arange(members, dtype=jnp.int32)
    scale = jnp.sum(
        jnp.where(position[None] == target[:, None, None], weight[None].astype(jnp.float32), 0.0), axis=-1
    )

    codes = jnp.stack([codes if m == 0 else trade(codes, (0, m), (0, m)) for m in range(members)])
    by_slot = jnp.stack([lax.dynamic_index_in_dim(codes, s ^ me, 0, keepdims=False) for s in range(members)])

    lifted = jnp.einsum("srk,skgf->srgf", by_slot, delta_mid[0], preferred_element_type=jnp.float32)
    total = held.shape[0]
    hidden = jax.nn.silu(projected[None, :total] + lifted[:, :, 0]) * (projected[None, total:] + lifted[:, :, 1])
    hidden_sum = jnp.sum(scale[:, :, None] * hidden, axis=0).astype(jnp.bfloat16)
    partial_codes = jnp.einsum(
        "srf,sfk->srk", hidden.astype(jnp.bfloat16), delta_down[0], preferred_element_type=jnp.float32
    ).astype(jnp.bfloat16)
    lowrank = lax.dynamic_index_in_dim(partial_codes, me, 0, keepdims=False).astype(jnp.float32)
    for m in range(1, members):
        sent = lax.dynamic_index_in_dim(partial_codes, me ^ m, 0, keepdims=False)
        lowrank = lowrank + trade(sent, (0, m), (0, m)).astype(jnp.float32)
    own_scale = lax.dynamic_index_in_dim(scale, me, 0, keepdims=False)
    scaled = (own_scale[:, None] * lowrank).astype(jnp.bfloat16)

    term = jnp.dot(hidden_sum, base_down[0], preferred_element_type=jnp.float32)
    term = (term + jnp.dot(scaled, delta_back[0], preferred_element_type=jnp.float32)).astype(jnp.bfloat16)

    def add(kept, received):
        return (kept.astype(jnp.float32) + received.astype(jnp.float32)).astype(jnp.bfloat16)

    half = term.shape[0] // 2
    kept, sent = ordered(core == 1, term[:half], term[half:])
    outputs = []
    for total in jnp.split(add(kept, trade(sent, (0, 1), (0, 1))), CHUNKS, axis=1):
        for z, x in reversed(list(zip(paired, across))):
            flag = (me // (2 * x)) % 2 == 1
            size = total.shape[0] // 4
            blocks = [total[i * size : (i + 1) * size] for i in range(4)]
            inner = ordered(core == 1, blocks[1], blocks[2])
            kept, sent = ordered(
                (core == 1) & flag,
                jnp.concatenate([blocks[0], inner[0]]),
                jnp.concatenate([inner[1], blocks[3]]),
            )
            total = add(kept, trade(sent, (z, 0), (0, 2 * x)))
            kept, sent = ordered((core == 0) & flag, total[:size], total[size:])
            total = add(kept, trade(sent, (0, 2 * x), (z, 0)))
        for mask in reversed(shared):
            size = total.shape[0] // 2
            total = add(total[:size], trade(total[size:], (mask, 0), (mask, 0)))
        outputs.append(total)
    return jnp.concatenate(outputs, axis=1)[None]


def solution(mesh):
    placed = (
        P(None, ("parts", "expert", "tensor"), None),
        P(None, ("parts", "expert", "tensor"), None),
        P(None, ("parts", "expert", "tensor"), None),
        P("parts"),
        P("expert", None, None, "tensor"),
        P("expert", "tensor", None),
        P(("expert", "tensor"), None, None),
        P("expert", None, None, None, "tensor"),
        P("expert", None, "tensor", None),
        P(("expert", "tensor"), None, None),
    )
    return jax.shard_map(
        local,
        mesh=mesh,
        in_specs=placed,
        out_specs=P(None, ("parts", "expert", "tensor"), None),
        check_vma=False,
    )
```

```python
import functools

import jax
import jax.numpy as jnp
from jax import lax
from jax.experimental import pallas as pl
from jax.experimental.pallas import tpu as pltpu
from jax.experimental.layout import Layout, with_layout_constraint
from jax.sharding import PartitionSpec as P

CHUNKS = 2
VMEM = pl.BlockSpec(memory_space=pltpu.VMEM)
HBM = pl.BlockSpec(memory_space=pltpu.HBM)


def in_hbm(value):
    return pltpu.with_memory_space_constraint(value, pltpu.HBM)


def by_rows(value):
    return with_layout_constraint(value, Layout((0, 1)))


def lookup(table, index):
    keys = jnp.arange(table.shape[0], dtype=jnp.int32)
    return jnp.sum(jnp.where(index[..., None] == keys, table, 0), axis=-1)


def trade(value, even, odd):
    members = lax.axis_size("tensor")
    pairs = []
    for e in range(lax.axis_size("expert")):
        for t in range(members):
            along, across = odd if t % 2 else even
            pairs.append((e * members + t, (e ^ along) * members + (t ^ across)))
    return lax.ppermute(value, ("expert", "tensor"), pairs)


def halves(size):
    masks = []
    while size > 1:
        size //= 2
        masks.append(size)
    return masks


def ordered(flip, first, second):
    return jnp.where(flip, second, first), jnp.where(flip, first, second)


def pack_kernel(tokens, routes, numerators, packed, routes_in, numerators_in, sems):
    width, top = tokens.shape[1], routes.shape[1]
    copies = [
        pltpu.make_async_copy(tokens, packed.at[:, pl.ds(0, width)], sems.at[0]),
        pltpu.make_async_copy(routes, routes_in, sems.at[1]),
        pltpu.make_async_copy(numerators, numerators_in, sems.at[2]),
    ]
    for copy in copies:
        copy.start()
    packed[:, width:] = jnp.zeros((packed.shape[0], packed.shape[1] - width), packed.dtype)
    for copy in copies[1:]:
        copy.wait()
    packed[:, width : width + top] = routes_in[...].astype(jnp.float32).astype(packed.dtype)
    packed[:, width + top : width + 2 * top] = numerators_in[...].astype(jnp.float32).astype(packed.dtype)
    copies[0].wait()


def pack(tokens, routes, numerators):
    count, width = tokens.shape
    return pl.pallas_call(
        pack_kernel,
        out_shape=jax.ShapeDtypeStruct((count, width + 128), tokens.dtype),
        in_specs=[HBM] * 3,
        out_specs=VMEM,
        scratch_shapes=[
            pltpu.VMEM(routes.shape, routes.dtype),
            pltpu.VMEM(numerators.shape, numerators.dtype),
            pltpu.SemaphoreType.DMA((3,)),
        ],
        compiler_params=pltpu.CompilerParams(vmem_limit_bytes=4 << 20),
        cost_estimate=pl.CostEstimate(flops=20 * 10**9, bytes_accessed=4 * tokens.size, transcendentals=0),
    )(in_hbm(tokens), in_hbm(routes), in_hbm(numerators))


def gate_up_kernel(x, base, out):
    depth, _, columns = base.shape
    step = 512
    row = lax.broadcasted_iota(jnp.int32, (128, 256), 0)
    column = lax.broadcasted_iota(jnp.int32, (128, 256), 1)
    spread = jnp.where(column // 2 == row, 1.0, 0.0).astype(jnp.bfloat16)
    is_odd = (lax.broadcasted_iota(jnp.int32, (1, 2 * step), 1) % 2).astype(jnp.float32)
    odd_mask, even_mask = is_odd.astype(jnp.bfloat16), (1.0 - is_odd).astype(jnp.bfloat16)
    count = x.shape[0]
    flat = base.reshape(2 * depth, columns)
    total = jnp.zeros(out.shape, jnp.float32)
    for k in range(0, depth, step):
        stacked = jnp.concatenate([x[:, i : i + 128] for i in range(k, k + step, 128)])
        wide = jnp.dot(stacked, spread, preferred_element_type=jnp.float32).astype(jnp.bfloat16)
        wide = jnp.concatenate([wide[i : i + count] for i in range(0, stacked.shape[0], count)], axis=1)
        total += jnp.dot(
            jnp.concatenate([wide * even_mask, wide * odd_mask]),
            flat[2 * k : 2 * (k + step), :],
            preferred_element_type=jnp.float32,
        )
    out[...] = total


def gate_up_product(x, base):
    depth, _, columns = base.shape
    return pl.pallas_call(
        gate_up_kernel,
        out_shape=jax.ShapeDtypeStruct((2 * x.shape[0], columns), jnp.float32),
        in_specs=[VMEM, VMEM],
        out_specs=VMEM,
        compiler_params=pltpu.CompilerParams(vmem_limit_bytes=16 << 20),
        cost_estimate=pl.CostEstimate(
            flops=4 * x.shape[0] * depth * columns, bytes_accessed=2 * base.size, transcendentals=0
        ),
    )(x, base)


def join_kernel(own, received, joined):
    half = own.shape[0]
    core = lax.axis_index("tensor") % 2
    joined[pl.ds(pl.multiple_of(core * half, half), half), :] = own[...]
    joined[pl.ds(pl.multiple_of((1 - core) * half, half), half), :] = received[...]


def join(own, received):
    rows, width = own.shape
    return pl.pallas_call(
        join_kernel,
        out_shape=jax.ShapeDtypeStruct((2 * rows, width), own.dtype),
        in_specs=[VMEM, VMEM],
        out_specs=VMEM,
        compiler_params=pltpu.CompilerParams(vmem_limit_bytes=16 << 20),
        cost_estimate=pl.CostEstimate(flops=0, bytes_accessed=6 * own.size, transcendentals=0),
    )(own, received)


def part_kernel(bit, term, received, *refs):
    *outs, total = refs
    half, width = total.shape
    size, step = half // 4, width // (len(outs) // 2)
    me = lax.axis_index("tensor")
    core, flag = me % 2, (me // (2 * bit)) % 2
    total[...] = term[pl.ds(pl.multiple_of(core * half, half), half), :].astype(jnp.float32) + received[
        ...
    ].astype(jnp.float32)
    sent = (2 - core * (1 + flag), 3 - core * flag)
    kept = (core * flag, 1 + core * (1 + flag))
    for i, out in enumerate(outs):
        columns = pl.ds((i // 2) * step, step)
        rows = [
            total[pl.ds(pl.multiple_of(block * size, size), size), columns] for block in (sent, kept)[i % 2]
        ]
        out[...] = jnp.concatenate(rows).astype(out.dtype)


def add_and_part(term, received, bit):
    half, width = received.shape
    outs = pl.pallas_call(
        functools.partial(part_kernel, bit),
        out_shape=[jax.ShapeDtypeStruct((half // 2, width // CHUNKS), term.dtype)] * (2 * CHUNKS),
        in_specs=[VMEM, VMEM],
        out_specs=[VMEM] * (2 * CHUNKS),
        scratch_shapes=[pltpu.VMEM((half, width), jnp.float32)],
        compiler_params=pltpu.CompilerParams(vmem_limit_bytes=16 << 20),
        cost_estimate=pl.CostEstimate(flops=0, bytes_accessed=6 * received.size, transcendentals=0),
    )(term, received)
    return list(zip(outs[::2], outs[1::2]))


def local(
    tokens,
    routes,
    numerators,
    place,
    base_in,
    base_down,
    delta_in,
    delta_mid,
    delta_down,
    delta_back,
):
    clusters = lax.axis_size("expert")
    members = lax.axis_size("tensor")
    me = lax.axis_index("tensor")
    cluster = lax.axis_index("expert")
    core = me % 2
    count, width = tokens.shape[1:]
    top = routes.shape[2]

    along, across = halves(clusters), halves(members // 2)
    shared, paired = along[: len(along) - len(across)], along[len(along) - len(across) :]

    packed = pack(tokens[0], routes[0], numerators[0])
    chips = members // 2
    pieces = {(0, 0): packed}
    for z in range(clusters - 1, 0, -1):
        pieces[0, z] = trade(packed, (z, 0), (z, 0))
    for x in range(1, chips):
        pieces[x, 0] = trade(packed, (0, 2 * x), (0, 2 * x))
    rest = jnp.concatenate([pieces[0, z] for z in range(1, clusters)])
    for x in range(1, chips):
        received = trade(rest, (0, 2 * x), (0, 2 * x))
        for z in range(1, clusters):
            pieces[x, z] = received[(z - 1) * count : z * count]

    for bit in across:
        for x in range(chips):
            if not x & bit:
                for z in range(clusters):
                    flag = (me // (2 * bit)) % 2 == 1
                    pieces[x, z], pieces[x | bit, z] = ordered(flag, pieces[x, z], pieces[x | bit, z])
    places = [(0, 0)]
    for mask in shared:
        places += [(x, z | mask) for x, z in places]
    for zbit, xbit in zip(paired, across):
        places += [(x | xbit, z) for x, z in places]
        places += [(x, z | zbit) for x, z in places]
    held = by_rows(jnp.concatenate([pieces[place] for place in places]))
    held = join(held, trade(held, (0, 1), (0, 1)))

    codes = jnp.dot(held[:, :width], delta_in[0], preferred_element_type=jnp.float32).astype(jnp.bfloat16)
    projected = gate_up_product(held, base_in[0])

    side = by_rows(held[:, width:])
    all_routes = side[:, :top].astype(jnp.int32)
    numerator = side[:, top : 2 * top].astype(jnp.float32)
    position = lookup(place, all_routes)
    weight = (2.5 * numerator / jnp.sum(numerator, axis=-1, keepdims=True)).astype(jnp.bfloat16)
    target = cluster * members + jnp.arange(members, dtype=jnp.int32)
    scale = jnp.sum(
        jnp.where(position[None] == target[:, None, None], weight[None].astype(jnp.float32), 0.0), axis=-1
    )

    codes = jnp.stack([codes if m == 0 else trade(codes, (0, m), (0, m)) for m in range(members)])
    by_slot = jnp.stack([lax.dynamic_index_in_dim(codes, s ^ me, 0, keepdims=False) for s in range(members)])

    lifted = jnp.einsum("srk,skgf->srgf", by_slot, delta_mid[0], preferred_element_type=jnp.float32)
    total = held.shape[0]
    hidden = jax.nn.silu(projected[None, :total] + lifted[:, :, 0]) * (projected[None, total:] + lifted[:, :, 1])
    hidden_sum = jnp.sum(scale[:, :, None] * hidden, axis=0).astype(jnp.bfloat16)
    partial_codes = jnp.einsum(
        "srf,sfk->srk", hidden.astype(jnp.bfloat16), delta_down[0], preferred_element_type=jnp.float32
    ).astype(jnp.bfloat16)
    lowrank = lax.dynamic_index_in_dim(partial_codes, me, 0, keepdims=False).astype(jnp.float32)
    for m in range(1, members):
        sent = lax.dynamic_index_in_dim(partial_codes, me ^ m, 0, keepdims=False)
        lowrank = lowrank + trade(sent, (0, m), (0, m)).astype(jnp.float32)
    own_scale = lax.dynamic_index_in_dim(scale, me, 0, keepdims=False)
    scaled = (own_scale[:, None] * lowrank).astype(jnp.bfloat16)

    term = jnp.dot(hidden_sum, base_down[0], preferred_element_type=jnp.float32)
    term = (term + jnp.dot(scaled, delta_back[0], preferred_element_type=jnp.float32)).astype(jnp.bfloat16)

    def add(kept, received):
        return (kept.astype(jnp.float32) + received.astype(jnp.float32)).astype(jnp.bfloat16)

    half = term.shape[0] // 2
    sent = ordered(core == 1, term[half:], term[:half])[0]
    outputs = []
    for sent, kept in add_and_part(term, trade(sent, (0, 1), (0, 1)), across[-1]):
        for i, (z, x) in enumerate(reversed(list(zip(paired, across)))):
            flag = (me // (2 * x)) % 2 == 1
            if i:
                size = total.shape[0] // 4
                blocks = [total[j * size : (j + 1) * size] for j in range(4)]
                inner = ordered(core == 1, blocks[1], blocks[2])
                kept, sent = ordered(
                    (core == 1) & flag,
                    jnp.concatenate([blocks[0], inner[0]]),
                    jnp.concatenate([inner[1], blocks[3]]),
                )
            total = add(kept, trade(sent, (z, 0), (0, 2 * x)))
            size = total.shape[0] // 2
            kept, sent = ordered((core == 0) & flag, total[:size], total[size:])
            total = add(kept, trade(sent, (0, 2 * x), (z, 0)))
        for mask in reversed(shared):
            size = total.shape[0] // 2
            total = add(total[:size], trade(total[size:], (mask, 0), (mask, 0)))
        outputs.append(total)
    return jnp.concatenate(outputs, axis=1)[None]


def solution(mesh):
    placed = (
        P(None, ("parts", "expert", "tensor"), None),
        P(None, ("parts", "expert", "tensor"), None),
        P(None, ("parts", "expert", "tensor"), None),
        P("parts"),
        P("expert", None, None, "tensor"),
        P("expert", "tensor", None),
        P(("expert", "tensor"), None, None),
        P("expert", None, None, None, "tensor"),
        P("expert", None, "tensor", None),
        P(("expert", "tensor"), None, None),
    )
    return jax.shard_map(
        local,
        mesh=mesh,
        in_specs=placed,
        out_specs=P(None, ("parts", "expert", "tensor"), None),
        check_vma=False,
    )
```

```python
import functools

import jax
import jax.numpy as jnp
from jax import lax
from jax.experimental import pallas as pl
from jax.experimental.pallas import tpu as pltpu
from jax.experimental.layout import Layout, with_layout_constraint
from jax.sharding import PartitionSpec as P

CHUNKS = 2
VMEM = pl.BlockSpec(memory_space=pltpu.VMEM)
HBM = pl.BlockSpec(memory_space=pltpu.HBM)


def in_hbm(value):
    return pltpu.with_memory_space_constraint(value, pltpu.HBM)


def by_rows(value):
    return with_layout_constraint(value, Layout((0, 1)))


def lookup(table, index):
    keys = jnp.arange(table.shape[0], dtype=jnp.int32)
    return jnp.sum(jnp.where(index[..., None] == keys, table, 0), axis=-1)


def trade(value, even, odd):
    members = lax.axis_size("tensor")
    pairs = []
    for e in range(lax.axis_size("expert")):
        for t in range(members):
            along, across = odd if t % 2 else even
            pairs.append((e * members + t, (e ^ along) * members + (t ^ across)))
    return lax.ppermute(value, ("expert", "tensor"), pairs)


def halves(size):
    masks = []
    while size > 1:
        size //= 2
        masks.append(size)
    return masks


def ordered(flip, first, second):
    return jnp.where(flip, second, first), jnp.where(flip, first, second)


def pack_kernel(tokens, routes, numerators, packed, routes_in, numerators_in, sems):
    width, top = tokens.shape[1], routes.shape[1]
    copies = [
        pltpu.make_async_copy(tokens, packed.at[:, pl.ds(0, width)], sems.at[0]),
        pltpu.make_async_copy(routes, routes_in, sems.at[1]),
        pltpu.make_async_copy(numerators, numerators_in, sems.at[2]),
    ]
    for copy in copies:
        copy.start()
    packed[:, width:] = jnp.zeros((packed.shape[0], packed.shape[1] - width), packed.dtype)
    for copy in copies[1:]:
        copy.wait()
    packed[:, width : width + top] = routes_in[...].astype(jnp.float32).astype(packed.dtype)
    packed[:, width + top : width + 2 * top] = numerators_in[...].astype(jnp.float32).astype(packed.dtype)
    copies[0].wait()


def pack(tokens, routes, numerators):
    count, width = tokens.shape
    return pl.pallas_call(
        pack_kernel,
        out_shape=jax.ShapeDtypeStruct((count, width + 128), tokens.dtype),
        in_specs=[HBM] * 3,
        out_specs=VMEM,
        scratch_shapes=[
            pltpu.VMEM(routes.shape, routes.dtype),
            pltpu.VMEM(numerators.shape, numerators.dtype),
            pltpu.SemaphoreType.DMA((3,)),
        ],
        compiler_params=pltpu.CompilerParams(vmem_limit_bytes=4 << 20),
        cost_estimate=pl.CostEstimate(flops=20 * 10**9, bytes_accessed=4 * tokens.size, transcendentals=0),
    )(in_hbm(tokens), in_hbm(routes), in_hbm(numerators))


def gate_up_kernel(x, base, out):
    depth, _, columns = base.shape
    step = 512
    row = lax.broadcasted_iota(jnp.int32, (128, 256), 0)
    column = lax.broadcasted_iota(jnp.int32, (128, 256), 1)
    spread = jnp.where(column // 2 == row, 1.0, 0.0).astype(jnp.bfloat16)
    is_odd = (lax.broadcasted_iota(jnp.int32, (1, 2 * step), 1) % 2).astype(jnp.float32)
    odd_mask, even_mask = is_odd.astype(jnp.bfloat16), (1.0 - is_odd).astype(jnp.bfloat16)
    count = x.shape[0]
    flat = base.reshape(2 * depth, columns)
    total = jnp.zeros(out.shape, jnp.float32)
    for k in range(0, depth, step):
        stacked = jnp.concatenate([x[:, i : i + 128] for i in range(k, k + step, 128)])
        wide = jnp.dot(stacked, spread, preferred_element_type=jnp.float32).astype(jnp.bfloat16)
        wide = jnp.concatenate([wide[i : i + count] for i in range(0, stacked.shape[0], count)], axis=1)
        total += jnp.dot(
            jnp.concatenate([wide * even_mask, wide * odd_mask]),
            flat[2 * k : 2 * (k + step), :],
            preferred_element_type=jnp.float32,
        )
    out[...] = total


def gate_up_product(x, base):
    depth, _, columns = base.shape
    return pl.pallas_call(
        gate_up_kernel,
        out_shape=jax.ShapeDtypeStruct((2 * x.shape[0], columns), jnp.float32),
        in_specs=[VMEM, VMEM],
        out_specs=VMEM,
        compiler_params=pltpu.CompilerParams(vmem_limit_bytes=16 << 20),
        cost_estimate=pl.CostEstimate(
            flops=4 * x.shape[0] * depth * columns, bytes_accessed=2 * base.size, transcendentals=0
        ),
    )(x, base)


def part_kernel(bit, term, received, *refs):
    *outs, total = refs
    half, width = total.shape
    size, step = half // 4, width // (len(outs) // 2)
    me = lax.axis_index("tensor")
    core, flag = me % 2, (me // (2 * bit)) % 2
    total[...] = term[pl.ds(pl.multiple_of(core * half, half), half), :].astype(jnp.float32) + received[
        ...
    ].astype(jnp.float32)
    sent = (2 - core * (1 + flag), 3 - core * flag)
    kept = (core * flag, 1 + core * (1 + flag))
    for i, out in enumerate(outs):
        columns = pl.ds((i // 2) * step, step)
        rows = [
            total[pl.ds(pl.multiple_of(block * size, size), size), columns] for block in (sent, kept)[i % 2]
        ]
        out[...] = jnp.concatenate(rows).astype(out.dtype)


def add_and_part(term, received, bit):
    half, width = received.shape
    outs = pl.pallas_call(
        functools.partial(part_kernel, bit),
        out_shape=[jax.ShapeDtypeStruct((half // 2, width // CHUNKS), term.dtype)] * (2 * CHUNKS),
        in_specs=[VMEM, VMEM],
        out_specs=[VMEM] * (2 * CHUNKS),
        scratch_shapes=[pltpu.VMEM((half, width), jnp.float32)],
        compiler_params=pltpu.CompilerParams(vmem_limit_bytes=16 << 20),
        cost_estimate=pl.CostEstimate(flops=0, bytes_accessed=6 * received.size, transcendentals=0),
    )(term, received)
    return list(zip(outs[::2], outs[1::2]))


def local(
    tokens,
    routes,
    numerators,
    place,
    base_in,
    base_down,
    delta_in,
    delta_mid,
    delta_down,
    delta_back,
):
    clusters = lax.axis_size("expert")
    members = lax.axis_size("tensor")
    me = lax.axis_index("tensor")
    cluster = lax.axis_index("expert")
    core = me % 2
    count, width = tokens.shape[1:]
    top = routes.shape[2]

    along, across = halves(clusters), halves(members // 2)
    shared, paired = along[: len(along) - len(across)], along[len(along) - len(across) :]

    packed = pack(tokens[0], routes[0], numerators[0])
    chips = members // 2
    pieces = {(0, 0): packed}
    for z in range(clusters - 1, 0, -1):
        pieces[0, z] = trade(packed, (z, 0), (z, 0))
    for x in range(1, chips):
        pieces[x, 0] = trade(packed, (0, 2 * x), (0, 2 * x))
    rest = jnp.concatenate([pieces[0, z] for z in range(1, clusters)])
    for x in range(1, chips):
        received = trade(rest, (0, 2 * x), (0, 2 * x))
        for z in range(1, clusters):
            pieces[x, z] = received[(z - 1) * count : z * count]

    for bit in across:
        for x in range(chips):
            if not x & bit:
                for z in range(clusters):
                    flag = (me // (2 * bit)) % 2 == 1
                    pieces[x, z], pieces[x | bit, z] = ordered(flag, pieces[x, z], pieces[x | bit, z])
    places = [(0, 0)]
    for mask in shared:
        places += [(x, z | mask) for x, z in places]
    for zbit, xbit in zip(paired, across):
        places += [(x | xbit, z) for x, z in places]
        places += [(x, z | zbit) for x, z in places]
    held = by_rows(jnp.concatenate([pieces[place] for place in places]))
    held = by_rows(jnp.concatenate(ordered(core == 1, held, trade(held, (0, 1), (0, 1)))))
    rows, code_table = lax.optimization_barrier((held, delta_in[0]))

    codes = jnp.dot(rows[:, :width], code_table, preferred_element_type=jnp.float32).astype(jnp.bfloat16)
    projected = gate_up_product(held, base_in[0])

    side = by_rows(rows[:, width:])
    all_routes = side[:, :top].astype(jnp.int32)
    numerator = side[:, top : 2 * top].astype(jnp.float32)
    position = lookup(place, all_routes)
    weight = (2.5 * numerator / jnp.sum(numerator, axis=-1, keepdims=True)).astype(jnp.bfloat16)
    target = cluster * members + jnp.arange(members, dtype=jnp.int32)
    scale = jnp.sum(
        jnp.where(position[None] == target[:, None, None], weight[None].astype(jnp.float32), 0.0), axis=-1
    )

    codes = jnp.stack([codes if m == 0 else trade(codes, (0, m), (0, m)) for m in range(members)])
    by_slot = jnp.stack([lax.dynamic_index_in_dim(codes, s ^ me, 0, keepdims=False) for s in range(members)])

    lifted = jnp.einsum("srk,skgf->srgf", by_slot, delta_mid[0], preferred_element_type=jnp.float32)
    total = held.shape[0]
    hidden = jax.nn.silu(projected[None, :total] + lifted[:, :, 0]) * (projected[None, total:] + lifted[:, :, 1])
    hidden_sum = jnp.sum(scale[:, :, None] * hidden, axis=0).astype(jnp.bfloat16)
    partial_codes = jnp.einsum(
        "srf,sfk->srk", hidden.astype(jnp.bfloat16), delta_down[0], preferred_element_type=jnp.float32
    ).astype(jnp.bfloat16)
    lowrank = lax.dynamic_index_in_dim(partial_codes, me, 0, keepdims=False).astype(jnp.float32)
    for m in range(1, members):
        sent = lax.dynamic_index_in_dim(partial_codes, me ^ m, 0, keepdims=False)
        lowrank = lowrank + trade(sent, (0, m), (0, m)).astype(jnp.float32)
    own_scale = lax.dynamic_index_in_dim(scale, me, 0, keepdims=False)
    scaled = (own_scale[:, None] * lowrank).astype(jnp.bfloat16)

    term = jnp.dot(hidden_sum, base_down[0], preferred_element_type=jnp.float32)
    term = (term + jnp.dot(scaled, delta_back[0], preferred_element_type=jnp.float32)).astype(jnp.bfloat16)

    def add(kept, received):
        return (kept.astype(jnp.float32) + received.astype(jnp.float32)).astype(jnp.bfloat16)

    half = term.shape[0] // 2
    sent = ordered(core == 1, term[half:], term[:half])[0]
    outputs = []
    for sent, kept in add_and_part(term, trade(sent, (0, 1), (0, 1)), across[-1]):
        for i, (z, x) in enumerate(reversed(list(zip(paired, across)))):
            flag = (me // (2 * x)) % 2 == 1
            if i:
                size = total.shape[0] // 4
                blocks = [total[j * size : (j + 1) * size] for j in range(4)]
                inner = ordered(core == 1, blocks[1], blocks[2])
                kept, sent = ordered(
                    (core == 1) & flag,
                    jnp.concatenate([blocks[0], inner[0]]),
                    jnp.concatenate([inner[1], blocks[3]]),
                )
            total = add(kept, trade(sent, (z, 0), (0, 2 * x)))
            size = total.shape[0] // 2
            kept, sent = ordered((core == 0) & flag, total[:size], total[size:])
            total = add(kept, trade(sent, (0, 2 * x), (z, 0)))
        for mask in reversed(shared):
            size = total.shape[0] // 2
            total = add(total[:size], trade(total[size:], (mask, 0), (mask, 0)))
        outputs.append(total)
    return jnp.concatenate(outputs, axis=1)[None]


def solution(mesh):
    placed = (
        P(None, ("parts", "expert", "tensor"), None),
        P(None, ("parts", "expert", "tensor"), None),
        P(None, ("parts", "expert", "tensor"), None),
        P("parts"),
        P("expert", None, None, "tensor"),
        P("expert", "tensor", None),
        P(("expert", "tensor"), None, None),
        P("expert", None, None, None, "tensor"),
        P("expert", None, "tensor", None),
        P(("expert", "tensor"), None, None),
    )
    return jax.shard_map(
        local,
        mesh=mesh,
        in_specs=placed,
        out_specs=P(None, ("parts", "expert", "tensor"), None),
        check_vma=False,
    )
```

```python
import functools

import jax
import jax.numpy as jnp
from jax import lax
from jax.experimental import pallas as pl
from jax.experimental.pallas import tpu as pltpu
from jax.experimental.layout import Layout, with_layout_constraint
from jax.sharding import PartitionSpec as P

CHUNKS = 2
VMEM = pl.BlockSpec(memory_space=pltpu.VMEM)
HBM = pl.BlockSpec(memory_space=pltpu.HBM)


def in_hbm(value):
    return pltpu.with_memory_space_constraint(value, pltpu.HBM)


def by_rows(value):
    return with_layout_constraint(value, Layout((0, 1)))


def lookup(table, index):
    keys = jnp.arange(table.shape[0], dtype=jnp.int32)
    return jnp.sum(jnp.where(index[..., None] == keys, table, 0), axis=-1)


def trade(value, even, odd):
    members = lax.axis_size("tensor")
    pairs = []
    for e in range(lax.axis_size("expert")):
        for t in range(members):
            along, across = odd if t % 2 else even
            pairs.append((e * members + t, (e ^ along) * members + (t ^ across)))
    return lax.ppermute(value, ("expert", "tensor"), pairs)


def halves(size):
    masks = []
    while size > 1:
        size //= 2
        masks.append(size)
    return masks


def ordered(flip, first, second):
    return jnp.where(flip, second, first), jnp.where(flip, first, second)


def pack_kernel(tokens, routes, numerators, packed, routes_in, numerators_in, sems):
    width, top = tokens.shape[1], routes.shape[1]
    copies = [
        pltpu.make_async_copy(tokens, packed.at[:, pl.ds(0, width)], sems.at[0]),
        pltpu.make_async_copy(routes, routes_in, sems.at[1]),
        pltpu.make_async_copy(numerators, numerators_in, sems.at[2]),
    ]
    for copy in copies:
        copy.start()
    packed[:, width:] = jnp.zeros((packed.shape[0], packed.shape[1] - width), packed.dtype)
    for copy in copies[1:]:
        copy.wait()
    packed[:, width : width + top] = routes_in[...].astype(jnp.float32).astype(packed.dtype)
    packed[:, width + top : width + 2 * top] = numerators_in[...].astype(jnp.float32).astype(packed.dtype)
    copies[0].wait()


def pack(tokens, routes, numerators):
    count, width = tokens.shape
    return pl.pallas_call(
        pack_kernel,
        out_shape=jax.ShapeDtypeStruct((count, width + 128), tokens.dtype),
        in_specs=[HBM] * 3,
        out_specs=VMEM,
        scratch_shapes=[
            pltpu.VMEM(routes.shape, routes.dtype),
            pltpu.VMEM(numerators.shape, numerators.dtype),
            pltpu.SemaphoreType.DMA((3,)),
        ],
        compiler_params=pltpu.CompilerParams(vmem_limit_bytes=4 << 20),
        cost_estimate=pl.CostEstimate(flops=20 * 10**9, bytes_accessed=4 * tokens.size, transcendentals=0),
    )(in_hbm(tokens), in_hbm(routes), in_hbm(numerators))


def gate_up_kernel(x, base, out):
    depth, _, columns = base.shape
    step = 512
    row = lax.broadcasted_iota(jnp.int32, (128, 256), 0)
    column = lax.broadcasted_iota(jnp.int32, (128, 256), 1)
    spread = jnp.where(column // 2 == row, 1.0, 0.0).astype(jnp.bfloat16)
    is_odd = (lax.broadcasted_iota(jnp.int32, (1, 2 * step), 1) % 2).astype(jnp.float32)
    odd_mask, even_mask = is_odd.astype(jnp.bfloat16), (1.0 - is_odd).astype(jnp.bfloat16)
    count = x.shape[0]
    flat = base.reshape(2 * depth, columns)
    total = jnp.zeros(out.shape, jnp.float32)
    for k in range(0, depth, step):
        stacked = jnp.concatenate([x[:, i : i + 128] for i in range(k, k + step, 128)])
        wide = jnp.dot(stacked, spread, preferred_element_type=jnp.float32).astype(jnp.bfloat16)
        wide = jnp.concatenate([wide[i : i + count] for i in range(0, stacked.shape[0], count)], axis=1)
        total += jnp.dot(
            jnp.concatenate([wide * even_mask, wide * odd_mask]),
            flat[2 * k : 2 * (k + step), :],
            preferred_element_type=jnp.float32,
        )
    out[...] = total


def gate_up_product(x, base):
    depth, _, columns = base.shape
    return pl.pallas_call(
        gate_up_kernel,
        out_shape=jax.ShapeDtypeStruct((2 * x.shape[0], columns), jnp.float32),
        in_specs=[VMEM, VMEM],
        out_specs=VMEM,
        compiler_params=pltpu.CompilerParams(vmem_limit_bytes=16 << 20),
        cost_estimate=pl.CostEstimate(
            flops=4 * x.shape[0] * depth * columns, bytes_accessed=2 * base.size, transcendentals=0
        ),
    )(x, base)


def down_kernel(hidden, base, out, weights, sems):
    step = base.shape[1] // sems.shape[0]
    parts = [pl.ds(k * step, step) for k in range(sems.shape[0])]
    copies = [pltpu.make_async_copy(base.at[:, part], weights.at[:, part], sems.at[k]) for k, part in enumerate(parts)]
    for copy in copies:
        copy.start()
    for copy, part in zip(copies, parts):
        copy.wait()
        out[:, part] = jnp.dot(hidden[...], weights[:, part], preferred_element_type=jnp.float32)


def down_product(hidden, base):
    rows, width = hidden.shape[0], base.shape[1]
    return pl.pallas_call(
        down_kernel,
        out_shape=jax.ShapeDtypeStruct((rows, width), jnp.float32),
        in_specs=[VMEM, HBM],
        out_specs=VMEM,
        scratch_shapes=[pltpu.VMEM(base.shape, base.dtype), pltpu.SemaphoreType.DMA((width // 1024,))],
        compiler_params=pltpu.CompilerParams(vmem_limit_bytes=16 << 20),
        cost_estimate=pl.CostEstimate(flops=2 * rows * base.size, bytes_accessed=2 * base.size, transcendentals=0),
    )(hidden, in_hbm(base))


def part_kernel(bit, term, received, *refs):
    *outs, total = refs
    half, width = total.shape
    size, step = half // 4, width // (len(outs) // 2)
    me = lax.axis_index("tensor")
    core, flag = me % 2, (me // (2 * bit)) % 2
    total[...] = term[pl.ds(pl.multiple_of(core * half, half), half), :].astype(jnp.float32) + received[
        ...
    ].astype(jnp.float32)
    sent = (2 - core * (1 + flag), 3 - core * flag)
    kept = (core * flag, 1 + core * (1 + flag))
    for i, out in enumerate(outs):
        columns = pl.ds((i // 2) * step, step)
        rows = [
            total[pl.ds(pl.multiple_of(block * size, size), size), columns] for block in (sent, kept)[i % 2]
        ]
        out[...] = jnp.concatenate(rows).astype(out.dtype)


def add_and_part(term, received, bit):
    half, width = received.shape
    outs = pl.pallas_call(
        functools.partial(part_kernel, bit),
        out_shape=[jax.ShapeDtypeStruct((half // 2, width // CHUNKS), term.dtype)] * (2 * CHUNKS),
        in_specs=[VMEM, VMEM],
        out_specs=[VMEM] * (2 * CHUNKS),
        scratch_shapes=[pltpu.VMEM((half, width), jnp.float32)],
        compiler_params=pltpu.CompilerParams(vmem_limit_bytes=16 << 20),
        cost_estimate=pl.CostEstimate(flops=0, bytes_accessed=6 * received.size, transcendentals=0),
    )(term, received)
    return list(zip(outs[::2], outs[1::2]))


def local(
    tokens,
    routes,
    numerators,
    place,
    base_in,
    base_down,
    delta_in,
    delta_mid,
    delta_down,
    delta_back,
):
    clusters = lax.axis_size("expert")
    members = lax.axis_size("tensor")
    me = lax.axis_index("tensor")
    cluster = lax.axis_index("expert")
    core = me % 2
    count, width = tokens.shape[1:]
    top = routes.shape[2]

    along, across = halves(clusters), halves(members // 2)
    shared, paired = along[: len(along) - len(across)], along[len(along) - len(across) :]

    packed = pack(tokens[0], routes[0], numerators[0])
    chips = members // 2
    pieces = {(0, 0): packed}
    for z in range(clusters - 1, 0, -1):
        pieces[0, z] = trade(packed, (z, 0), (z, 0))
    for x in range(1, chips):
        pieces[x, 0] = trade(packed, (0, 2 * x), (0, 2 * x))
    rest = jnp.concatenate([pieces[0, z] for z in range(1, clusters)])
    for x in range(1, chips):
        received = trade(rest, (0, 2 * x), (0, 2 * x))
        for z in range(1, clusters):
            pieces[x, z] = received[(z - 1) * count : z * count]

    for bit in across:
        for x in range(chips):
            if not x & bit:
                for z in range(clusters):
                    flag = (me // (2 * bit)) % 2 == 1
                    pieces[x, z], pieces[x | bit, z] = ordered(flag, pieces[x, z], pieces[x | bit, z])
    places = [(0, 0)]
    for mask in shared:
        places += [(x, z | mask) for x, z in places]
    for zbit, xbit in zip(paired, across):
        places += [(x | xbit, z) for x, z in places]
        places += [(x, z | zbit) for x, z in places]
    held = by_rows(jnp.concatenate([pieces[place] for place in places]))
    held = by_rows(jnp.concatenate(ordered(core == 1, held, trade(held, (0, 1), (0, 1)))))
    rows, code_table = lax.optimization_barrier((held, delta_in[0]))

    codes = jnp.dot(rows[:, :width], code_table, preferred_element_type=jnp.float32).astype(jnp.bfloat16)
    projected = gate_up_product(held, base_in[0])

    side = by_rows(rows[:, width:])
    all_routes = side[:, :top].astype(jnp.int32)
    numerator = side[:, top : 2 * top].astype(jnp.float32)
    position = lookup(place, all_routes)
    weight = (2.5 * numerator / jnp.sum(numerator, axis=-1, keepdims=True)).astype(jnp.bfloat16)
    target = cluster * members + jnp.arange(members, dtype=jnp.int32)
    scale = jnp.sum(
        jnp.where(position[None] == target[:, None, None], weight[None].astype(jnp.float32), 0.0), axis=-1
    )

    codes = jnp.stack([codes if m == 0 else trade(codes, (0, m), (0, m)) for m in range(members)])
    by_slot = jnp.stack([lax.dynamic_index_in_dim(codes, s ^ me, 0, keepdims=False) for s in range(members)])

    lifted = jnp.einsum("srk,skgf->srgf", by_slot, delta_mid[0], preferred_element_type=jnp.float32)
    total = held.shape[0]
    hidden = jax.nn.silu(projected[None, :total] + lifted[:, :, 0]) * (projected[None, total:] + lifted[:, :, 1])
    hidden_sum = jnp.sum(scale[:, :, None] * hidden, axis=0).astype(jnp.bfloat16)
    partial_codes = jnp.einsum(
        "srf,sfk->srk", hidden.astype(jnp.bfloat16), delta_down[0], preferred_element_type=jnp.float32
    ).astype(jnp.bfloat16)
    lowrank = lax.dynamic_index_in_dim(partial_codes, me, 0, keepdims=False).astype(jnp.float32)
    for m in range(1, members):
        sent = lax.dynamic_index_in_dim(partial_codes, me ^ m, 0, keepdims=False)
        lowrank = lowrank + trade(sent, (0, m), (0, m)).astype(jnp.float32)
    own_scale = lax.dynamic_index_in_dim(scale, me, 0, keepdims=False)
    scaled = (own_scale[:, None] * lowrank).astype(jnp.bfloat16)

    term = down_product(hidden_sum, base_down[0])
    term = (term + jnp.dot(scaled, delta_back[0], preferred_element_type=jnp.float32)).astype(jnp.bfloat16)

    def add(kept, received):
        return (kept.astype(jnp.float32) + received.astype(jnp.float32)).astype(jnp.bfloat16)

    half = term.shape[0] // 2
    sent = ordered(core == 1, term[half:], term[:half])[0]
    outputs = []
    for sent, kept in add_and_part(term, trade(sent, (0, 1), (0, 1)), across[-1]):
        for i, (z, x) in enumerate(reversed(list(zip(paired, across)))):
            flag = (me // (2 * x)) % 2 == 1
            if i:
                size = total.shape[0] // 4
                blocks = [total[j * size : (j + 1) * size] for j in range(4)]
                inner = ordered(core == 1, blocks[1], blocks[2])
                kept, sent = ordered(
                    (core == 1) & flag,
                    jnp.concatenate([blocks[0], inner[0]]),
                    jnp.concatenate([inner[1], blocks[3]]),
                )
            total = add(kept, trade(sent, (z, 0), (0, 2 * x)))
            size = total.shape[0] // 2
            kept, sent = ordered((core == 0) & flag, total[:size], total[size:])
            total = add(kept, trade(sent, (0, 2 * x), (z, 0)))
        for mask in reversed(shared):
            size = total.shape[0] // 2
            total = add(total[:size], trade(total[size:], (mask, 0), (mask, 0)))
        outputs.append(total)
    return jnp.concatenate(outputs, axis=1)[None]


def solution(mesh):
    placed = (
        P(None, ("parts", "expert", "tensor"), None),
        P(None, ("parts", "expert", "tensor"), None),
        P(None, ("parts", "expert", "tensor"), None),
        P("parts"),
        P("expert", None, None, "tensor"),
        P("expert", "tensor", None),
        P(("expert", "tensor"), None, None),
        P("expert", None, None, None, "tensor"),
        P("expert", None, "tensor", None),
        P(("expert", "tensor"), None, None),
    )
    return jax.shard_map(
        local,
        mesh=mesh,
        in_specs=placed,
        out_specs=P(None, ("parts", "expert", "tensor"), None),
        check_vma=False,
    )
```

```python
import functools

import jax
import jax.numpy as jnp
from jax import lax
from jax.experimental import pallas as pl
from jax.experimental.pallas import tpu as pltpu
from jax.experimental.layout import Layout, with_layout_constraint
from jax.sharding import PartitionSpec as P

CHUNKS = 2
VMEM = pl.BlockSpec(memory_space=pltpu.VMEM)
HBM = pl.BlockSpec(memory_space=pltpu.HBM)


def in_hbm(value):
    return pltpu.with_memory_space_constraint(value, pltpu.HBM)


def by_rows(value):
    return with_layout_constraint(value, Layout((0, 1)))


def lookup(table, index):
    keys = jnp.arange(table.shape[0], dtype=jnp.int32)
    return jnp.sum(jnp.where(index[..., None] == keys, table, 0), axis=-1)


def trade(value, even, odd):
    members = lax.axis_size("tensor")
    pairs = []
    for e in range(lax.axis_size("expert")):
        for t in range(members):
            along, across = odd if t % 2 else even
            pairs.append((e * members + t, (e ^ along) * members + (t ^ across)))
    return lax.ppermute(value, ("expert", "tensor"), pairs)


def halves(size):
    masks = []
    while size > 1:
        size //= 2
        masks.append(size)
    return masks


def ordered(flip, first, second):
    return jnp.where(flip, second, first), jnp.where(flip, first, second)


def add(kept, received):
    return (kept.astype(jnp.float32) + received.astype(jnp.float32)).astype(jnp.bfloat16)


def pack_kernel(tokens, routes, numerators, packed, routes_in, numerators_in, sems):
    width, top = tokens.shape[1], routes.shape[1]
    copies = [
        pltpu.make_async_copy(tokens, packed.at[:, pl.ds(0, width)], sems.at[0]),
        pltpu.make_async_copy(routes, routes_in, sems.at[1]),
        pltpu.make_async_copy(numerators, numerators_in, sems.at[2]),
    ]
    for copy in copies:
        copy.start()
    packed[:, width:] = jnp.zeros((packed.shape[0], packed.shape[1] - width), packed.dtype)
    for copy in copies[1:]:
        copy.wait()
    packed[:, width : width + top] = routes_in[...].astype(jnp.float32).astype(packed.dtype)
    packed[:, width + top : width + 2 * top] = numerators_in[...].astype(jnp.float32).astype(packed.dtype)
    copies[0].wait()


def pack(tokens, routes, numerators):
    count, width = tokens.shape
    return pl.pallas_call(
        pack_kernel,
        out_shape=jax.ShapeDtypeStruct((count, width + 128), tokens.dtype),
        in_specs=[HBM] * 3,
        out_specs=VMEM,
        scratch_shapes=[
            pltpu.VMEM(routes.shape, routes.dtype),
            pltpu.VMEM(numerators.shape, numerators.dtype),
            pltpu.SemaphoreType.DMA((3,)),
        ],
        compiler_params=pltpu.CompilerParams(vmem_limit_bytes=4 << 20),
        cost_estimate=pl.CostEstimate(flops=20 * 10**9, bytes_accessed=4 * tokens.size, transcendentals=0),
    )(in_hbm(tokens), in_hbm(routes), in_hbm(numerators))


def gate_up_kernel(x, base, out, weights, sems):
    depth, _, columns = weights.shape
    step = depth // sems.shape[0]
    copies = [
        pltpu.make_async_copy(base.at[pl.ds(k, step)], weights.at[pl.ds(k, step)], sems.at[k // step])
        for k in range(0, depth, step)
    ]
    for copy in copies:
        copy.start()
    row = lax.broadcasted_iota(jnp.int32, (128, 256), 0)
    column = lax.broadcasted_iota(jnp.int32, (128, 256), 1)
    spread = jnp.where(column // 2 == row, 1.0, 0.0).astype(jnp.bfloat16)
    is_odd = (lax.broadcasted_iota(jnp.int32, (1, 2 * step), 1) % 2).astype(jnp.float32)
    odd_mask, even_mask = is_odd.astype(jnp.bfloat16), (1.0 - is_odd).astype(jnp.bfloat16)
    count = x.shape[0]
    flat = weights.reshape(2 * depth, columns)
    total = jnp.zeros(out.shape, jnp.float32)
    for k in range(0, depth, step):
        stacked = jnp.concatenate([x[:, i : i + 128] for i in range(k, k + step, 128)])
        wide = jnp.dot(stacked, spread, preferred_element_type=jnp.float32).astype(jnp.bfloat16)
        wide = jnp.concatenate([wide[i : i + count] for i in range(0, stacked.shape[0], count)], axis=1)
        copies[k // step].wait()
        total += jnp.dot(
            jnp.concatenate([wide * even_mask, wide * odd_mask]), flat[2 * k : 2 * (k + step), :], preferred_element_type=jnp.float32
        )
    out[...] = total


def gate_up_product(x, base):
    depth, _, columns = base.shape
    return pl.pallas_call(
        gate_up_kernel,
        out_shape=jax.ShapeDtypeStruct((2 * x.shape[0], columns), jnp.float32),
        in_specs=[VMEM, HBM],
        out_specs=VMEM,
        scratch_shapes=[pltpu.VMEM(base.shape, base.dtype), pltpu.SemaphoreType.DMA((depth // 512,))],
        compiler_params=pltpu.CompilerParams(vmem_limit_bytes=32 << 20),
        cost_estimate=pl.CostEstimate(
            flops=4 * x.shape[0] * depth * columns, bytes_accessed=2 * base.size, transcendentals=0
        ),
    )(x, in_hbm(base))


def part_kernel(bit, term, received, *refs):
    *outs, total = refs
    half, width = total.shape
    size, step = half // 4, width // (len(outs) // 2)
    me = lax.axis_index("tensor")
    core, flag = me % 2, (me // (2 * bit)) % 2
    total[...] = term[pl.ds(pl.multiple_of(core * half, half), half), :].astype(jnp.float32) + received[
        ...
    ].astype(jnp.float32)
    sent = (2 - core * (1 + flag), 3 - core * flag)
    kept = (core * flag, 1 + core * (1 + flag))
    for i, out in enumerate(outs):
        columns = pl.ds((i // 2) * step, step)
        rows = [
            total[pl.ds(pl.multiple_of(block * size, size), size), columns] for block in (sent, kept)[i % 2]
        ]
        out[...] = jnp.concatenate(rows).astype(out.dtype)


def add_and_part(term, received, bit):
    half, width = received.shape
    outs = pl.pallas_call(
        functools.partial(part_kernel, bit),
        out_shape=[jax.ShapeDtypeStruct((half // 2, width // CHUNKS), term.dtype)] * (2 * CHUNKS),
        in_specs=[VMEM, VMEM],
        out_specs=[VMEM] * (2 * CHUNKS),
        scratch_shapes=[pltpu.VMEM((half, width), jnp.float32)],
        compiler_params=pltpu.CompilerParams(vmem_limit_bytes=16 << 20),
        cost_estimate=pl.CostEstimate(flops=0, bytes_accessed=6 * received.size, transcendentals=0),
    )(term, received)
    return list(zip(outs[::2], outs[1::2]))


def local(
    tokens,
    routes,
    numerators,
    place,
    base_in,
    base_down,
    delta_in,
    delta_mid,
    delta_down,
    delta_back,
):
    clusters = lax.axis_size("expert")
    members = lax.axis_size("tensor")
    me = lax.axis_index("tensor")
    cluster = lax.axis_index("expert")
    core = me % 2
    count, width = tokens.shape[1:]
    top = routes.shape[2]

    along, across = halves(clusters), halves(members // 2)
    shared, paired = along[: len(along) - len(across)], along[len(along) - len(across) :]

    packed = pack(tokens[0], routes[0], numerators[0])
    chips = members // 2
    pieces = {(0, 0): packed}
    for z in range(clusters - 1, 0, -1):
        pieces[0, z] = trade(packed, (z, 0), (z, 0))
    for x in range(1, chips):
        pieces[x, 0] = trade(packed, (0, 2 * x), (0, 2 * x))
    rest = jnp.concatenate([pieces[0, z] for z in range(1, clusters)])
    for x in range(1, chips):
        received = trade(rest, (0, 2 * x), (0, 2 * x))
        for z in range(1, clusters):
            pieces[x, z] = received[(z - 1) * count : z * count]

    for bit in across:
        for x in range(chips):
            if not x & bit:
                for z in range(clusters):
                    flag = (me // (2 * bit)) % 2 == 1
                    pieces[x, z], pieces[x | bit, z] = ordered(flag, pieces[x, z], pieces[x | bit, z])
    places = [(0, 0)]
    for mask in shared:
        places += [(x, z | mask) for x, z in places]
    for zbit, xbit in zip(paired, across):
        places += [(x | xbit, z) for x, z in places]
        places += [(x, z | zbit) for x, z in places]
    held = by_rows(jnp.concatenate([pieces[place] for place in places]))
    held = by_rows(jnp.concatenate(ordered(core == 1, held, trade(held, (0, 1), (0, 1)))))
    rows, code_table = lax.optimization_barrier((held, delta_in[0]))

    codes = jnp.dot(rows[:, :width], code_table, preferred_element_type=jnp.float32).astype(jnp.bfloat16)
    projected = gate_up_product(held, base_in[0])

    side = by_rows(rows[:, width:])
    all_routes = side[:, :top].astype(jnp.int32)
    numerator = side[:, top : 2 * top].astype(jnp.float32)
    position = lookup(place, all_routes)
    weight = (2.5 * numerator / jnp.sum(numerator, axis=-1, keepdims=True)).astype(jnp.bfloat16)
    target = cluster * members + jnp.arange(members, dtype=jnp.int32)
    scale = jnp.sum(
        jnp.where(position[None] == target[:, None, None], weight[None].astype(jnp.float32), 0.0), axis=-1
    )

    codes = jnp.stack([codes if m == 0 else trade(codes, (0, m), (0, m)) for m in range(members)])
    by_slot = jnp.stack([lax.dynamic_index_in_dim(codes, s ^ me, 0, keepdims=False) for s in range(members)])

    lifted = jnp.einsum("srk,skgf->srgf", by_slot, delta_mid[0], preferred_element_type=jnp.float32)
    total = held.shape[0]
    hidden = jax.nn.silu(projected[None, :total] + lifted[:, :, 0]) * (projected[None, total:] + lifted[:, :, 1])
    hidden_sum = jnp.sum(scale[:, :, None] * hidden, axis=0).astype(jnp.bfloat16)
    partial_codes = jnp.einsum(
        "srf,sfk->srk", hidden.astype(jnp.bfloat16), delta_down[0], preferred_element_type=jnp.float32
    ).astype(jnp.bfloat16)
    by_core = partial_codes.reshape(chips, 2, *partial_codes.shape[1:])
    kept, sent = (lax.dynamic_index_in_dim(by_core, c, 1, keepdims=False) for c in (core, 1 - core))
    by_chip = add(kept, trade(sent, (0, 1), (0, 1)))
    chip = me // 2
    lowrank = lax.dynamic_index_in_dim(by_chip, chip, 0, keepdims=False).astype(jnp.float32)
    for m in range(1, chips):
        sent = lax.dynamic_index_in_dim(by_chip, chip ^ m, 0, keepdims=False)
        lowrank = lowrank + trade(sent, (0, 2 * m), (0, 2 * m)).astype(jnp.float32)
    own_scale = lax.dynamic_index_in_dim(scale, me, 0, keepdims=False)
    scaled = (own_scale[:, None] * lowrank).astype(jnp.bfloat16)

    term = jnp.dot(hidden_sum, base_down[0], preferred_element_type=jnp.float32)
    term = (term + jnp.dot(scaled, delta_back[0], preferred_element_type=jnp.float32)).astype(jnp.bfloat16)

    half = term.shape[0] // 2
    sent = ordered(core == 1, term[half:], term[:half])[0]
    outputs = []
    for sent, kept in add_and_part(term, trade(sent, (0, 1), (0, 1)), across[-1]):
        for i, (z, x) in enumerate(reversed(list(zip(paired, across)))):
            flag = (me // (2 * x)) % 2 == 1
            if i:
                size = total.shape[0] // 4
                blocks = [total[j * size : (j + 1) * size] for j in range(4)]
                inner = ordered(core == 1, blocks[1], blocks[2])
                kept, sent = ordered(
                    (core == 1) & flag,
                    jnp.concatenate([blocks[0], inner[0]]),
                    jnp.concatenate([inner[1], blocks[3]]),
                )
            total = add(kept, trade(sent, (z, 0), (0, 2 * x)))
            size = total.shape[0] // 2
            kept, sent = ordered((core == 0) & flag, total[:size], total[size:])
            total = add(kept, trade(sent, (0, 2 * x), (z, 0)))
        for mask in reversed(shared):
            size = total.shape[0] // 2
            total = add(total[:size], trade(total[size:], (mask, 0), (mask, 0)))
        outputs.append(total)
    return jnp.concatenate(outputs, axis=1)[None]


def solution(mesh):
    placed = (
        P(None, ("parts", "expert", "tensor"), None),
        P(None, ("parts", "expert", "tensor"), None),
        P(None, ("parts", "expert", "tensor"), None),
        P("parts"),
        P("expert", None, None, "tensor"),
        P("expert", "tensor", None),
        P(("expert", "tensor"), None, None),
        P("expert", None, None, None, "tensor"),
        P("expert", None, "tensor", None),
        P(("expert", "tensor"), None, None),
    )
    return jax.shard_map(
        local,
        mesh=mesh,
        in_specs=placed,
        out_specs=P(None, ("parts", "expert", "tensor"), None),
        check_vma=False,
    )
```

```python
import functools

import jax
import jax.numpy as jnp
from jax import lax
from jax.experimental import pallas as pl
from jax.experimental.pallas import tpu as pltpu
from jax.experimental.layout import Layout, with_layout_constraint
from jax.sharding import PartitionSpec as P

CHUNKS = 2
VMEM = pl.BlockSpec(memory_space=pltpu.VMEM)
HBM = pl.BlockSpec(memory_space=pltpu.HBM)


def in_hbm(value):
    return pltpu.with_memory_space_constraint(value, pltpu.HBM)


def by_rows(value):
    return with_layout_constraint(value, Layout((0, 1)))


def lookup(table, index):
    keys = jnp.arange(table.shape[0], dtype=jnp.int32)
    return jnp.sum(jnp.where(index[..., None] == keys, table, 0), axis=-1)


def trade(value, even, odd):
    members = lax.axis_size("tensor")
    pairs = []
    for e in range(lax.axis_size("expert")):
        for t in range(members):
            along, across = odd if t % 2 else even
            pairs.append((e * members + t, (e ^ along) * members + (t ^ across)))
    return lax.ppermute(value, ("expert", "tensor"), pairs)


def halves(size):
    masks = []
    while size > 1:
        size //= 2
        masks.append(size)
    return masks


def ordered(flip, first, second):
    return jnp.where(flip, second, first), jnp.where(flip, first, second)


def add(kept, received):
    return (kept.astype(jnp.float32) + received.astype(jnp.float32)).astype(jnp.bfloat16)


def pack_kernel(tokens, routes, numerators, packed, routes_in, numerators_in, sems):
    width, top = tokens.shape[1], routes.shape[1]
    copies = [
        pltpu.make_async_copy(tokens, packed.at[:, pl.ds(0, width)], sems.at[0]),
        pltpu.make_async_copy(routes, routes_in, sems.at[1]),
        pltpu.make_async_copy(numerators, numerators_in, sems.at[2]),
    ]
    for copy in copies:
        copy.start()
    packed[:, width:] = jnp.zeros((packed.shape[0], packed.shape[1] - width), packed.dtype)
    for copy in copies[1:]:
        copy.wait()
    packed[:, width : width + top] = routes_in[...].astype(jnp.float32).astype(packed.dtype)
    packed[:, width + top : width + 2 * top] = numerators_in[...].astype(jnp.float32).astype(packed.dtype)
    copies[0].wait()


def pack(tokens, routes, numerators):
    count, width = tokens.shape
    return pl.pallas_call(
        pack_kernel,
        out_shape=jax.ShapeDtypeStruct((count, width + 128), tokens.dtype),
        in_specs=[HBM] * 3,
        out_specs=VMEM,
        scratch_shapes=[
            pltpu.VMEM(routes.shape, routes.dtype),
            pltpu.VMEM(numerators.shape, numerators.dtype),
            pltpu.SemaphoreType.DMA((3,)),
        ],
        compiler_params=pltpu.CompilerParams(vmem_limit_bytes=4 << 20),
        cost_estimate=pl.CostEstimate(flops=20 * 10**9, bytes_accessed=4 * tokens.size, transcendentals=0),
    )(in_hbm(tokens), in_hbm(routes), in_hbm(numerators))


def gate_up_kernel(x, base, out, weights, sems):
    depth, _, columns = weights.shape
    step = depth // sems.shape[0]
    copies = [
        pltpu.make_async_copy(base.at[pl.ds(k, step)], weights.at[pl.ds(k, step)], sems.at[k // step])
        for k in range(0, depth, step)
    ]
    for copy in copies:
        copy.start()
    row = lax.broadcasted_iota(jnp.int32, (128, 256), 0)
    column = lax.broadcasted_iota(jnp.int32, (128, 256), 1)
    spread = jnp.where(column // 2 == row, 1.0, 0.0).astype(jnp.bfloat16)
    is_odd = (lax.broadcasted_iota(jnp.int32, (1, 2 * step), 1) % 2).astype(jnp.float32)
    odd_mask, even_mask = is_odd.astype(jnp.bfloat16), (1.0 - is_odd).astype(jnp.bfloat16)
    count = x.shape[0]
    flat = weights.reshape(2 * depth, columns)
    total = jnp.zeros(out.shape, jnp.float32)
    for k in range(0, depth, step):
        stacked = jnp.concatenate([x[:, i : i + 128] for i in range(k, k + step, 128)])
        wide = jnp.dot(stacked, spread, preferred_element_type=jnp.float32).astype(jnp.bfloat16)
        wide = jnp.concatenate([wide[i : i + count] for i in range(0, stacked.shape[0], count)], axis=1)
        copies[k // step].wait()
        total += jnp.dot(
            jnp.concatenate([wide * even_mask, wide * odd_mask]), flat[2 * k : 2 * (k + step), :], preferred_element_type=jnp.float32
        )
    out[...] = total


def gate_up_product(x, base):
    depth, _, columns = base.shape
    return pl.pallas_call(
        gate_up_kernel,
        out_shape=jax.ShapeDtypeStruct((2 * x.shape[0], columns), jnp.float32),
        in_specs=[VMEM, HBM],
        out_specs=VMEM,
        scratch_shapes=[pltpu.VMEM(base.shape, base.dtype), pltpu.SemaphoreType.DMA((depth // 512,))],
        compiler_params=pltpu.CompilerParams(vmem_limit_bytes=32 << 20),
        cost_estimate=pl.CostEstimate(
            flops=4 * x.shape[0] * depth * columns, bytes_accessed=2 * base.size, transcendentals=0
        ),
    )(x, in_hbm(base))


def part_kernel(bit, term, received, *refs):
    *outs, total = refs
    half, width = total.shape
    size, step = half // 4, width // (len(outs) // 2)
    me = lax.axis_index("tensor")
    core, flag = me % 2, (me // (2 * bit)) % 2
    total[...] = term[pl.ds(pl.multiple_of(core * half, half), half), :].astype(jnp.float32) + received[
        ...
    ].astype(jnp.float32)
    by_x = 1 - core
    sent = (2 - by_x * (1 + flag), 3 - by_x * flag)
    kept = (by_x * flag, 1 + by_x * (1 + flag))
    for i, out in enumerate(outs):
        columns = pl.ds((i // 2) * step, step)
        rows = [
            total[pl.ds(pl.multiple_of(block * size, size), size), columns] for block in (sent, kept)[i % 2]
        ]
        out[...] = jnp.concatenate(rows).astype(out.dtype)


def add_and_part(term, received, bit):
    half, width = received.shape
    outs = pl.pallas_call(
        functools.partial(part_kernel, bit),
        out_shape=[jax.ShapeDtypeStruct((half // 2, width // CHUNKS), term.dtype)] * (2 * CHUNKS),
        in_specs=[VMEM, VMEM],
        out_specs=[VMEM] * (2 * CHUNKS),
        scratch_shapes=[pltpu.VMEM((half, width), jnp.float32)],
        compiler_params=pltpu.CompilerParams(vmem_limit_bytes=16 << 20),
        cost_estimate=pl.CostEstimate(flops=0, bytes_accessed=6 * received.size, transcendentals=0),
    )(term, received)
    return list(zip(outs[::2], outs[1::2]))


def local(
    tokens,
    routes,
    numerators,
    place,
    base_in,
    base_down,
    delta_in,
    delta_mid,
    delta_down,
    delta_back,
):
    clusters = lax.axis_size("expert")
    members = lax.axis_size("tensor")
    me = lax.axis_index("tensor")
    cluster = lax.axis_index("expert")
    core = me % 2
    count, width = tokens.shape[1:]
    top = routes.shape[2]

    along, across = halves(clusters), halves(members // 2)
    shared, paired = along[: len(along) - len(across)], along[len(along) - len(across) :]

    packed = pack(tokens[0], routes[0], numerators[0])
    chips = members // 2
    pieces = {(0, 0): packed}
    for z in range(clusters - 1, 0, -1):
        pieces[0, z] = trade(packed, (z, 0), (z, 0))
    for x in range(1, chips):
        pieces[x, 0] = trade(packed, (0, 2 * x), (0, 2 * x))
    rest = jnp.concatenate([pieces[0, z] for z in range(1, clusters)])
    for x in range(1, chips):
        received = trade(rest, (0, 2 * x), (0, 2 * x))
        for z in range(1, clusters):
            pieces[x, z] = received[(z - 1) * count : z * count]

    for bit in across:
        for x in range(chips):
            if not x & bit:
                for z in range(clusters):
                    flag = (me // (2 * bit)) % 2 == 1
                    pieces[x, z], pieces[x | bit, z] = ordered(flag, pieces[x, z], pieces[x | bit, z])
    places = [(0, 0)]
    for mask in shared:
        places += [(x, z | mask) for x, z in places]
    for zbit, xbit in zip(paired, across):
        places += [(x | xbit, z) for x, z in places]
        places += [(x, z | zbit) for x, z in places]
    held = by_rows(jnp.concatenate([pieces[place] for place in places]))
    held = by_rows(jnp.concatenate(ordered(core == 1, held, trade(held, (0, 1), (0, 1)))))
    rows, code_table = lax.optimization_barrier((held, delta_in[0]))

    codes = jnp.dot(rows[:, :width], code_table, preferred_element_type=jnp.float32).astype(jnp.bfloat16)
    projected = gate_up_product(held, base_in[0])

    side = by_rows(rows[:, width:])
    all_routes = side[:, :top].astype(jnp.int32)
    numerator = side[:, top : 2 * top].astype(jnp.float32)
    position = lookup(place, all_routes)
    weight = (2.5 * numerator / jnp.sum(numerator, axis=-1, keepdims=True)).astype(jnp.bfloat16)
    target = cluster * members + jnp.arange(members, dtype=jnp.int32)
    scale = jnp.sum(
        jnp.where(position[None] == target[:, None, None], weight[None].astype(jnp.float32), 0.0), axis=-1
    )

    codes = jnp.stack([codes if m == 0 else trade(codes, (0, m), (0, m)) for m in range(members)])
    by_slot = jnp.stack([lax.dynamic_index_in_dim(codes, s ^ me, 0, keepdims=False) for s in range(members)])

    lifted = jnp.einsum("srk,skgf->srgf", by_slot, delta_mid[0], preferred_element_type=jnp.float32)
    total = held.shape[0]
    hidden = jax.nn.silu(projected[None, :total] + lifted[:, :, 0]) * (projected[None, total:] + lifted[:, :, 1])
    hidden_sum = jnp.sum(scale[:, :, None] * hidden, axis=0).astype(jnp.bfloat16)
    partial_codes = jnp.einsum(
        "srf,sfk->srk", hidden.astype(jnp.bfloat16), delta_down[0], preferred_element_type=jnp.float32
    ).astype(jnp.bfloat16)
    by_core = partial_codes.reshape(chips, 2, *partial_codes.shape[1:])
    kept, sent = (lax.dynamic_index_in_dim(by_core, c, 1, keepdims=False) for c in (core, 1 - core))
    by_chip = add(kept, trade(sent, (0, 1), (0, 1)))
    chip = me // 2
    lowrank = lax.dynamic_index_in_dim(by_chip, chip, 0, keepdims=False).astype(jnp.float32)
    for m in range(1, chips):
        sent = lax.dynamic_index_in_dim(by_chip, chip ^ m, 0, keepdims=False)
        lowrank = lowrank + trade(sent, (0, 2 * m), (0, 2 * m)).astype(jnp.float32)
    own_scale = lax.dynamic_index_in_dim(scale, me, 0, keepdims=False)
    scaled = (own_scale[:, None] * lowrank).astype(jnp.bfloat16)

    hidden_sum, down_table = lax.optimization_barrier((hidden_sum, base_down[0]))
    term = jnp.dot(hidden_sum, down_table, preferred_element_type=jnp.float32)
    term = (term + jnp.dot(scaled, delta_back[0], preferred_element_type=jnp.float32)).astype(jnp.bfloat16)

    half = term.shape[0] // 2
    sent = ordered(core == 1, term[half:], term[:half])[0]
    outputs = []
    for sent, kept in add_and_part(term, trade(sent, (0, 1), (0, 1)), across[-1]):
        for i, (z, x) in enumerate(reversed(list(zip(paired, across)))):
            flag = (me // (2 * x)) % 2 == 1
            if i:
                size = total.shape[0] // 4
                blocks = [total[j * size : (j + 1) * size] for j in range(4)]
                inner = ordered(core == 0, blocks[1], blocks[2])
                kept, sent = ordered(
                    (core == 0) & flag,
                    jnp.concatenate([blocks[0], inner[0]]),
                    jnp.concatenate([inner[1], blocks[3]]),
                )
            total = add(kept, trade(sent, (0, 2 * x), (z, 0)))
            size = total.shape[0] // 2
            kept, sent = ordered((core == 1) & flag, total[:size], total[size:])
            total = add(kept, trade(sent, (z, 0), (0, 2 * x)))
        for mask in reversed(shared):
            size = total.shape[0] // 2
            total = add(total[:size], trade(total[size:], (mask, 0), (mask, 0)))
        outputs.append(total)
    return jnp.concatenate(outputs, axis=1)[None]


def solution(mesh):
    placed = (
        P(None, ("parts", "expert", "tensor"), None),
        P(None, ("parts", "expert", "tensor"), None),
        P(None, ("parts", "expert", "tensor"), None),
        P("parts"),
        P("expert", None, None, "tensor"),
        P("expert", "tensor", None),
        P(("expert", "tensor"), None, None),
        P("expert", None, None, None, "tensor"),
        P("expert", None, "tensor", None),
        P(("expert", "tensor"), None, None),
    )
    return jax.shard_map(
        local,
        mesh=mesh,
        in_specs=placed,
        out_specs=P(None, ("parts", "expert", "tensor"), None),
        check_vma=False,
    )
```

```python
import functools
import itertools

import jax
import jax.numpy as jnp
from jax import lax
from jax.experimental import pallas as pl
from jax.experimental.pallas import tpu as pltpu
from jax.experimental.layout import Layout, with_layout_constraint
from jax.sharding import PartitionSpec as P

CHUNKS = 2
VMEM = pl.BlockSpec(memory_space=pltpu.VMEM)
HBM = pl.BlockSpec(memory_space=pltpu.HBM)


def in_hbm(value):
    return pltpu.with_memory_space_constraint(value, pltpu.HBM)


def by_rows(value):
    return with_layout_constraint(value, Layout((0, 1)))


def lookup(table, index):
    keys = jnp.arange(table.shape[0], dtype=jnp.int32)
    return jnp.sum(jnp.where(index[..., None] == keys, table, 0), axis=-1)


def trade(value, even, odd):
    members = lax.axis_size("tensor")
    pairs = []
    for e in range(lax.axis_size("expert")):
        for t in range(members):
            along, across = odd if t % 2 else even
            pairs.append((e * members + t, (e ^ along) * members + (t ^ across)))
    return lax.ppermute(value, ("expert", "tensor"), pairs)


def halves(size):
    masks = []
    while size > 1:
        size //= 2
        masks.append(size)
    return masks


def ordered(flip, first, second):
    return jnp.where(flip, second, first), jnp.where(flip, first, second)


def add(kept, received):
    return (kept.astype(jnp.float32) + received.astype(jnp.float32)).astype(jnp.bfloat16)


def pack_kernel(tokens, routes, numerators, packed, routes_in, numerators_in, sems):
    width, top = tokens.shape[1], routes.shape[1]
    copies = [
        pltpu.make_async_copy(tokens, packed.at[:, pl.ds(0, width)], sems.at[0]),
        pltpu.make_async_copy(routes, routes_in, sems.at[1]),
        pltpu.make_async_copy(numerators, numerators_in, sems.at[2]),
    ]
    for copy in copies:
        copy.start()
    packed[:, width:] = jnp.zeros((packed.shape[0], packed.shape[1] - width), packed.dtype)
    for copy in copies[1:]:
        copy.wait()
    packed[:, width : width + top] = routes_in[...].astype(jnp.float32).astype(packed.dtype)
    packed[:, width + top : width + 2 * top] = numerators_in[...].astype(jnp.float32).astype(packed.dtype)
    copies[0].wait()


def pack(tokens, routes, numerators):
    count, width = tokens.shape
    return pl.pallas_call(
        pack_kernel,
        out_shape=jax.ShapeDtypeStruct((count, width + 128), tokens.dtype),
        in_specs=[HBM] * 3,
        out_specs=VMEM,
        scratch_shapes=[
            pltpu.VMEM(routes.shape, routes.dtype),
            pltpu.VMEM(numerators.shape, numerators.dtype),
            pltpu.SemaphoreType.DMA((3,)),
        ],
        compiler_params=pltpu.CompilerParams(vmem_limit_bytes=4 << 20),
        cost_estimate=pl.CostEstimate(flops=20 * 10**9, bytes_accessed=4 * tokens.size, transcendentals=0),
    )(in_hbm(tokens), in_hbm(routes), in_hbm(numerators))


def gate_up_kernel(x, base, out):
    depth, _, columns = base.shape
    step = 512
    row = lax.broadcasted_iota(jnp.int32, (128, 256), 0)
    column = lax.broadcasted_iota(jnp.int32, (128, 256), 1)
    spread = jnp.where(column // 2 == row, 1.0, 0.0).astype(jnp.bfloat16)
    is_odd = (lax.broadcasted_iota(jnp.int32, (1, 2 * step), 1) % 2).astype(jnp.float32)
    odd_mask, even_mask = is_odd.astype(jnp.bfloat16), (1.0 - is_odd).astype(jnp.bfloat16)
    count = x.shape[0]
    flat = base.reshape(2 * depth, columns)
    total = jnp.zeros(out.shape, jnp.float32)
    for k in range(0, depth, step):
        stacked = jnp.concatenate([x[:, i : i + 128] for i in range(k, k + step, 128)])
        wide = jnp.dot(stacked, spread, preferred_element_type=jnp.float32).astype(jnp.bfloat16)
        wide = jnp.concatenate([wide[i : i + count] for i in range(0, stacked.shape[0], count)], axis=1)
        total += jnp.dot(
            jnp.concatenate([wide * even_mask, wide * odd_mask]),
            flat[2 * k : 2 * (k + step), :],
            preferred_element_type=jnp.float32,
        )
    out[...] = total


def gate_up_product(x, base):
    depth, _, columns = base.shape
    return pl.pallas_call(
        gate_up_kernel,
        out_shape=jax.ShapeDtypeStruct((2 * x.shape[0], columns), jnp.float32),
        in_specs=[VMEM, VMEM],
        out_specs=VMEM,
        compiler_params=pltpu.CompilerParams(vmem_limit_bytes=16 << 20),
        cost_estimate=pl.CostEstimate(
            flops=4 * x.shape[0] * depth * columns, bytes_accessed=2 * base.size, transcendentals=0
        ),
    )(x, base)


def down_kernel(hidden, base, out, weights, sems):
    step = base.shape[1] // sems.shape[0]
    parts = [pl.ds(k * step, step) for k in range(sems.shape[0])]
    copies = [pltpu.make_async_copy(base.at[:, part], weights.at[:, part], sems.at[k]) for k, part in enumerate(parts)]
    for copy in copies:
        copy.start()
    for copy, part in zip(copies, parts):
        copy.wait()
        out[:, part] = jnp.dot(hidden[...], weights[:, part], preferred_element_type=jnp.float32)


def down_product(hidden, base):
    rows, width = hidden.shape[0], base.shape[1]
    return pl.pallas_call(
        down_kernel,
        out_shape=jax.ShapeDtypeStruct((rows, width), jnp.float32),
        in_specs=[VMEM, HBM],
        out_specs=VMEM,
        scratch_shapes=[pltpu.VMEM(base.shape, base.dtype), pltpu.SemaphoreType.DMA((width // 1024,))],
        compiler_params=pltpu.CompilerParams(vmem_limit_bytes=16 << 20),
        cost_estimate=pl.CostEstimate(flops=2 * rows * base.size, bytes_accessed=2 * base.size, transcendentals=0),
    )(hidden, in_hbm(base))


def part_kernel(bit, term, received, *refs):
    *outs, total = refs
    half, width = total.shape
    size, step = half // 4, width // (len(outs) // 2)
    me = lax.axis_index("tensor")
    core, flag = me % 2, (me // (2 * bit)) % 2
    total[...] = term[pl.ds(pl.multiple_of(core * half, half), half), :].astype(jnp.float32) + received[
        ...
    ].astype(jnp.float32)
    by_x = 1 - core
    sent = (core + by_x * 2 * (1 - flag), 3 - by_x * 2 * flag)
    kept = (by_x * 2 * flag, 2 * core + by_x * (2 * flag + 1))
    for i, out in enumerate(outs):
        columns = pl.ds((i // 2) * step, step)
        rows = [
            total[pl.ds(pl.multiple_of(block * size, size), size), columns] for block in (sent, kept)[i % 2]
        ]
        out[...] = jnp.concatenate(rows).astype(out.dtype)


def add_and_part(term, received, bit):
    half, width = received.shape
    outs = pl.pallas_call(
        functools.partial(part_kernel, bit),
        out_shape=[jax.ShapeDtypeStruct((half // 2, width // CHUNKS), term.dtype)] * (2 * CHUNKS),
        in_specs=[VMEM, VMEM],
        out_specs=[VMEM] * (2 * CHUNKS),
        scratch_shapes=[pltpu.VMEM((half, width), jnp.float32)],
        compiler_params=pltpu.CompilerParams(vmem_limit_bytes=16 << 20),
        cost_estimate=pl.CostEstimate(flops=0, bytes_accessed=6 * received.size, transcendentals=0),
    )(term, received)
    return list(zip(outs[::2], outs[1::2]))


def local(
    tokens,
    routes,
    numerators,
    place,
    base_in,
    base_down,
    delta_in,
    delta_mid,
    delta_down,
    delta_back,
):
    clusters = lax.axis_size("expert")
    members = lax.axis_size("tensor")
    me = lax.axis_index("tensor")
    cluster = lax.axis_index("expert")
    core = me % 2
    count, width = tokens.shape[1:]
    top = routes.shape[2]

    along, across = halves(clusters), halves(members // 2)
    shared, paired = along[: len(along) - len(across)], along[len(along) - len(across) :]

    packed = pack(tokens[0], routes[0], numerators[0])
    chips = members // 2
    pieces = {(0, 0): packed}
    for z in range(clusters - 1, 0, -1):
        pieces[0, z] = trade(packed, (z, 0), (z, 0))
    for x in range(1, chips):
        pieces[x, 0] = trade(packed, (0, 2 * x), (0, 2 * x))
    places = [(0, 0)]
    for mask in shared:
        places += [(x, z | mask) for x, z in places]
    for zbit, xbit in zip(paired, across):
        places += [(x, z | zbit) for x, z in places]
        places += [(x | xbit, z) for x, z in places]
    later = [z for x, z in places if x == 0 and z]
    rest = jnp.concatenate([pieces[0, z] for z in later])
    rest, *firsts = lax.optimization_barrier((rest, *(pieces[x, 0] for x in range(1, chips))))
    pieces.update({(x, 0): first for x, first in enumerate(firsts, 1)})
    for x in range(chips):
        received = trade(rest, (0, 2 * x), (0, 2 * x)) if x else rest
        for i, z in enumerate(later):
            pieces[x, z] = received[i * count : (i + 1) * count]
    segments = [(x, tuple(z for _, z in run)) for x, run in itertools.groupby(places, lambda place: place[0])]
    runs = {(x, zs): jnp.concatenate([pieces[x, z] for z in zs]) for x, zs in segments}
    for bit in across:
        flag = (me // (2 * bit)) % 2 == 1
        for x, zs in runs:
            if not x & bit:
                runs[x, zs], runs[x | bit, zs] = ordered(flag, runs[x, zs], runs[x | bit, zs])
    held = by_rows(jnp.concatenate([runs[segment] for segment in segments]))
    held = by_rows(jnp.concatenate(ordered(core == 1, held, trade(held, (0, 1), (0, 1)))))

    codes = jnp.dot(held[:, :width], delta_in[0], preferred_element_type=jnp.float32).astype(jnp.bfloat16)
    projected = gate_up_product(held, base_in[0])

    side = by_rows(held[:, width:])
    all_routes = side[:, :top].astype(jnp.int32)
    numerator = side[:, top : 2 * top].astype(jnp.float32)
    position = lookup(place, all_routes)
    weight = (2.5 * numerator / jnp.sum(numerator, axis=-1, keepdims=True)).astype(jnp.bfloat16)
    target = cluster * members + jnp.arange(members, dtype=jnp.int32)
    scale = jnp.sum(
        jnp.where(position[None] == target[:, None, None], weight[None].astype(jnp.float32), 0.0), axis=-1
    )

    codes = jnp.stack([codes if m == 0 else trade(codes, (0, m), (0, m)) for m in range(members)])
    by_slot = jnp.stack([lax.dynamic_index_in_dim(codes, s ^ me, 0, keepdims=False) for s in range(members)])

    lifted = jnp.einsum("srk,skgf->srgf", by_slot, delta_mid[0], preferred_element_type=jnp.float32)
    total = held.shape[0]
    hidden = jax.nn.silu(projected[None, :total] + lifted[:, :, 0]) * (projected[None, total:] + lifted[:, :, 1])
    hidden_sum = jnp.sum(scale[:, :, None] * hidden, axis=0).astype(jnp.bfloat16)
    partial_codes = jnp.einsum(
        "srf,sfk->srk", hidden.astype(jnp.bfloat16), delta_down[0], preferred_element_type=jnp.float32
    ).astype(jnp.bfloat16)
    by_core = partial_codes.reshape(chips, 2, *partial_codes.shape[1:])
    kept, sent = (lax.dynamic_index_in_dim(by_core, c, 1, keepdims=False) for c in (core, 1 - core))
    by_chip = add(kept, trade(sent, (0, 1), (0, 1)))
    chip = me // 2
    lowrank = lax.dynamic_index_in_dim(by_chip, chip, 0, keepdims=False).astype(jnp.float32)
    for m in range(1, chips):
        sent = lax.dynamic_index_in_dim(by_chip, chip ^ m, 0, keepdims=False)
        lowrank = lowrank + trade(sent, (0, 2 * m), (0, 2 * m)).astype(jnp.float32)
    own_scale = lax.dynamic_index_in_dim(scale, me, 0, keepdims=False)
    scaled = (own_scale[:, None] * lowrank).astype(jnp.bfloat16)

    term = down_product(hidden_sum, base_down[0])
    term = (term + jnp.dot(scaled, delta_back[0], preferred_element_type=jnp.float32)).astype(jnp.bfloat16)

    half = term.shape[0] // 2
    sent = ordered(core == 1, term[half:], term[:half])[0]
    outputs = []
    for sent, kept in add_and_part(term, trade(sent, (0, 1), (0, 1)), across[-1]):
        for i, (z, x) in enumerate(reversed(list(zip(paired, across)))):
            flag = (me // (2 * x)) % 2 == 1
            if i:
                size = total.shape[0] // 4
                blocks = [total[j * size : (j + 1) * size] for j in range(4)]
                inner = ordered(core == 1, blocks[1], blocks[2])
                kept, sent = ordered(
                    (core == 0) & flag,
                    jnp.concatenate([blocks[0], inner[0]]),
                    jnp.concatenate([inner[1], blocks[3]]),
                )
            total = add(kept, trade(sent, (0, 2 * x), (z, 0)))
            size = total.shape[0] // 2
            kept, sent = ordered((core == 1) & flag, total[:size], total[size:])
            total = add(kept, trade(sent, (z, 0), (0, 2 * x)))
        for mask in reversed(shared):
            size = total.shape[0] // 2
            total = add(total[:size], trade(total[size:], (mask, 0), (mask, 0)))
        outputs.append(total)
    return jnp.concatenate(outputs, axis=1)[None]


def solution(mesh):
    placed = (
        P(None, ("parts", "expert", "tensor"), None),
        P(None, ("parts", "expert", "tensor"), None),
        P(None, ("parts", "expert", "tensor"), None),
        P("parts"),
        P("expert", None, None, "tensor"),
        P("expert", "tensor", None),
        P(("expert", "tensor"), None, None),
        P("expert", None, None, None, "tensor"),
        P("expert", None, "tensor", None),
        P(("expert", "tensor"), None, None),
    )
    return jax.shard_map(
        local,
        mesh=mesh,
        in_specs=placed,
        out_specs=P(None, ("parts", "expert", "tensor"), None),
        check_vma=False,
    )
```

```python
import functools
import itertools

import jax
import jax.numpy as jnp
from jax import lax
from jax.experimental import pallas as pl
from jax.experimental.pallas import tpu as pltpu
from jax.experimental.layout import Layout, with_layout_constraint
from jax.sharding import PartitionSpec as P

CHUNKS = 2
VMEM = pl.BlockSpec(memory_space=pltpu.VMEM)
HBM = pl.BlockSpec(memory_space=pltpu.HBM)


def in_hbm(value):
    return pltpu.with_memory_space_constraint(value, pltpu.HBM)


def by_rows(value):
    return with_layout_constraint(value, Layout((0, 1)))


def lookup(table, index):
    keys = jnp.arange(table.shape[0], dtype=jnp.int32)
    return jnp.sum(jnp.where(index[..., None] == keys, table, 0), axis=-1)


def trade(value, even, odd):
    members = lax.axis_size("tensor")
    pairs = []
    for e in range(lax.axis_size("expert")):
        for t in range(members):
            along, across = odd if t % 2 else even
            pairs.append((e * members + t, (e ^ along) * members + (t ^ across)))
    return lax.ppermute(value, ("expert", "tensor"), pairs)


def halves(size):
    masks = []
    while size > 1:
        size //= 2
        masks.append(size)
    return masks


def ordered(flip, first, second):
    return jnp.where(flip, second, first), jnp.where(flip, first, second)


def add(kept, received):
    return (kept.astype(jnp.float32) + received.astype(jnp.float32)).astype(jnp.bfloat16)


def pack_kernel(tokens, routes, numerators, packed, routes_in, numerators_in, sems):
    width, top = tokens.shape[1], routes.shape[1]
    copies = [
        pltpu.make_async_copy(tokens, packed.at[:, pl.ds(0, width)], sems.at[0]),
        pltpu.make_async_copy(routes, routes_in, sems.at[1]),
        pltpu.make_async_copy(numerators, numerators_in, sems.at[2]),
    ]
    for copy in copies:
        copy.start()
    packed[:, width:] = jnp.zeros((packed.shape[0], packed.shape[1] - width), packed.dtype)
    for copy in copies[1:]:
        copy.wait()
    packed[:, width : width + top] = routes_in[...].astype(jnp.float32).astype(packed.dtype)
    packed[:, width + top : width + 2 * top] = numerators_in[...].astype(jnp.float32).astype(packed.dtype)
    copies[0].wait()


def pack(tokens, routes, numerators):
    count, width = tokens.shape
    return pl.pallas_call(
        pack_kernel,
        out_shape=jax.ShapeDtypeStruct((count, width + 128), tokens.dtype),
        in_specs=[HBM] * 3,
        out_specs=VMEM,
        scratch_shapes=[
            pltpu.VMEM(routes.shape, routes.dtype),
            pltpu.VMEM(numerators.shape, numerators.dtype),
            pltpu.SemaphoreType.DMA((3,)),
        ],
        compiler_params=pltpu.CompilerParams(vmem_limit_bytes=4 << 20),
        cost_estimate=pl.CostEstimate(flops=20 * 10**9, bytes_accessed=4 * tokens.size, transcendentals=0),
    )(in_hbm(tokens), in_hbm(routes), in_hbm(numerators))


def gate_up_kernel(x, base, out, weights, sems):
    depth, _, columns = weights.shape
    step = depth // sems.shape[0]
    copies = [
        pltpu.make_async_copy(base.at[pl.ds(k, step)], weights.at[pl.ds(k, step)], sems.at[k // step])
        for k in range(0, depth, step)
    ]
    for copy in copies:
        copy.start()
    row = lax.broadcasted_iota(jnp.int32, (128, 256), 0)
    column = lax.broadcasted_iota(jnp.int32, (128, 256), 1)
    spread = jnp.where(column // 2 == row, 1.0, 0.0).astype(jnp.bfloat16)
    is_odd = (lax.broadcasted_iota(jnp.int32, (1, 2 * step), 1) % 2).astype(jnp.float32)
    odd_mask, even_mask = is_odd.astype(jnp.bfloat16), (1.0 - is_odd).astype(jnp.bfloat16)
    count = x.shape[0]
    flat = weights.reshape(2 * depth, columns)
    total = jnp.zeros(out.shape, jnp.float32)
    for k in range(0, depth, step):
        stacked = jnp.concatenate([x[:, i : i + 128] for i in range(k, k + step, 128)])
        wide = jnp.dot(stacked, spread, preferred_element_type=jnp.float32).astype(jnp.bfloat16)
        wide = jnp.concatenate([wide[i : i + count] for i in range(0, stacked.shape[0], count)], axis=1)
        copies[k // step].wait()
        total += jnp.dot(
            jnp.concatenate([wide * even_mask, wide * odd_mask]), flat[2 * k : 2 * (k + step), :], preferred_element_type=jnp.float32
        )
    out[...] = total


def gate_up_product(x, base):
    depth, _, columns = base.shape
    return pl.pallas_call(
        gate_up_kernel,
        out_shape=jax.ShapeDtypeStruct((2 * x.shape[0], columns), jnp.float32),
        in_specs=[VMEM, HBM],
        out_specs=VMEM,
        scratch_shapes=[pltpu.VMEM(base.shape, base.dtype), pltpu.SemaphoreType.DMA((depth // 512,))],
        compiler_params=pltpu.CompilerParams(vmem_limit_bytes=32 << 20),
        cost_estimate=pl.CostEstimate(
            flops=4 * x.shape[0] * depth * columns, bytes_accessed=2 * base.size, transcendentals=0
        ),
    )(x, in_hbm(base))


def part_kernel(bit, term, received, *refs):
    *outs, total = refs
    half, width = total.shape
    size, step = half // 4, width // (len(outs) // 2)
    me = lax.axis_index("tensor")
    core, flag = me % 2, (me // (2 * bit)) % 2
    total[...] = term[pl.ds(pl.multiple_of(core * half, half), half), :].astype(jnp.float32) + received[
        ...
    ].astype(jnp.float32)
    by_x = 1 - core
    sent = (core + by_x * 2 * (1 - flag), 3 - by_x * 2 * flag)
    kept = (by_x * 2 * flag, 2 * core + by_x * (2 * flag + 1))
    for i, out in enumerate(outs):
        columns = pl.ds((i // 2) * step, step)
        rows = [
            total[pl.ds(pl.multiple_of(block * size, size), size), columns] for block in (sent, kept)[i % 2]
        ]
        out[...] = jnp.concatenate(rows).astype(out.dtype)


def add_and_part(term, received, bit):
    half, width = received.shape
    outs = pl.pallas_call(
        functools.partial(part_kernel, bit),
        out_shape=[jax.ShapeDtypeStruct((half // 2, width // CHUNKS), term.dtype)] * (2 * CHUNKS),
        in_specs=[VMEM, VMEM],
        out_specs=[VMEM] * (2 * CHUNKS),
        scratch_shapes=[pltpu.VMEM((half, width), jnp.float32)],
        compiler_params=pltpu.CompilerParams(vmem_limit_bytes=16 << 20),
        cost_estimate=pl.CostEstimate(flops=0, bytes_accessed=6 * received.size, transcendentals=0),
    )(term, received)
    return list(zip(outs[::2], outs[1::2]))


def local(
    tokens,
    routes,
    numerators,
    place,
    base_in,
    base_down,
    delta_in,
    delta_mid,
    delta_down,
    delta_back,
):
    clusters = lax.axis_size("expert")
    members = lax.axis_size("tensor")
    me = lax.axis_index("tensor")
    cluster = lax.axis_index("expert")
    core = me % 2
    count, width = tokens.shape[1:]
    top = routes.shape[2]

    along, across = halves(clusters), halves(members // 2)
    shared, paired = along[: len(along) - len(across)], along[len(along) - len(across) :]

    packed = pack(tokens[0], routes[0], numerators[0])
    chips = members // 2
    pieces = {(0, 0): packed}
    for z in range(clusters - 1, 0, -1):
        pieces[0, z] = trade(packed, (z, 0), (z, 0))
    for x in range(1, chips):
        pieces[x, 0] = trade(packed, (0, 2 * x), (0, 2 * x))
    places = [(0, 0)]
    for mask in shared:
        places += [(x, z | mask) for x, z in places]
    for zbit, xbit in zip(paired, across):
        places += [(x, z | zbit) for x, z in places]
        places += [(x | xbit, z) for x, z in places]
    later = [z for x, z in places if x == 0 and z]
    rest = jnp.concatenate([pieces[0, z] for z in later])
    rest, *firsts = lax.optimization_barrier((rest, *(pieces[x, 0] for x in range(1, chips))))
    pieces.update({(x, 0): first for x, first in enumerate(firsts, 1)})
    for x in range(chips):
        received = trade(rest, (0, 2 * x), (0, 2 * x)) if x else rest
        for i, z in enumerate(later):
            pieces[x, z] = received[i * count : (i + 1) * count]
    segments = [(x, tuple(z for _, z in run)) for x, run in itertools.groupby(places, lambda place: place[0])]
    runs = {(x, zs): jnp.concatenate([pieces[x, z] for z in zs]) for x, zs in segments}
    for bit in across:
        flag = (me // (2 * bit)) % 2 == 1
        for x, zs in runs:
            if not x & bit:
                runs[x, zs], runs[x | bit, zs] = ordered(flag, runs[x, zs], runs[x | bit, zs])
    held = by_rows(jnp.concatenate([runs[segment] for segment in segments]))
    held = by_rows(jnp.concatenate(ordered(core == 1, held, trade(held, (0, 1), (0, 1)))))
    rows, code_table = lax.optimization_barrier((held, delta_in[0]))

    codes = jnp.dot(rows[:, :width], code_table, preferred_element_type=jnp.float32).astype(jnp.bfloat16)
    projected = gate_up_product(held, base_in[0])

    side = by_rows(rows[:, width:])
    all_routes = side[:, :top].astype(jnp.int32)
    numerator = side[:, top : 2 * top].astype(jnp.float32)
    position = lookup(place, all_routes)
    weight = (2.5 * numerator / jnp.sum(numerator, axis=-1, keepdims=True)).astype(jnp.bfloat16)
    target = cluster * members + jnp.arange(members, dtype=jnp.int32)
    scale = jnp.sum(
        jnp.where(position[None] == target[:, None, None], weight[None].astype(jnp.float32), 0.0), axis=-1
    )

    codes = jnp.stack([codes if m == 0 else trade(codes, (0, m), (0, m)) for m in range(members)])
    by_slot = jnp.stack([lax.dynamic_index_in_dim(codes, s ^ me, 0, keepdims=False) for s in range(members)])

    lifted = jnp.einsum("srk,skgf->srgf", by_slot, delta_mid[0], preferred_element_type=jnp.float32)
    total = held.shape[0]
    hidden = jax.nn.silu(projected[None, :total] + lifted[:, :, 0]) * (projected[None, total:] + lifted[:, :, 1])
    hidden_sum = jnp.sum(scale[:, :, None] * hidden, axis=0).astype(jnp.bfloat16)
    partial_codes = jnp.einsum(
        "srf,sfk->srk", hidden.astype(jnp.bfloat16), delta_down[0], preferred_element_type=jnp.float32
    ).astype(jnp.bfloat16)
    by_core = partial_codes.reshape(chips, 2, *partial_codes.shape[1:])
    kept, sent = (lax.dynamic_index_in_dim(by_core, c, 1, keepdims=False) for c in (core, 1 - core))
    by_chip = add(kept, trade(sent, (0, 1), (0, 1)))
    chip = me // 2
    lowrank = lax.dynamic_index_in_dim(by_chip, chip, 0, keepdims=False).astype(jnp.float32)
    for m in range(1, chips):
        sent = lax.dynamic_index_in_dim(by_chip, chip ^ m, 0, keepdims=False)
        lowrank = lowrank + trade(sent, (0, 2 * m), (0, 2 * m)).astype(jnp.float32)
    own_scale = lax.dynamic_index_in_dim(scale, me, 0, keepdims=False)
    scaled = (own_scale[:, None] * lowrank).astype(jnp.bfloat16)

    term = jnp.dot(hidden_sum, base_down[0], preferred_element_type=jnp.float32)
    term = (term + jnp.dot(scaled, delta_back[0], preferred_element_type=jnp.float32)).astype(jnp.bfloat16)

    half = term.shape[0] // 2
    sent = ordered(core == 1, term[half:], term[:half])[0]
    outputs = []
    for sent, kept in add_and_part(term, trade(sent, (0, 1), (0, 1)), across[-1]):
        for i, (z, x) in enumerate(reversed(list(zip(paired, across)))):
            flag = (me // (2 * x)) % 2 == 1
            if i:
                size = total.shape[0] // 4
                blocks = [total[j * size : (j + 1) * size] for j in range(4)]
                inner = ordered(core == 1, blocks[1], blocks[2])
                kept, sent = ordered(
                    (core == 0) & flag,
                    jnp.concatenate([blocks[0], inner[0]]),
                    jnp.concatenate([inner[1], blocks[3]]),
                )
            total = add(kept, trade(sent, (0, 2 * x), (z, 0)))
            size = total.shape[0] // 2
            kept, sent = ordered((core == 1) & flag, total[:size], total[size:])
            total = add(kept, trade(sent, (z, 0), (0, 2 * x)))
        for mask in reversed(shared):
            size = total.shape[0] // 2
            total = add(total[:size], trade(total[size:], (mask, 0), (mask, 0)))
        outputs.append(total)
    return jnp.concatenate(outputs, axis=1)[None]


def solution(mesh):
    placed = (
        P(None, ("parts", "expert", "tensor"), None),
        P(None, ("parts", "expert", "tensor"), None),
        P(None, ("parts", "expert", "tensor"), None),
        P("parts"),
        P("expert", None, None, "tensor"),
        P("expert", "tensor", None),
        P(("expert", "tensor"), None, None),
        P("expert", None, None, None, "tensor"),
        P("expert", None, "tensor", None),
        P(("expert", "tensor"), None, None),
    )
    return jax.shard_map(
        local,
        mesh=mesh,
        in_specs=placed,
        out_specs=P(None, ("parts", "expert", "tensor"), None),
        check_vma=False,
    )
```

```python
import functools
import itertools

import jax
import jax.numpy as jnp
from jax import lax
from jax.experimental import pallas as pl
from jax.experimental.pallas import tpu as pltpu
from jax.experimental.layout import Layout, with_layout_constraint
from jax.sharding import PartitionSpec as P

CHUNKS = 2
VMEM = pl.BlockSpec(memory_space=pltpu.VMEM)
HBM = pl.BlockSpec(memory_space=pltpu.HBM)


def in_hbm(value):
    return pltpu.with_memory_space_constraint(value, pltpu.HBM)


def by_rows(value):
    return with_layout_constraint(value, Layout((0, 1)))


def lookup(table, index):
    keys = jnp.arange(table.shape[0], dtype=jnp.int32)
    return jnp.sum(jnp.where(index[..., None] == keys, table, 0), axis=-1)


def trade(value, even, odd):
    members = lax.axis_size("tensor")
    pairs = []
    for e in range(lax.axis_size("expert")):
        for t in range(members):
            along, across = odd if t % 2 else even
            pairs.append((e * members + t, (e ^ along) * members + (t ^ across)))
    return lax.ppermute(value, ("expert", "tensor"), pairs)


def halves(size):
    masks = []
    while size > 1:
        size //= 2
        masks.append(size)
    return masks


def ordered(flip, first, second):
    return jnp.where(flip, second, first), jnp.where(flip, first, second)


def add(kept, received):
    return (kept.astype(jnp.float32) + received.astype(jnp.float32)).astype(jnp.bfloat16)


def pack_kernel(tokens, routes, numerators, packed, routes_in, numerators_in, sems):
    width, top = tokens.shape[1], routes.shape[1]
    copies = [
        pltpu.make_async_copy(tokens, packed.at[:, pl.ds(0, width)], sems.at[0]),
        pltpu.make_async_copy(routes, routes_in, sems.at[1]),
        pltpu.make_async_copy(numerators, numerators_in, sems.at[2]),
    ]
    for copy in copies:
        copy.start()
    packed[:, width:] = jnp.zeros((packed.shape[0], packed.shape[1] - width), packed.dtype)
    for copy in copies[1:]:
        copy.wait()
    packed[:, width : width + top] = routes_in[...].astype(jnp.float32).astype(packed.dtype)
    packed[:, width + top : width + 2 * top] = numerators_in[...].astype(jnp.float32).astype(packed.dtype)
    copies[0].wait()


def pack(tokens, routes, numerators):
    count, width = tokens.shape
    return pl.pallas_call(
        pack_kernel,
        out_shape=jax.ShapeDtypeStruct((count, width + 128), tokens.dtype),
        in_specs=[HBM] * 3,
        out_specs=VMEM,
        scratch_shapes=[
            pltpu.VMEM(routes.shape, routes.dtype),
            pltpu.VMEM(numerators.shape, numerators.dtype),
            pltpu.SemaphoreType.DMA((3,)),
        ],
        compiler_params=pltpu.CompilerParams(vmem_limit_bytes=4 << 20),
        cost_estimate=pl.CostEstimate(flops=20 * 10**9, bytes_accessed=4 * tokens.size, transcendentals=0),
    )(in_hbm(tokens), in_hbm(routes), in_hbm(numerators))


def gate_up_kernel(x, base, out):
    depth, _, columns = base.shape
    step = 512
    row = lax.broadcasted_iota(jnp.int32, (128, 256), 0)
    column = lax.broadcasted_iota(jnp.int32, (128, 256), 1)
    spread = jnp.where(column // 2 == row, 1.0, 0.0).astype(jnp.bfloat16)
    is_odd = (lax.broadcasted_iota(jnp.int32, (1, 2 * step), 1) % 2).astype(jnp.float32)
    odd_mask, even_mask = is_odd.astype(jnp.bfloat16), (1.0 - is_odd).astype(jnp.bfloat16)
    count = x.shape[0]
    flat = base.reshape(2 * depth, columns)
    total = jnp.zeros(out.shape, jnp.float32)
    for k in range(0, depth, step):
        stacked = jnp.concatenate([x[:, i : i + 128] for i in range(k, k + step, 128)])
        wide = jnp.dot(stacked, spread, preferred_element_type=jnp.float32).astype(jnp.bfloat16)
        wide = jnp.concatenate([wide[i : i + count] for i in range(0, stacked.shape[0], count)], axis=1)
        total += jnp.dot(
            jnp.concatenate([wide * even_mask, wide * odd_mask]),
            flat[2 * k : 2 * (k + step), :],
            preferred_element_type=jnp.float32,
        )
    out[...] = total


def gate_up_product(x, base):
    depth, _, columns = base.shape
    return pl.pallas_call(
        gate_up_kernel,
        out_shape=jax.ShapeDtypeStruct((2 * x.shape[0], columns), jnp.float32),
        in_specs=[VMEM, VMEM],
        out_specs=VMEM,
        compiler_params=pltpu.CompilerParams(vmem_limit_bytes=16 << 20),
        cost_estimate=pl.CostEstimate(
            flops=4 * x.shape[0] * depth * columns, bytes_accessed=2 * base.size, transcendentals=0
        ),
    )(x, base)


def part_kernel(bit, term, received, *refs):
    *outs, total = refs
    half, width = total.shape
    size, step = half // 4, width // (len(outs) // 2)
    me = lax.axis_index("tensor")
    core, flag = me % 2, (me // (2 * bit)) % 2
    total[...] = term[pl.ds(pl.multiple_of(core * half, half), half), :].astype(jnp.float32) + received[
        ...
    ].astype(jnp.float32)
    by_x = 1 - core
    sent = (core + by_x * 2 * (1 - flag), 3 - by_x * 2 * flag)
    kept = (by_x * 2 * flag, 2 * core + by_x * (2 * flag + 1))
    for i, out in enumerate(outs):
        columns = pl.ds((i // 2) * step, step)
        rows = [
            total[pl.ds(pl.multiple_of(block * size, size), size), columns] for block in (sent, kept)[i % 2]
        ]
        out[...] = jnp.concatenate(rows).astype(out.dtype)


def add_and_part(term, received, bit):
    half, width = received.shape
    outs = pl.pallas_call(
        functools.partial(part_kernel, bit),
        out_shape=[jax.ShapeDtypeStruct((half // 2, width // CHUNKS), term.dtype)] * (2 * CHUNKS),
        in_specs=[VMEM, VMEM],
        out_specs=[VMEM] * (2 * CHUNKS),
        scratch_shapes=[pltpu.VMEM((half, width), jnp.float32)],
        compiler_params=pltpu.CompilerParams(vmem_limit_bytes=16 << 20),
        cost_estimate=pl.CostEstimate(flops=0, bytes_accessed=6 * received.size, transcendentals=0),
    )(term, received)
    return list(zip(outs[::2], outs[1::2]))


def local(
    tokens,
    routes,
    numerators,
    place,
    base_in,
    base_down,
    delta_in,
    delta_mid,
    delta_down,
    delta_back,
):
    clusters = lax.axis_size("expert")
    members = lax.axis_size("tensor")
    me = lax.axis_index("tensor")
    cluster = lax.axis_index("expert")
    core = me % 2
    count, width = tokens.shape[1:]
    top = routes.shape[2]

    along, across = halves(clusters), halves(members // 2)
    shared, paired = along[: len(along) - len(across)], along[len(along) - len(across) :]

    packed = pack(tokens[0], routes[0], numerators[0])
    chips = members // 2
    pieces = {(0, 0): packed}
    for z in range(clusters - 1, 0, -1):
        pieces[0, z] = trade(packed, (z, 0), (z, 0))
    for x in range(1, chips):
        pieces[x, 0] = trade(packed, (0, 2 * x), (0, 2 * x))
    places = [(0, 0)]
    for mask in shared:
        places += [(x, z | mask) for x, z in places]
    for zbit, xbit in zip(paired, across):
        places += [(x, z | zbit) for x, z in places]
        places += [(x | xbit, z) for x, z in places]
    later = [z for x, z in places if x == 0 and z]
    rest = jnp.concatenate([pieces[0, z] for z in later])
    rest, *firsts = lax.optimization_barrier((rest, *(pieces[x, 0] for x in range(1, chips))))
    pieces.update({(x, 0): first for x, first in enumerate(firsts, 1)})
    for x in range(chips):
        received = trade(rest, (0, 2 * x), (0, 2 * x)) if x else rest
        for i, z in enumerate(later):
            pieces[x, z] = received[i * count : (i + 1) * count]
    segments = [(x, tuple(z for _, z in run)) for x, run in itertools.groupby(places, lambda place: place[0])]
    runs = {(x, zs): jnp.concatenate([pieces[x, z] for z in zs]) for x, zs in segments}
    for bit in across:
        flag = (me // (2 * bit)) % 2 == 1
        for x, zs in runs:
            if not x & bit:
                runs[x, zs], runs[x | bit, zs] = ordered(flag, runs[x, zs], runs[x | bit, zs])
    held = by_rows(jnp.concatenate([runs[segment] for segment in segments]))
    held = by_rows(jnp.concatenate(ordered(core == 1, held, trade(held, (0, 1), (0, 1)))))
    _, code_table = lax.optimization_barrier((held, delta_in[0]))

    codes = jnp.dot(held[:, :width], code_table, preferred_element_type=jnp.float32).astype(jnp.bfloat16)
    projected = gate_up_product(held, base_in[0])

    side = by_rows(held[:, width:])
    all_routes = side[:, :top].astype(jnp.int32)
    numerator = side[:, top : 2 * top].astype(jnp.float32)
    position = lookup(place, all_routes)
    weight = (2.5 * numerator / jnp.sum(numerator, axis=-1, keepdims=True)).astype(jnp.bfloat16)
    target = cluster * members + jnp.arange(members, dtype=jnp.int32)
    scale = jnp.sum(
        jnp.where(position[None] == target[:, None, None], weight[None].astype(jnp.float32), 0.0), axis=-1
    )

    codes = jnp.stack([codes if m == 0 else trade(codes, (0, m), (0, m)) for m in range(members)])
    by_slot = jnp.stack([lax.dynamic_index_in_dim(codes, s ^ me, 0, keepdims=False) for s in range(members)])

    lifted = jnp.einsum("srk,skgf->srgf", by_slot, delta_mid[0], preferred_element_type=jnp.float32)
    total = held.shape[0]
    hidden = jax.nn.silu(projected[None, :total] + lifted[:, :, 0]) * (projected[None, total:] + lifted[:, :, 1])
    hidden_sum = jnp.sum(scale[:, :, None] * hidden, axis=0).astype(jnp.bfloat16)
    partial_codes = jnp.einsum(
        "srf,sfk->srk", hidden.astype(jnp.bfloat16), delta_down[0], preferred_element_type=jnp.float32
    ).astype(jnp.bfloat16)
    by_core = partial_codes.reshape(chips, 2, *partial_codes.shape[1:])
    kept, sent = (lax.dynamic_index_in_dim(by_core, c, 1, keepdims=False) for c in (core, 1 - core))
    by_chip = add(kept, trade(sent, (0, 1), (0, 1)))
    chip = me // 2
    lowrank = lax.dynamic_index_in_dim(by_chip, chip, 0, keepdims=False).astype(jnp.float32)
    for m in range(1, chips):
        sent = lax.dynamic_index_in_dim(by_chip, chip ^ m, 0, keepdims=False)
        lowrank = lowrank + trade(sent, (0, 2 * m), (0, 2 * m)).astype(jnp.float32)
    own_scale = lax.dynamic_index_in_dim(scale, me, 0, keepdims=False)
    scaled = (own_scale[:, None] * lowrank).astype(jnp.bfloat16)

    term = jnp.dot(hidden_sum, base_down[0], preferred_element_type=jnp.float32)
    term = (term + jnp.dot(scaled, delta_back[0], preferred_element_type=jnp.float32)).astype(jnp.bfloat16)

    half = term.shape[0] // 2
    sent = ordered(core == 1, term[half:], term[:half])[0]
    outputs = []
    for sent, kept in add_and_part(term, trade(sent, (0, 1), (0, 1)), across[-1]):
        for i, (z, x) in enumerate(reversed(list(zip(paired, across)))):
            flag = (me // (2 * x)) % 2 == 1
            if i:
                size = total.shape[0] // 4
                blocks = [total[j * size : (j + 1) * size] for j in range(4)]
                inner = ordered(core == 1, blocks[1], blocks[2])
                kept, sent = ordered(
                    (core == 0) & flag,
                    jnp.concatenate([blocks[0], inner[0]]),
                    jnp.concatenate([inner[1], blocks[3]]),
                )
            total = add(kept, trade(sent, (0, 2 * x), (z, 0)))
            size = total.shape[0] // 2
            kept, sent = ordered((core == 1) & flag, total[:size], total[size:])
            total = add(kept, trade(sent, (z, 0), (0, 2 * x)))
        for mask in reversed(shared):
            size = total.shape[0] // 2
            total = add(total[:size], trade(total[size:], (mask, 0), (mask, 0)))
        outputs.append(total)
    return jnp.concatenate(outputs, axis=1)[None]


def solution(mesh):
    placed = (
        P(None, ("parts", "expert", "tensor"), None),
        P(None, ("parts", "expert", "tensor"), None),
        P(None, ("parts", "expert", "tensor"), None),
        P("parts"),
        P("expert", None, None, "tensor"),
        P("expert", "tensor", None),
        P(("expert", "tensor"), None, None),
        P("expert", None, None, None, "tensor"),
        P("expert", None, "tensor", None),
        P(("expert", "tensor"), None, None),
    )
    return jax.shard_map(
        local,
        mesh=mesh,
        in_specs=placed,
        out_specs=P(None, ("parts", "expert", "tensor"), None),
        check_vma=False,
    )
```

```python
import functools
import itertools

import jax
import jax.numpy as jnp
from jax import lax
from jax.experimental import pallas as pl
from jax.experimental.pallas import tpu as pltpu
from jax.experimental.layout import Layout, with_layout_constraint
from jax.sharding import PartitionSpec as P

CHUNKS = 2
VMEM = pl.BlockSpec(memory_space=pltpu.VMEM)
HBM = pl.BlockSpec(memory_space=pltpu.HBM)


def in_hbm(value):
    return pltpu.with_memory_space_constraint(value, pltpu.HBM)


def by_rows(value):
    return with_layout_constraint(value, Layout((0, 1)))


def lookup(table, index):
    keys = jnp.arange(table.shape[0], dtype=jnp.int32)
    return jnp.sum(jnp.where(index[..., None] == keys, table, 0), axis=-1)


def trade(value, even, odd):
    members = lax.axis_size("tensor")
    pairs = []
    for e in range(lax.axis_size("expert")):
        for t in range(members):
            along, across = odd if t % 2 else even
            pairs.append((e * members + t, (e ^ along) * members + (t ^ across)))
    return lax.ppermute(value, ("expert", "tensor"), pairs)


def halves(size):
    masks = []
    while size > 1:
        size //= 2
        masks.append(size)
    return masks


def ordered(flip, first, second):
    return jnp.where(flip, second, first), jnp.where(flip, first, second)


def add(kept, received):
    return (kept.astype(jnp.float32) + received.astype(jnp.float32)).astype(jnp.bfloat16)


def pack_kernel(tokens, routes, numerators, packed, routes_in, numerators_in, sems):
    width, top = tokens.shape[1], routes.shape[1]
    copies = [
        pltpu.make_async_copy(tokens, packed.at[:, pl.ds(0, width)], sems.at[0]),
        pltpu.make_async_copy(routes, routes_in, sems.at[1]),
        pltpu.make_async_copy(numerators, numerators_in, sems.at[2]),
    ]
    for copy in copies:
        copy.start()
    packed[:, width:] = jnp.zeros((packed.shape[0], packed.shape[1] - width), packed.dtype)
    for copy in copies[1:]:
        copy.wait()
    packed[:, width : width + top] = routes_in[...].astype(jnp.float32).astype(packed.dtype)
    packed[:, width + top : width + 2 * top] = numerators_in[...].astype(jnp.float32).astype(packed.dtype)
    copies[0].wait()


def pack(tokens, routes, numerators):
    count, width = tokens.shape
    return pl.pallas_call(
        pack_kernel,
        out_shape=jax.ShapeDtypeStruct((count, width + 128), tokens.dtype),
        in_specs=[HBM] * 3,
        out_specs=VMEM,
        scratch_shapes=[
            pltpu.VMEM(routes.shape, routes.dtype),
            pltpu.VMEM(numerators.shape, numerators.dtype),
            pltpu.SemaphoreType.DMA((3,)),
        ],
        compiler_params=pltpu.CompilerParams(vmem_limit_bytes=4 << 20),
        cost_estimate=pl.CostEstimate(flops=20 * 10**9, bytes_accessed=4 * tokens.size, transcendentals=0),
    )(in_hbm(tokens), in_hbm(routes), in_hbm(numerators))


def gate_up_kernel(x, base, out, weights, sems):
    depth, _, columns = weights.shape
    step = depth // sems.shape[0]
    copies = [
        pltpu.make_async_copy(base.at[pl.ds(k, step)], weights.at[pl.ds(k, step)], sems.at[k // step])
        for k in range(0, depth, step)
    ]
    for copy in copies:
        copy.start()
    row = lax.broadcasted_iota(jnp.int32, (128, 256), 0)
    column = lax.broadcasted_iota(jnp.int32, (128, 256), 1)
    spread = jnp.where(column // 2 == row, 1.0, 0.0).astype(jnp.bfloat16)
    is_odd = (lax.broadcasted_iota(jnp.int32, (1, 2 * step), 1) % 2).astype(jnp.float32)
    odd_mask, even_mask = is_odd.astype(jnp.bfloat16), (1.0 - is_odd).astype(jnp.bfloat16)
    count = x.shape[0]
    flat = weights.reshape(2 * depth, columns)
    total = jnp.zeros(out.shape, jnp.float32)
    for k in range(0, depth, step):
        stacked = jnp.concatenate([x[:, i : i + 128] for i in range(k, k + step, 128)])
        wide = jnp.dot(stacked, spread, preferred_element_type=jnp.float32).astype(jnp.bfloat16)
        wide = jnp.concatenate([wide[i : i + count] for i in range(0, stacked.shape[0], count)], axis=1)
        copies[k // step].wait()
        total += jnp.dot(
            jnp.concatenate([wide * even_mask, wide * odd_mask]), flat[2 * k : 2 * (k + step), :], preferred_element_type=jnp.float32
        )
    out[...] = total


def gate_up_product(x, base):
    depth, _, columns = base.shape
    return pl.pallas_call(
        gate_up_kernel,
        out_shape=jax.ShapeDtypeStruct((2 * x.shape[0], columns), jnp.float32),
        in_specs=[VMEM, HBM],
        out_specs=VMEM,
        scratch_shapes=[pltpu.VMEM(base.shape, base.dtype), pltpu.SemaphoreType.DMA((depth // 512,))],
        compiler_params=pltpu.CompilerParams(vmem_limit_bytes=32 << 20),
        cost_estimate=pl.CostEstimate(
            flops=4 * x.shape[0] * depth * columns, bytes_accessed=2 * base.size, transcendentals=0
        ),
    )(x, in_hbm(base))


def down_kernel(hidden, base, out, weights, sems):
    step = base.shape[1] // sems.shape[0]
    parts = [pl.ds(k * step, step) for k in range(sems.shape[0])]
    copies = [pltpu.make_async_copy(base.at[:, part], weights.at[:, part], sems.at[k]) for k, part in enumerate(parts)]
    for copy in copies:
        copy.start()
    for copy, part in zip(copies, parts):
        copy.wait()
        out[:, part] = jnp.dot(hidden[...], weights[:, part], preferred_element_type=jnp.float32)


def down_product(hidden, base):
    rows, width = hidden.shape[0], base.shape[1]
    return pl.pallas_call(
        down_kernel,
        out_shape=jax.ShapeDtypeStruct((rows, width), jnp.float32),
        in_specs=[VMEM, HBM],
        out_specs=VMEM,
        scratch_shapes=[pltpu.VMEM(base.shape, base.dtype), pltpu.SemaphoreType.DMA((width // 1024,))],
        compiler_params=pltpu.CompilerParams(vmem_limit_bytes=16 << 20),
        cost_estimate=pl.CostEstimate(flops=2 * rows * base.size, bytes_accessed=2 * base.size, transcendentals=0),
    )(hidden, in_hbm(base))


def part_kernel(bit, term, received, *refs):
    *outs, total = refs
    half = total.shape[0]
    size = half // 4
    me = lax.axis_index("tensor")
    core, flag = me % 2, (me // (2 * bit)) % 2
    total[...] = term[pl.ds(pl.multiple_of(core * half, half), half), :].astype(jnp.float32) + received[
        ...
    ].astype(jnp.float32)
    by_x = 1 - core
    sent = (core + by_x * 2 * (1 - flag), 3 - by_x * 2 * flag)
    kept = (by_x * 2 * flag, 2 * core + by_x * (2 * flag + 1))
    for blocks, out in zip((sent, kept), outs):
        rows = [total[pl.ds(pl.multiple_of(block * size, size), size), :] for block in blocks]
        out[...] = jnp.concatenate(rows).astype(out.dtype)


def add_and_part(term, received, bit):
    half, width = received.shape
    return pl.pallas_call(
        functools.partial(part_kernel, bit),
        out_shape=[jax.ShapeDtypeStruct((half // 2, width), term.dtype)] * 2,
        in_specs=[VMEM, VMEM],
        out_specs=[VMEM] * 2,
        scratch_shapes=[pltpu.VMEM((half, width), jnp.float32)],
        compiler_params=pltpu.CompilerParams(vmem_limit_bytes=16 << 20),
        cost_estimate=pl.CostEstimate(flops=0, bytes_accessed=6 * received.size, transcendentals=0),
    )(term, received)


def local(
    tokens,
    routes,
    numerators,
    place,
    base_in,
    base_down,
    delta_in,
    delta_mid,
    delta_down,
    delta_back,
):
    clusters = lax.axis_size("expert")
    members = lax.axis_size("tensor")
    me = lax.axis_index("tensor")
    cluster = lax.axis_index("expert")
    core = me % 2
    count, width = tokens.shape[1:]
    top = routes.shape[2]

    along, across = halves(clusters), halves(members // 2)
    shared, paired = along[: len(along) - len(across)], along[len(along) - len(across) :]

    packed = pack(tokens[0], routes[0], numerators[0])
    chips = members // 2
    pieces = {(0, 0): packed}
    for z in range(clusters - 1, 0, -1):
        pieces[0, z] = trade(packed, (z, 0), (z, 0))
    for x in range(1, chips):
        pieces[x, 0] = trade(packed, (0, 2 * x), (0, 2 * x))
    places = [(0, 0)]
    for mask in shared:
        places += [(x, z | mask) for x, z in places]
    for zbit, xbit in zip(paired, across):
        places += [(x, z | zbit) for x, z in places]
        places += [(x | xbit, z) for x, z in places]
    later = [z for x, z in places if x == 0 and z]
    rest = jnp.concatenate([pieces[0, z] for z in later])
    rest, *firsts = lax.optimization_barrier((rest, *(pieces[x, 0] for x in range(1, chips))))
    pieces.update({(x, 0): first for x, first in enumerate(firsts, 1)})
    for x in range(chips):
        received = trade(rest, (0, 2 * x), (0, 2 * x)) if x else rest
        for i, z in enumerate(later):
            pieces[x, z] = received[i * count : (i + 1) * count]
    segments = [(x, tuple(z for _, z in run)) for x, run in itertools.groupby(places, lambda place: place[0])]
    runs = {(x, zs): jnp.concatenate([pieces[x, z] for z in zs]) for x, zs in segments}
    for bit in across:
        flag = (me // (2 * bit)) % 2 == 1
        for x, zs in runs:
            if not x & bit:
                runs[x, zs], runs[x | bit, zs] = ordered(flag, runs[x, zs], runs[x | bit, zs])
    held = by_rows(jnp.concatenate([runs[segment] for segment in segments]))
    held = by_rows(jnp.concatenate(ordered(core == 1, held, trade(held, (0, 1), (0, 1)))))
    rows, code_table = lax.optimization_barrier((held, delta_in[0]))

    codes = jnp.dot(rows[:, :width], code_table, preferred_element_type=jnp.float32).astype(jnp.bfloat16)
    projected = gate_up_product(held, base_in[0])

    side = by_rows(rows[:, width:])
    all_routes = side[:, :top].astype(jnp.int32)
    numerator = side[:, top : 2 * top].astype(jnp.float32)
    position = lookup(place, all_routes)
    weight = (2.5 * numerator / jnp.sum(numerator, axis=-1, keepdims=True)).astype(jnp.bfloat16)
    target = cluster * members + jnp.arange(members, dtype=jnp.int32)
    scale = jnp.sum(
        jnp.where(position[None] == target[:, None, None], weight[None].astype(jnp.float32), 0.0), axis=-1
    )

    codes = jnp.stack([codes if m == 0 else trade(codes, (0, m), (0, m)) for m in range(members)])
    by_slot = jnp.stack([lax.dynamic_index_in_dim(codes, s ^ me, 0, keepdims=False) for s in range(members)])

    lifted = jnp.einsum("srk,skgf->srgf", by_slot, delta_mid[0], preferred_element_type=jnp.float32)
    total = held.shape[0]
    hidden = jax.nn.silu(projected[None, :total] + lifted[:, :, 0]) * (projected[None, total:] + lifted[:, :, 1])
    hidden_sum = jnp.sum(scale[:, :, None] * hidden, axis=0).astype(jnp.bfloat16)
    partial_codes = jnp.einsum(
        "srf,sfk->srk", hidden.astype(jnp.bfloat16), delta_down[0], preferred_element_type=jnp.float32
    ).astype(jnp.bfloat16)
    by_core = partial_codes.reshape(chips, 2, *partial_codes.shape[1:])
    kept, sent = (lax.dynamic_index_in_dim(by_core, c, 1, keepdims=False) for c in (core, 1 - core))
    by_chip = add(kept, trade(sent, (0, 1), (0, 1)))
    chip = me // 2
    lowrank = lax.dynamic_index_in_dim(by_chip, chip, 0, keepdims=False).astype(jnp.float32)
    for m in range(1, chips):
        sent = lax.dynamic_index_in_dim(by_chip, chip ^ m, 0, keepdims=False)
        lowrank = lowrank + trade(sent, (0, 2 * m), (0, 2 * m)).astype(jnp.float32)
    own_scale = lax.dynamic_index_in_dim(scale, me, 0, keepdims=False)
    scaled = (own_scale[:, None] * lowrank).astype(jnp.bfloat16)

    base = down_product(hidden_sum, base_down[0])

    half, step = base.shape[0] // 2, width // CHUNKS
    outputs = []
    for c in range(CHUNKS):
        columns = slice(c * step, (c + 1) * step)
        term = jnp.dot(scaled, delta_back[0, :, columns], preferred_element_type=jnp.float32)
        term = (base[:, columns] + term).astype(jnp.bfloat16)
        sent = ordered(core == 1, term[half:], term[:half])[0]
        sent, kept = add_and_part(term, trade(sent, (0, 1), (0, 1)), across[-1])
        for i, (z, x) in enumerate(reversed(list(zip(paired, across)))):
            flag = (me // (2 * x)) % 2 == 1
            if i:
                size = total.shape[0] // 4
                blocks = [total[j * size : (j + 1) * size] for j in range(4)]
                inner = ordered(core == 1, blocks[1], blocks[2])
                kept, sent = ordered(
                    (core == 0) & flag,
                    jnp.concatenate([blocks[0], inner[0]]),
                    jnp.concatenate([inner[1], blocks[3]]),
                )
            total = add(kept, trade(sent, (0, 2 * x), (z, 0)))
            size = total.shape[0] // 2
            kept, sent = ordered((core == 1) & flag, total[:size], total[size:])
            total = add(kept, trade(sent, (z, 0), (0, 2 * x)))
        for mask in reversed(shared):
            size = total.shape[0] // 2
            total = add(total[:size], trade(total[size:], (mask, 0), (mask, 0)))
        outputs.append(total)
    return jnp.concatenate(outputs, axis=1)[None]


def solution(mesh):
    placed = (
        P(None, ("parts", "expert", "tensor"), None),
        P(None, ("parts", "expert", "tensor"), None),
        P(None, ("parts", "expert", "tensor"), None),
        P("parts"),
        P("expert", None, None, "tensor"),
        P("expert", "tensor", None),
        P(("expert", "tensor"), None, None),
        P("expert", None, None, None, "tensor"),
        P("expert", None, "tensor", None),
        P(("expert", "tensor"), None, None),
    )
    return jax.shard_map(
        local,
        mesh=mesh,
        in_specs=placed,
        out_specs=P(None, ("parts", "expert", "tensor"), None),
        check_vma=False,
    )
```

```python
import functools
import itertools

import jax
import jax.numpy as jnp
from jax import lax
from jax.experimental import pallas as pl
from jax.experimental.pallas import tpu as pltpu
from jax.experimental.layout import Layout, with_layout_constraint
from jax.sharding import PartitionSpec as P

CHUNKS = 2
PIECES = (1, 2, 4, 4)
DOWN_PIECES = (1, 3)
VMEM = pl.BlockSpec(memory_space=pltpu.VMEM)
HBM = pl.BlockSpec(memory_space=pltpu.HBM)


def in_hbm(value):
    return pltpu.with_memory_space_constraint(value, pltpu.HBM)


def by_rows(value):
    return with_layout_constraint(value, Layout((0, 1)))


def lookup(table, index):
    keys = jnp.arange(table.shape[0], dtype=jnp.int32)
    return jnp.sum(jnp.where(index[..., None] == keys, table, 0), axis=-1)


def trade(value, even, odd):
    members = lax.axis_size("tensor")
    pairs = []
    for e in range(lax.axis_size("expert")):
        for t in range(members):
            along, across = odd if t % 2 else even
            pairs.append((e * members + t, (e ^ along) * members + (t ^ across)))
    return lax.ppermute(value, ("expert", "tensor"), pairs)


def halves(size):
    masks = []
    while size > 1:
        size //= 2
        masks.append(size)
    return masks


def ordered(flip, first, second):
    return jnp.where(flip, second, first), jnp.where(flip, first, second)


def add(kept, received):
    return (kept.astype(jnp.float32) + received.astype(jnp.float32)).astype(jnp.bfloat16)


def pack_kernel(tokens, routes, numerators, packed, routes_in, numerators_in, sems):
    width, top = tokens.shape[1], routes.shape[1]
    copies = [
        pltpu.make_async_copy(tokens, packed.at[:, pl.ds(0, width)], sems.at[0]),
        pltpu.make_async_copy(routes, routes_in, sems.at[1]),
        pltpu.make_async_copy(numerators, numerators_in, sems.at[2]),
    ]
    for copy in copies:
        copy.start()
    packed[:, width:] = jnp.zeros((packed.shape[0], packed.shape[1] - width), packed.dtype)
    for copy in copies[1:]:
        copy.wait()
    packed[:, width : width + top] = routes_in[...].astype(jnp.float32).astype(packed.dtype)
    packed[:, width + top : width + 2 * top] = numerators_in[...].astype(jnp.float32).astype(packed.dtype)
    copies[0].wait()


def pack(tokens, routes, numerators):
    count, width = tokens.shape
    return pl.pallas_call(
        pack_kernel,
        out_shape=jax.ShapeDtypeStruct((count, width + 128), tokens.dtype),
        in_specs=[HBM] * 3,
        out_specs=VMEM,
        scratch_shapes=[
            pltpu.VMEM(routes.shape, routes.dtype),
            pltpu.VMEM(numerators.shape, numerators.dtype),
            pltpu.SemaphoreType.DMA((3,)),
        ],
        compiler_params=pltpu.CompilerParams(vmem_limit_bytes=4 << 20),
        cost_estimate=pl.CostEstimate(flops=20 * 10**9, bytes_accessed=4 * tokens.size, transcendentals=0),
    )(in_hbm(tokens), in_hbm(routes), in_hbm(numerators))


def piece_bounds(size, step, pieces):
    ends = [0]
    for piece in pieces:
        ends.append(ends[-1] + piece * step)
    return list(zip(ends, [*ends[1:], size]))


def gate_up_kernel(x, base, out, weights, sems):
    depth, _, columns = weights.shape
    step = 512
    bounds = piece_bounds(depth, step, PIECES)
    copies = {
        low: pltpu.make_async_copy(base.at[pl.ds(low, high - low)], weights.at[pl.ds(low, high - low)], sems.at[i])
        for i, (low, high) in enumerate(bounds)
    }
    for copy in copies.values():
        copy.start()
    row = lax.broadcasted_iota(jnp.int32, (128, 256), 0)
    column = lax.broadcasted_iota(jnp.int32, (128, 256), 1)
    spread = jnp.where(column // 2 == row, 1.0, 0.0).astype(jnp.bfloat16)
    is_odd = (lax.broadcasted_iota(jnp.int32, (1, 2 * step), 1) % 2).astype(jnp.float32)
    odd_mask, even_mask = is_odd.astype(jnp.bfloat16), (1.0 - is_odd).astype(jnp.bfloat16)
    count = x.shape[0]
    flat = weights.reshape(2 * depth, columns)
    total = jnp.zeros(out.shape, jnp.float32)
    for k in range(0, depth, step):
        stacked = jnp.concatenate([x[:, i : i + 128] for i in range(k, k + step, 128)])
        wide = jnp.dot(stacked, spread, preferred_element_type=jnp.float32).astype(jnp.bfloat16)
        wide = jnp.concatenate([wide[i : i + count] for i in range(0, stacked.shape[0], count)], axis=1)
        if k in copies:
            copies[k].wait()
        total += jnp.dot(
            jnp.concatenate([wide * even_mask, wide * odd_mask]), flat[2 * k : 2 * (k + step), :], preferred_element_type=jnp.float32
        )
    out[...] = total


def gate_up_product(x, base):
    depth, _, columns = base.shape
    return pl.pallas_call(
        gate_up_kernel,
        out_shape=jax.ShapeDtypeStruct((2 * x.shape[0], columns), jnp.float32),
        in_specs=[VMEM, HBM],
        out_specs=VMEM,
        scratch_shapes=[pltpu.VMEM(base.shape, base.dtype), pltpu.SemaphoreType.DMA((len(PIECES) + 1,))],
        compiler_params=pltpu.CompilerParams(vmem_limit_bytes=32 << 20),
        cost_estimate=pl.CostEstimate(
            flops=4 * x.shape[0] * depth * columns, bytes_accessed=2 * base.size, transcendentals=0
        ),
    )(x, in_hbm(base))


def down_kernel(hidden, base, out, weights, sems):
    step = 1024
    copies = {
        low: pltpu.make_async_copy(
            base.at[:, pl.ds(low, high - low)], weights.at[:, pl.ds(low, high - low)], sems.at[i]
        )
        for i, (low, high) in enumerate(piece_bounds(base.shape[1], step, DOWN_PIECES))
    }
    for copy in copies.values():
        copy.start()
    for k in range(0, base.shape[1], step):
        if k in copies:
            copies[k].wait()
        part = pl.ds(k, step)
        out[:, part] = jnp.dot(hidden[...], weights[:, part], preferred_element_type=jnp.float32)


def down_product(hidden, base):
    rows, width = hidden.shape[0], base.shape[1]
    return pl.pallas_call(
        down_kernel,
        out_shape=jax.ShapeDtypeStruct((rows, width), jnp.float32),
        in_specs=[VMEM, HBM],
        out_specs=VMEM,
        scratch_shapes=[pltpu.VMEM(base.shape, base.dtype), pltpu.SemaphoreType.DMA((len(DOWN_PIECES) + 1,))],
        compiler_params=pltpu.CompilerParams(vmem_limit_bytes=16 << 20),
        cost_estimate=pl.CostEstimate(flops=2 * rows * base.size, bytes_accessed=2 * base.size, transcendentals=0),
    )(hidden, in_hbm(base))


def part_kernel(bit, term, received, *refs):
    *outs, total = refs
    half = total.shape[0]
    size = half // 4
    me = lax.axis_index("tensor")
    core, flag = me % 2, (me // (2 * bit)) % 2
    total[...] = term[pl.ds(pl.multiple_of(core * half, half), half), :].astype(jnp.float32) + received[
        ...
    ].astype(jnp.float32)
    by_x = 1 - core
    sent = (core + by_x * 2 * (1 - flag), 3 - by_x * 2 * flag)
    kept = (by_x * 2 * flag, 2 * core + by_x * (2 * flag + 1))
    for blocks, out in zip((sent, kept), outs):
        rows = [total[pl.ds(pl.multiple_of(block * size, size), size), :] for block in blocks]
        out[...] = jnp.concatenate(rows).astype(out.dtype)


def add_and_part(term, received, bit):
    half, width = received.shape
    return pl.pallas_call(
        functools.partial(part_kernel, bit),
        out_shape=[jax.ShapeDtypeStruct((half // 2, width), term.dtype)] * 2,
        in_specs=[VMEM, VMEM],
        out_specs=[VMEM] * 2,
        scratch_shapes=[pltpu.VMEM((half, width), jnp.float32)],
        compiler_params=pltpu.CompilerParams(vmem_limit_bytes=16 << 20),
        cost_estimate=pl.CostEstimate(flops=0, bytes_accessed=6 * received.size, transcendentals=0),
    )(term, received)


def local(
    tokens,
    routes,
    numerators,
    place,
    base_in,
    base_down,
    delta_in,
    delta_mid,
    delta_down,
    delta_back,
):
    clusters = lax.axis_size("expert")
    members = lax.axis_size("tensor")
    me = lax.axis_index("tensor")
    cluster = lax.axis_index("expert")
    core = me % 2
    count, width = tokens.shape[1:]
    top = routes.shape[2]

    along, across = halves(clusters), halves(members // 2)
    shared, paired = along[: len(along) - len(across)], along[len(along) - len(across) :]

    packed = pack(tokens[0], routes[0], numerators[0])
    chips = members // 2
    pieces = {(0, 0): packed}
    for z in range(clusters - 1, 0, -1):
        pieces[0, z] = trade(packed, (z, 0), (z, 0))
    for x in range(1, chips):
        pieces[x, 0] = trade(packed, (0, 2 * x), (0, 2 * x))
    places = [(0, 0)]
    for mask in shared:
        places += [(x, z | mask) for x, z in places]
    for zbit, xbit in zip(paired, across):
        places += [(x, z | zbit) for x, z in places]
        places += [(x | xbit, z) for x, z in places]
    later = [z for x, z in places if x == 0 and z]
    rest = jnp.concatenate([pieces[0, z] for z in later])
    rest, *firsts = lax.optimization_barrier((rest, *(pieces[x, 0] for x in range(1, chips))))
    pieces.update({(x, 0): first for x, first in enumerate(firsts, 1)})
    for x in range(chips):
        received = trade(rest, (0, 2 * x), (0, 2 * x)) if x else rest
        for i, z in enumerate(later):
            pieces[x, z] = received[i * count : (i + 1) * count]
    segments = [(x, tuple(z for _, z in run)) for x, run in itertools.groupby(places, lambda place: place[0])]
    runs = {(x, zs): jnp.concatenate([pieces[x, z] for z in zs]) for x, zs in segments}
    for bit in across:
        flag = (me // (2 * bit)) % 2 == 1
        for x, zs in runs:
            if not x & bit:
                runs[x, zs], runs[x | bit, zs] = ordered(flag, runs[x, zs], runs[x | bit, zs])
    held = by_rows(jnp.concatenate([runs[segment] for segment in segments]))
    held = by_rows(jnp.concatenate(ordered(core == 1, held, trade(held, (0, 1), (0, 1)))))
    rows, code_table = lax.optimization_barrier((held, delta_in[0]))

    codes = jnp.dot(rows[:, :width], code_table, preferred_element_type=jnp.float32).astype(jnp.bfloat16)
    projected = gate_up_product(held, base_in[0])

    side = by_rows(rows[:, width:])
    all_routes = side[:, :top].astype(jnp.int32)
    numerator = side[:, top : 2 * top].astype(jnp.float32)
    position = lookup(place, all_routes)
    weight = (2.5 * numerator / jnp.sum(numerator, axis=-1, keepdims=True)).astype(jnp.bfloat16)
    target = cluster * members + jnp.arange(members, dtype=jnp.int32)
    scale = jnp.sum(
        jnp.where(position[None] == target[:, None, None], weight[None].astype(jnp.float32), 0.0), axis=-1
    )

    codes = jnp.stack([codes if m == 0 else trade(codes, (0, m), (0, m)) for m in range(members)])
    by_slot = jnp.stack([lax.dynamic_index_in_dim(codes, s ^ me, 0, keepdims=False) for s in range(members)])

    lifted = jnp.einsum("srk,skgf->srgf", by_slot, delta_mid[0], preferred_element_type=jnp.float32)
    total = held.shape[0]
    hidden = jax.nn.silu(projected[None, :total] + lifted[:, :, 0]) * (projected[None, total:] + lifted[:, :, 1])
    hidden_sum = jnp.sum(scale[:, :, None] * hidden, axis=0).astype(jnp.bfloat16)
    partial_codes = jnp.einsum(
        "srf,sfk->srk", hidden.astype(jnp.bfloat16), delta_down[0], preferred_element_type=jnp.float32
    ).astype(jnp.bfloat16)
    by_core = partial_codes.reshape(chips, 2, *partial_codes.shape[1:])
    kept, sent = (lax.dynamic_index_in_dim(by_core, c, 1, keepdims=False) for c in (core, 1 - core))
    by_chip = add(kept, trade(sent, (0, 1), (0, 1)))
    chip = me // 2
    lowrank = lax.dynamic_index_in_dim(by_chip, chip, 0, keepdims=False).astype(jnp.float32)
    for m in range(1, chips):
        sent = lax.dynamic_index_in_dim(by_chip, chip ^ m, 0, keepdims=False)
        lowrank = lowrank + trade(sent, (0, 2 * m), (0, 2 * m)).astype(jnp.float32)
    own_scale = lax.dynamic_index_in_dim(scale, me, 0, keepdims=False)
    scaled = (own_scale[:, None] * lowrank).astype(jnp.bfloat16)

    base = down_product(hidden_sum, base_down[0])

    half, step = base.shape[0] // 2, width // CHUNKS
    outputs = []
    for c in range(CHUNKS):
        columns = slice(c * step, (c + 1) * step)
        term = jnp.dot(scaled, delta_back[0, :, columns], preferred_element_type=jnp.float32)
        term = (base[:, columns] + term).astype(jnp.bfloat16)
        sent = ordered(core == 1, term[half:], term[:half])[0]
        sent, kept = add_and_part(term, trade(sent, (0, 1), (0, 1)), across[-1])
        for i, (z, x) in enumerate(reversed(list(zip(paired, across)))):
            flag = (me // (2 * x)) % 2 == 1
            if i:
                size = total.shape[0] // 4
                blocks = [total[j * size : (j + 1) * size] for j in range(4)]
                inner = ordered(core == 1, blocks[1], blocks[2])
                kept, sent = ordered(
                    (core == 0) & flag,
                    jnp.concatenate([blocks[0], inner[0]]),
                    jnp.concatenate([inner[1], blocks[3]]),
                )
            total = add(kept, trade(sent, (0, 2 * x), (z, 0)))
            size = total.shape[0] // 2
            kept, sent = ordered((core == 1) & flag, total[:size], total[size:])
            total = add(kept, trade(sent, (z, 0), (0, 2 * x)))
        for mask in reversed(shared):
            size = total.shape[0] // 2
            total = add(total[:size], trade(total[size:], (mask, 0), (mask, 0)))
        outputs.append(total)
    return jnp.concatenate(outputs, axis=1)[None]


def solution(mesh):
    placed = (
        P(None, ("parts", "expert", "tensor"), None),
        P(None, ("parts", "expert", "tensor"), None),
        P(None, ("parts", "expert", "tensor"), None),
        P("parts"),
        P("expert", None, None, "tensor"),
        P("expert", "tensor", None),
        P(("expert", "tensor"), None, None),
        P("expert", None, None, None, "tensor"),
        P("expert", None, "tensor", None),
        P(("expert", "tensor"), None, None),
    )
    return jax.shard_map(
        local,
        mesh=mesh,
        in_specs=placed,
        out_specs=P(None, ("parts", "expert", "tensor"), None),
        check_vma=False,
    )
```

```python
import functools
import itertools

import jax
import jax.numpy as jnp
from jax import lax
from jax.experimental import pallas as pl
from jax.experimental.pallas import tpu as pltpu
from jax.experimental.layout import Layout, with_layout_constraint
from jax.sharding import PartitionSpec as P

CHUNKS = 2
PIECES = (1, 2, 4, 4)
VMEM = pl.BlockSpec(memory_space=pltpu.VMEM)
HBM = pl.BlockSpec(memory_space=pltpu.HBM)


def in_hbm(value):
    return pltpu.with_memory_space_constraint(value, pltpu.HBM)


def by_rows(value):
    return with_layout_constraint(value, Layout((0, 1)))


def lookup(table, index):
    keys = jnp.arange(table.shape[0], dtype=jnp.int32)
    return jnp.sum(jnp.where(index[..., None] == keys, table, 0), axis=-1)


def trade(value, even, odd):
    members = lax.axis_size("tensor")
    pairs = []
    for e in range(lax.axis_size("expert")):
        for t in range(members):
            along, across = odd if t % 2 else even
            pairs.append((e * members + t, (e ^ along) * members + (t ^ across)))
    return lax.ppermute(value, ("expert", "tensor"), pairs)


def halves(size):
    masks = []
    while size > 1:
        size //= 2
        masks.append(size)
    return masks


def ordered(flip, first, second):
    return jnp.where(flip, second, first), jnp.where(flip, first, second)


def add(kept, received):
    return (kept.astype(jnp.float32) + received.astype(jnp.float32)).astype(jnp.bfloat16)


def pack_kernel(tokens, routes, numerators, packed, routes_in, numerators_in, sems):
    width, top = tokens.shape[1], routes.shape[1]
    copies = [
        pltpu.make_async_copy(tokens, packed.at[:, pl.ds(0, width)], sems.at[0]),
        pltpu.make_async_copy(routes, routes_in, sems.at[1]),
        pltpu.make_async_copy(numerators, numerators_in, sems.at[2]),
    ]
    for copy in copies:
        copy.start()
    packed[:, width:] = jnp.zeros((packed.shape[0], packed.shape[1] - width), packed.dtype)
    for copy in copies[1:]:
        copy.wait()
    packed[:, width : width + top] = routes_in[...].astype(jnp.float32).astype(packed.dtype)
    packed[:, width + top : width + 2 * top] = numerators_in[...].astype(jnp.float32).astype(packed.dtype)
    copies[0].wait()


def pack(tokens, routes, numerators):
    count, width = tokens.shape
    return pl.pallas_call(
        pack_kernel,
        out_shape=jax.ShapeDtypeStruct((count, width + 128), tokens.dtype),
        in_specs=[HBM] * 3,
        out_specs=VMEM,
        scratch_shapes=[
            pltpu.VMEM(routes.shape, routes.dtype),
            pltpu.VMEM(numerators.shape, numerators.dtype),
            pltpu.SemaphoreType.DMA((3,)),
        ],
        compiler_params=pltpu.CompilerParams(vmem_limit_bytes=4 << 20),
        cost_estimate=pl.CostEstimate(flops=20 * 10**9, bytes_accessed=4 * tokens.size, transcendentals=0),
    )(in_hbm(tokens), in_hbm(routes), in_hbm(numerators))


def piece_bounds(size, step, pieces):
    ends = [0]
    for piece in pieces:
        ends.append(ends[-1] + piece * step)
    return list(zip(ends, [*ends[1:], size]))


def gate_up_kernel(x, base, out, weights, sems):
    depth, _, columns = weights.shape
    step = 512
    bounds = piece_bounds(depth, step, PIECES)
    copies = {
        low: pltpu.make_async_copy(base.at[pl.ds(low, high - low)], weights.at[pl.ds(low, high - low)], sems.at[i])
        for i, (low, high) in enumerate(bounds)
    }
    for copy in copies.values():
        copy.start()
    row = lax.broadcasted_iota(jnp.int32, (128, 256), 0)
    column = lax.broadcasted_iota(jnp.int32, (128, 256), 1)
    spread = jnp.where(column // 2 == row, 1.0, 0.0).astype(jnp.bfloat16)
    is_odd = (lax.broadcasted_iota(jnp.int32, (1, 2 * step), 1) % 2).astype(jnp.float32)
    odd_mask, even_mask = is_odd.astype(jnp.bfloat16), (1.0 - is_odd).astype(jnp.bfloat16)
    count = x.shape[0]
    flat = weights.reshape(2 * depth, columns)
    total = jnp.zeros(out.shape, jnp.float32)
    for k in range(0, depth, step):
        stacked = jnp.concatenate([x[:, i : i + 128] for i in range(k, k + step, 128)])
        wide = jnp.dot(stacked, spread, preferred_element_type=jnp.float32).astype(jnp.bfloat16)
        wide = jnp.concatenate([wide[i : i + count] for i in range(0, stacked.shape[0], count)], axis=1)
        if k in copies:
            copies[k].wait()
        total += jnp.dot(
            jnp.concatenate([wide * even_mask, wide * odd_mask]), flat[2 * k : 2 * (k + step), :], preferred_element_type=jnp.float32
        )
    out[...] = total


def gate_up_product(x, base):
    depth, _, columns = base.shape
    return pl.pallas_call(
        gate_up_kernel,
        out_shape=jax.ShapeDtypeStruct((2 * x.shape[0], columns), jnp.float32),
        in_specs=[VMEM, HBM],
        out_specs=VMEM,
        scratch_shapes=[pltpu.VMEM(base.shape, base.dtype), pltpu.SemaphoreType.DMA((len(PIECES) + 1,))],
        compiler_params=pltpu.CompilerParams(vmem_limit_bytes=32 << 20),
        cost_estimate=pl.CostEstimate(
            flops=4 * x.shape[0] * depth * columns, bytes_accessed=2 * base.size, transcendentals=0
        ),
    )(x, in_hbm(base))


def part_kernel(bit, term, received, *refs):
    *outs, total = refs
    half = total.shape[0]
    size = half // 4
    me = lax.axis_index("tensor")
    core, flag = me % 2, (me // (2 * bit)) % 2
    total[...] = term[pl.ds(pl.multiple_of(core * half, half), half), :].astype(jnp.float32) + received[
        ...
    ].astype(jnp.float32)
    by_x = 1 - core
    sent = (core + by_x * 2 * (1 - flag), 3 - by_x * 2 * flag)
    kept = (by_x * 2 * flag, 2 * core + by_x * (2 * flag + 1))
    for blocks, out in zip((sent, kept), outs):
        rows = [total[pl.ds(pl.multiple_of(block * size, size), size), :] for block in blocks]
        out[...] = jnp.concatenate(rows).astype(out.dtype)


def add_and_part(term, received, bit):
    half, width = received.shape
    return pl.pallas_call(
        functools.partial(part_kernel, bit),
        out_shape=[jax.ShapeDtypeStruct((half // 2, width), term.dtype)] * 2,
        in_specs=[VMEM, VMEM],
        out_specs=[VMEM] * 2,
        scratch_shapes=[pltpu.VMEM((half, width), jnp.float32)],
        compiler_params=pltpu.CompilerParams(vmem_limit_bytes=16 << 20),
        cost_estimate=pl.CostEstimate(flops=0, bytes_accessed=6 * received.size, transcendentals=0),
    )(term, received)


def local(
    tokens,
    routes,
    numerators,
    place,
    base_in,
    base_down,
    delta_in,
    delta_mid,
    delta_down,
    delta_back,
):
    clusters = lax.axis_size("expert")
    members = lax.axis_size("tensor")
    me = lax.axis_index("tensor")
    cluster = lax.axis_index("expert")
    core = me % 2
    count, width = tokens.shape[1:]
    top = routes.shape[2]

    along, across = halves(clusters), halves(members // 2)
    shared, paired = along[: len(along) - len(across)], along[len(along) - len(across) :]

    packed = pack(tokens[0], routes[0], numerators[0])
    chips = members // 2
    pieces = {(0, 0): packed}
    for z in range(clusters - 1, 0, -1):
        pieces[0, z] = trade(packed, (z, 0), (z, 0))
    for x in range(1, chips):
        pieces[x, 0] = trade(packed, (0, 2 * x), (0, 2 * x))
    places = [(0, 0)]
    for mask in shared:
        places += [(x, z | mask) for x, z in places]
    for zbit, xbit in zip(paired, across):
        places += [(x, z | zbit) for x, z in places]
        places += [(x | xbit, z) for x, z in places]
    later = [z for x, z in places if x == 0 and z]
    rest = jnp.concatenate([pieces[0, z] for z in later])
    rest, *firsts = lax.optimization_barrier((rest, *(pieces[x, 0] for x in range(1, chips))))
    pieces.update({(x, 0): first for x, first in enumerate(firsts, 1)})
    for x in range(chips):
        received = trade(rest, (0, 2 * x), (0, 2 * x)) if x else rest
        for i, z in enumerate(later):
            pieces[x, z] = received[i * count : (i + 1) * count]
    segments = [(x, tuple(z for _, z in run)) for x, run in itertools.groupby(places, lambda place: place[0])]
    runs = {(x, zs): jnp.concatenate([pieces[x, z] for z in zs]) for x, zs in segments}
    for bit in across:
        flag = (me // (2 * bit)) % 2 == 1
        for x, zs in runs:
            if not x & bit:
                runs[x, zs], runs[x | bit, zs] = ordered(flag, runs[x, zs], runs[x | bit, zs])
    held = by_rows(jnp.concatenate([runs[segment] for segment in segments]))
    held = by_rows(jnp.concatenate(ordered(core == 1, held, trade(held, (0, 1), (0, 1)))))
    rows, code_table = lax.optimization_barrier((held, delta_in[0]))

    codes = jnp.dot(rows[:, :width], code_table, preferred_element_type=jnp.float32).astype(jnp.bfloat16)
    projected = gate_up_product(held, base_in[0])

    codes = jnp.stack([codes if m == 0 else trade(codes, (0, m), (0, m)) for m in range(members)])
    by_slot = jnp.stack([lax.dynamic_index_in_dim(codes, s ^ me, 0, keepdims=False) for s in range(members)])

    lifted = jnp.einsum("srk,skgf->srgf", by_slot, delta_mid[0], preferred_element_type=jnp.float32)
    total = held.shape[0]
    hidden = jax.nn.silu(projected[None, :total] + lifted[:, :, 0]) * (projected[None, total:] + lifted[:, :, 1])
    partial_codes = jnp.einsum(
        "srf,sfk->srk", hidden.astype(jnp.bfloat16), delta_down[0], preferred_element_type=jnp.float32
    ).astype(jnp.bfloat16)
    hidden, rows, partial_codes = lax.optimization_barrier((hidden, rows, partial_codes))
    side = by_rows(rows[:, width:])
    all_routes = side[:, :top].astype(jnp.int32)
    numerator = side[:, top : 2 * top].astype(jnp.float32)
    position = lookup(place, all_routes)
    weight = (2.5 * numerator / jnp.sum(numerator, axis=-1, keepdims=True)).astype(jnp.bfloat16)
    target = cluster * members + jnp.arange(members, dtype=jnp.int32)
    scale = jnp.sum(
        jnp.where(position[None] == target[:, None, None], weight[None].astype(jnp.float32), 0.0), axis=-1
    )
    hidden_sum = jnp.sum(scale[:, :, None] * hidden, axis=0).astype(jnp.bfloat16)

    by_core = partial_codes.reshape(chips, 2, *partial_codes.shape[1:])
    kept, sent = (lax.dynamic_index_in_dim(by_core, c, 1, keepdims=False) for c in (core, 1 - core))
    by_chip = add(kept, trade(sent, (0, 1), (0, 1)))
    chip = me // 2
    lowrank = lax.dynamic_index_in_dim(by_chip, chip, 0, keepdims=False).astype(jnp.float32)
    for m in range(1, chips):
        sent = lax.dynamic_index_in_dim(by_chip, chip ^ m, 0, keepdims=False)
        lowrank = lowrank + trade(sent, (0, 2 * m), (0, 2 * m)).astype(jnp.float32)
    own_scale = lax.dynamic_index_in_dim(scale, me, 0, keepdims=False)
    scaled = (own_scale[:, None] * lowrank).astype(jnp.bfloat16)

    base = jnp.dot(hidden_sum, base_down[0], preferred_element_type=jnp.float32)

    half, step = base.shape[0] // 2, width // CHUNKS
    outputs = []
    for c in range(CHUNKS):
        columns = slice(c * step, (c + 1) * step)
        term = jnp.dot(scaled, delta_back[0, :, columns], preferred_element_type=jnp.float32)
        term = (base[:, columns] + term).astype(jnp.bfloat16)
        sent = ordered(core == 1, term[half:], term[:half])[0]
        sent, kept = add_and_part(term, trade(sent, (0, 1), (0, 1)), across[-1])
        for i, (z, x) in enumerate(reversed(list(zip(paired, across)))):
            flag = (me // (2 * x)) % 2 == 1
            if i:
                size = total.shape[0] // 4
                blocks = [total[j * size : (j + 1) * size] for j in range(4)]
                inner = ordered(core == 1, blocks[1], blocks[2])
                kept, sent = ordered(
                    (core == 0) & flag,
                    jnp.concatenate([blocks[0], inner[0]]),
                    jnp.concatenate([inner[1], blocks[3]]),
                )
            total = add(kept, trade(sent, (0, 2 * x), (z, 0)))
            size = total.shape[0] // 2
            kept, sent = ordered((core == 1) & flag, total[:size], total[size:])
            total = add(kept, trade(sent, (z, 0), (0, 2 * x)))
        for mask in reversed(shared):
            size = total.shape[0] // 2
            total = add(total[:size], trade(total[size:], (mask, 0), (mask, 0)))
        outputs.append(total)
    return jnp.concatenate(outputs, axis=1)[None]


def solution(mesh):
    placed = (
        P(None, ("parts", "expert", "tensor"), None),
        P(None, ("parts", "expert", "tensor"), None),
        P(None, ("parts", "expert", "tensor"), None),
        P("parts"),
        P("expert", None, None, "tensor"),
        P("expert", "tensor", None),
        P(("expert", "tensor"), None, None),
        P("expert", None, None, None, "tensor"),
        P("expert", None, "tensor", None),
        P(("expert", "tensor"), None, None),
    )
    return jax.shard_map(
        local,
        mesh=mesh,
        in_specs=placed,
        out_specs=P(None, ("parts", "expert", "tensor"), None),
        check_vma=False,
    )
```

```python
import functools
import itertools

import jax
import jax.numpy as jnp
from jax import lax
from jax.experimental import pallas as pl
from jax.experimental.pallas import tpu as pltpu
from jax.experimental.layout import Layout, with_layout_constraint
from jax.sharding import PartitionSpec as P

CHUNKS = 2
PIECES = (1, 2, 4, 4)
VMEM = pl.BlockSpec(memory_space=pltpu.VMEM)
HBM = pl.BlockSpec(memory_space=pltpu.HBM)


def in_hbm(value):
    return pltpu.with_memory_space_constraint(value, pltpu.HBM)


def by_rows(value):
    return with_layout_constraint(value, Layout((0, 1)))


def lookup(table, index):
    keys = jnp.arange(table.shape[0], dtype=jnp.int32)
    return jnp.sum(jnp.where(index[..., None] == keys, table, 0), axis=-1)


def trade(value, even, odd):
    members = lax.axis_size("tensor")
    pairs = []
    for e in range(lax.axis_size("expert")):
        for t in range(members):
            along, across = odd if t % 2 else even
            pairs.append((e * members + t, (e ^ along) * members + (t ^ across)))
    return lax.ppermute(value, ("expert", "tensor"), pairs)


def halves(size):
    masks = []
    while size > 1:
        size //= 2
        masks.append(size)
    return masks


def ordered(flip, first, second):
    return jnp.where(flip, second, first), jnp.where(flip, first, second)


def add(kept, received):
    return (kept.astype(jnp.float32) + received.astype(jnp.float32)).astype(jnp.bfloat16)


def pack_kernel(tokens, routes, numerators, packed, routes_in, numerators_in, sems):
    width, top = tokens.shape[1], routes.shape[1]
    copies = [
        pltpu.make_async_copy(tokens, packed.at[:, pl.ds(0, width)], sems.at[0]),
        pltpu.make_async_copy(routes, routes_in, sems.at[1]),
        pltpu.make_async_copy(numerators, numerators_in, sems.at[2]),
    ]
    for copy in copies:
        copy.start()
    packed[:, width:] = jnp.zeros((packed.shape[0], packed.shape[1] - width), packed.dtype)
    for copy in copies[1:]:
        copy.wait()
    packed[:, width : width + top] = routes_in[...].astype(jnp.float32).astype(packed.dtype)
    packed[:, width + top : width + 2 * top] = numerators_in[...].astype(jnp.float32).astype(packed.dtype)
    copies[0].wait()


def pack(tokens, routes, numerators):
    count, width = tokens.shape
    return pl.pallas_call(
        pack_kernel,
        out_shape=jax.ShapeDtypeStruct((count, width + 128), tokens.dtype),
        in_specs=[HBM] * 3,
        out_specs=VMEM,
        scratch_shapes=[
            pltpu.VMEM(routes.shape, routes.dtype),
            pltpu.VMEM(numerators.shape, numerators.dtype),
            pltpu.SemaphoreType.DMA((3,)),
        ],
        compiler_params=pltpu.CompilerParams(vmem_limit_bytes=4 << 20),
        cost_estimate=pl.CostEstimate(flops=20 * 10**9, bytes_accessed=4 * tokens.size, transcendentals=0),
    )(in_hbm(tokens), in_hbm(routes), in_hbm(numerators))


def piece_bounds(size, step, pieces):
    ends = [0]
    for piece in pieces:
        ends.append(ends[-1] + piece * step)
    return list(zip(ends, [*ends[1:], size]))


def gate_up_kernel(x, base, out, weights, sems):
    depth, _, columns = weights.shape
    step = 512
    bounds = piece_bounds(depth, step, PIECES)
    copies = {
        low: pltpu.make_async_copy(base.at[pl.ds(low, high - low)], weights.at[pl.ds(low, high - low)], sems.at[i])
        for i, (low, high) in enumerate(bounds)
    }
    for copy in copies.values():
        copy.start()
    row = lax.broadcasted_iota(jnp.int32, (128, 256), 0)
    column = lax.broadcasted_iota(jnp.int32, (128, 256), 1)
    spread = jnp.where(column // 2 == row, 1.0, 0.0).astype(jnp.bfloat16)
    is_odd = (lax.broadcasted_iota(jnp.int32, (1, 2 * step), 1) % 2).astype(jnp.float32)
    odd_mask, even_mask = is_odd.astype(jnp.bfloat16), (1.0 - is_odd).astype(jnp.bfloat16)
    count = x.shape[0]
    flat = weights.reshape(2 * depth, columns)
    total = jnp.zeros(out.shape, jnp.float32)
    for k in range(0, depth, step):
        stacked = jnp.concatenate([x[:, i : i + 128] for i in range(k, k + step, 128)])
        wide = jnp.dot(stacked, spread, preferred_element_type=jnp.float32).astype(jnp.bfloat16)
        wide = jnp.concatenate([wide[i : i + count] for i in range(0, stacked.shape[0], count)], axis=1)
        if k in copies:
            copies[k].wait()
        total += jnp.dot(
            jnp.concatenate([wide * even_mask, wide * odd_mask]), flat[2 * k : 2 * (k + step), :], preferred_element_type=jnp.float32
        )
    out[...] = total


def gate_up_product(x, base):
    depth, _, columns = base.shape
    return pl.pallas_call(
        gate_up_kernel,
        out_shape=jax.ShapeDtypeStruct((2 * x.shape[0], columns), jnp.float32),
        in_specs=[VMEM, HBM],
        out_specs=VMEM,
        scratch_shapes=[pltpu.VMEM(base.shape, base.dtype), pltpu.SemaphoreType.DMA((len(PIECES) + 1,))],
        compiler_params=pltpu.CompilerParams(vmem_limit_bytes=32 << 20),
        cost_estimate=pl.CostEstimate(
            flops=4 * x.shape[0] * depth * columns, bytes_accessed=2 * base.size, transcendentals=0
        ),
    )(x, in_hbm(base))


def part_kernel(bit, term, received, *refs):
    *outs, total = refs
    half = total.shape[0]
    size = half // 4
    me = lax.axis_index("tensor")
    core, flag = me % 2, (me // (2 * bit)) % 2
    total[...] = term[pl.ds(pl.multiple_of(core * half, half), half), :].astype(jnp.float32) + received[
        ...
    ].astype(jnp.float32)
    by_x = 1 - core
    sent = (core + by_x * 2 * (1 - flag), 3 - by_x * 2 * flag)
    kept = (by_x * 2 * flag, 2 * core + by_x * (2 * flag + 1))
    for blocks, out in zip((sent, kept), outs):
        rows = [total[pl.ds(pl.multiple_of(block * size, size), size), :] for block in blocks]
        out[...] = jnp.concatenate(rows).astype(out.dtype)


def add_and_part(term, received, bit):
    half, width = received.shape
    return pl.pallas_call(
        functools.partial(part_kernel, bit),
        out_shape=[jax.ShapeDtypeStruct((half // 2, width), term.dtype)] * 2,
        in_specs=[VMEM, VMEM],
        out_specs=[VMEM] * 2,
        scratch_shapes=[pltpu.VMEM((half, width), jnp.float32)],
        compiler_params=pltpu.CompilerParams(vmem_limit_bytes=16 << 20),
        cost_estimate=pl.CostEstimate(flops=0, bytes_accessed=6 * received.size, transcendentals=0),
    )(term, received)


def local(
    tokens,
    routes,
    numerators,
    place,
    base_in,
    base_down,
    delta_in,
    delta_mid,
    delta_down,
    delta_back,
):
    clusters = lax.axis_size("expert")
    members = lax.axis_size("tensor")
    me = lax.axis_index("tensor")
    cluster = lax.axis_index("expert")
    core = me % 2
    count, width = tokens.shape[1:]
    top = routes.shape[2]

    along, across = halves(clusters), halves(members // 2)
    shared, paired = along[: len(along) - len(across)], along[len(along) - len(across) :]

    packed = pack(tokens[0], routes[0], numerators[0])
    chips = members // 2
    pieces = {(0, 0): packed}
    for z in range(clusters - 1, 0, -1):
        pieces[0, z] = trade(packed, (z, 0), (z, 0))
    for x in range(1, chips):
        pieces[x, 0] = trade(packed, (0, 2 * x), (0, 2 * x))
    places = [(0, 0)]
    for mask in shared:
        places += [(x, z | mask) for x, z in places]
    for zbit, xbit in zip(paired, across):
        places += [(x, z | zbit) for x, z in places]
        places += [(x | xbit, z) for x, z in places]
    later = [z for x, z in places if x == 0 and z]
    rest = jnp.concatenate([pieces[0, z] for z in later])
    rest, *firsts = lax.optimization_barrier((rest, *(pieces[x, 0] for x in range(1, chips))))
    pieces.update({(x, 0): first for x, first in enumerate(firsts, 1)})
    for x in range(chips):
        received = trade(rest, (0, 2 * x), (0, 2 * x)) if x else rest
        for i, z in enumerate(later):
            pieces[x, z] = received[i * count : (i + 1) * count]
    segments = [(x, tuple(z for _, z in run)) for x, run in itertools.groupby(places, lambda place: place[0])]
    runs = {(x, zs): jnp.concatenate([pieces[x, z] for z in zs]) for x, zs in segments}
    for bit in across:
        flag = (me // (2 * bit)) % 2 == 1
        for x, zs in runs:
            if not x & bit:
                runs[x, zs], runs[x | bit, zs] = ordered(flag, runs[x, zs], runs[x | bit, zs])
    held = by_rows(jnp.concatenate([runs[segment] for segment in segments]))
    held = by_rows(jnp.concatenate(ordered(core == 1, held, trade(held, (0, 1), (0, 1)))))
    rows, code_table = lax.optimization_barrier((held, delta_in[0]))

    codes = jnp.dot(rows[:, :width], code_table, preferred_element_type=jnp.float32).astype(jnp.bfloat16)
    projected = gate_up_product(held, base_in[0])

    side = by_rows(rows[:, width:])
    all_routes = side[:, :top].astype(jnp.int32)
    numerator = side[:, top : 2 * top].astype(jnp.float32)
    position = lookup(place, all_routes)
    weight = (2.5 * numerator / jnp.sum(numerator, axis=-1, keepdims=True)).astype(jnp.bfloat16)
    target = cluster * members + jnp.arange(members, dtype=jnp.int32)
    scale = jnp.sum(
        jnp.where(position[None] == target[:, None, None], weight[None].astype(jnp.float32), 0.0), axis=-1
    )

    codes = jnp.stack([codes if m == 0 else trade(codes, (0, m), (0, m)) for m in range(members)])
    by_slot = jnp.stack([lax.dynamic_index_in_dim(codes, s ^ me, 0, keepdims=False) for s in range(members)])

    lifted = jnp.einsum("srk,skgf->srgf", by_slot, delta_mid[0], preferred_element_type=jnp.float32)
    total = held.shape[0]
    hidden = jax.nn.silu(projected[None, :total] + lifted[:, :, 0]) * (projected[None, total:] + lifted[:, :, 1])
    hidden_sum = jnp.sum(scale[:, :, None] * hidden, axis=0).astype(jnp.bfloat16)
    partial_codes = jnp.einsum(
        "srf,sfk->srk", hidden.astype(jnp.bfloat16), delta_down[0], preferred_element_type=jnp.float32
    ).astype(jnp.bfloat16)
    by_core = partial_codes.reshape(chips, 2, *partial_codes.shape[1:])
    kept, sent = (lax.dynamic_index_in_dim(by_core, c, 1, keepdims=False) for c in (core, 1 - core))
    by_chip = add(kept, trade(sent, (0, 1), (0, 1)))
    chip = me // 2
    lowrank = lax.dynamic_index_in_dim(by_chip, chip, 0, keepdims=False).astype(jnp.float32)
    for m in range(1, chips):
        sent = lax.dynamic_index_in_dim(by_chip, chip ^ m, 0, keepdims=False)
        lowrank = lowrank + trade(sent, (0, 2 * m), (0, 2 * m)).astype(jnp.float32)
    own_scale = lax.dynamic_index_in_dim(scale, me, 0, keepdims=False)
    scaled = (own_scale[:, None] * lowrank).astype(jnp.bfloat16)

    base = jnp.dot(hidden_sum, base_down[0], preferred_element_type=jnp.float32)

    half, step = base.shape[0] // 2, width // CHUNKS
    outputs = []
    for c in range(CHUNKS):
        columns = slice(c * step, (c + 1) * step)
        term = jnp.dot(scaled, delta_back[0, :, columns], preferred_element_type=jnp.float32)
        term = (base[:, columns] + term).astype(jnp.bfloat16)
        sent = ordered(core == 1, term[half:], term[:half])[0]
        sent, kept = add_and_part(term, trade(sent, (0, 1), (0, 1)), across[-1])
        for i, (z, x) in enumerate(reversed(list(zip(paired, across)))):
            flag = (me // (2 * x)) % 2 == 1
            if i:
                size = total.shape[0] // 4
                blocks = [total[j * size : (j + 1) * size] for j in range(4)]
                inner = ordered(core == 1, blocks[1], blocks[2])
                kept, sent = ordered(
                    (core == 0) & flag,
                    jnp.concatenate([blocks[0], inner[0]]),
                    jnp.concatenate([inner[1], blocks[3]]),
                )
            total = add(kept, trade(sent, (0, 2 * x), (z, 0)))
            size = total.shape[0] // 2
            kept, sent = ordered((core == 1) & flag, total[:size], total[size:])
            total = add(kept, trade(sent, (z, 0), (0, 2 * x)))
        for mask in reversed(shared):
            size = total.shape[0] // 2
            total = add(total[:size], trade(total[size:], (mask, 0), (mask, 0)))
        outputs.append(total)
    return jnp.concatenate(outputs, axis=1)[None]


def solution(mesh):
    placed = (
        P(None, ("parts", "expert", "tensor"), None),
        P(None, ("parts", "expert", "tensor"), None),
        P(None, ("parts", "expert", "tensor"), None),
        P("parts"),
        P("expert", None, None, "tensor"),
        P("expert", "tensor", None),
        P(("expert", "tensor"), None, None),
        P("expert", None, None, None, "tensor"),
        P("expert", None, "tensor", None),
        P(("expert", "tensor"), None, None),
    )
    return jax.shard_map(
        local,
        mesh=mesh,
        in_specs=placed,
        out_specs=P(None, ("parts", "expert", "tensor"), None),
        check_vma=False,
    )
```

```python
import functools
import itertools

import jax
import jax.numpy as jnp
from jax import lax
from jax.experimental import pallas as pl
from jax.experimental.pallas import tpu as pltpu
from jax.experimental.layout import Layout, with_layout_constraint
from jax.sharding import PartitionSpec as P

CHUNKS = 2
PIECES = (1, 2, 4, 4)
VMEM = pl.BlockSpec(memory_space=pltpu.VMEM)
HBM = pl.BlockSpec(memory_space=pltpu.HBM)


def in_hbm(value):
    return pltpu.with_memory_space_constraint(value, pltpu.HBM)


def by_rows(value):
    return with_layout_constraint(value, Layout((0, 1)))


def trade(value, even, odd):
    members = lax.axis_size("tensor")
    pairs = []
    for e in range(lax.axis_size("expert")):
        for t in range(members):
            along, across = odd if t % 2 else even
            pairs.append((e * members + t, (e ^ along) * members + (t ^ across)))
    return lax.ppermute(value, ("expert", "tensor"), pairs)


def halves(size):
    masks = []
    while size > 1:
        size //= 2
        masks.append(size)
    return masks


def ordered(flip, first, second):
    return jnp.where(flip, second, first), jnp.where(flip, first, second)


def add(kept, received):
    return (kept.astype(jnp.float32) + received.astype(jnp.float32)).astype(jnp.bfloat16)


def pack_kernel(tokens, routes, numerators, place, packed, routes_in, numerators_in, place_in, sems):
    width, top = tokens.shape[1], routes.shape[1]
    copies = [
        pltpu.make_async_copy(tokens, packed.at[:, pl.ds(0, width)], sems.at[0]),
        pltpu.make_async_copy(routes, routes_in, sems.at[1]),
        pltpu.make_async_copy(numerators, numerators_in, sems.at[2]),
        pltpu.make_async_copy(place, place_in, sems.at[3]),
    ]
    for copy in copies:
        copy.start()
    for copy in copies[1:]:
        copy.wait()
    named = routes_in[...]
    position = jnp.zeros(named.shape, jnp.int32)
    for expert in range(place.shape[0]):
        position = jnp.where(named == expert, place_in[expert], position)
    numerator = numerators_in[...].astype(jnp.float32)
    weight = 2.5 * numerator / jnp.sum(numerator, axis=1, keepdims=True)
    column = lax.broadcasted_iota(jnp.int32, (packed.shape[0], packed.shape[1] - width), 1)
    table = jnp.zeros(column.shape, jnp.float32)
    for k in range(top):
        table += jnp.where(column == position[:, k : k + 1], weight[:, k : k + 1], 0.0)
    packed[:, width:] = table.astype(packed.dtype)
    copies[0].wait()


def pack(tokens, routes, numerators, place):
    count, width = tokens.shape
    return pl.pallas_call(
        pack_kernel,
        out_shape=jax.ShapeDtypeStruct((count, width + 128), tokens.dtype),
        in_specs=[HBM] * 4,
        out_specs=VMEM,
        scratch_shapes=[
            pltpu.VMEM(routes.shape, routes.dtype),
            pltpu.VMEM(numerators.shape, numerators.dtype),
            pltpu.SMEM(place.shape, place.dtype),
            pltpu.SemaphoreType.DMA((4,)),
        ],
        compiler_params=pltpu.CompilerParams(vmem_limit_bytes=4 << 20),
        cost_estimate=pl.CostEstimate(flops=20 * 10**9, bytes_accessed=4 * tokens.size, transcendentals=0),
    )(in_hbm(tokens), in_hbm(routes), in_hbm(numerators), in_hbm(place))


def piece_bounds(size, step, pieces):
    ends = [0]
    for piece in pieces:
        ends.append(ends[-1] + piece * step)
    return list(zip(ends, [*ends[1:], size]))


def gate_up_kernel(x, base, out, weights, sems):
    depth, _, columns = weights.shape
    step = 512
    bounds = piece_bounds(depth, step, PIECES)
    copies = {
        low: pltpu.make_async_copy(base.at[pl.ds(low, high - low)], weights.at[pl.ds(low, high - low)], sems.at[i])
        for i, (low, high) in enumerate(bounds)
    }
    for copy in copies.values():
        copy.start()
    row = lax.broadcasted_iota(jnp.int32, (128, 256), 0)
    column = lax.broadcasted_iota(jnp.int32, (128, 256), 1)
    spread = jnp.where(column // 2 == row, 1.0, 0.0).astype(jnp.bfloat16)
    is_odd = (lax.broadcasted_iota(jnp.int32, (1, 2 * step), 1) % 2).astype(jnp.float32)
    odd_mask, even_mask = is_odd.astype(jnp.bfloat16), (1.0 - is_odd).astype(jnp.bfloat16)
    count = x.shape[0]
    flat = weights.reshape(2 * depth, columns)
    total = jnp.zeros(out.shape, jnp.float32)
    for k in range(0, depth, step):
        stacked = jnp.concatenate([x[:, i : i + 128] for i in range(k, k + step, 128)])
        wide = jnp.dot(stacked, spread, preferred_element_type=jnp.float32).astype(jnp.bfloat16)
        wide = jnp.concatenate([wide[i : i + count] for i in range(0, stacked.shape[0], count)], axis=1)
        if k in copies:
            copies[k].wait()
        total += jnp.dot(
            jnp.concatenate([wide * even_mask, wide * odd_mask]), flat[2 * k : 2 * (k + step), :], preferred_element_type=jnp.float32
        )
    out[...] = total


def gate_up_product(x, base):
    depth, _, columns = base.shape
    return pl.pallas_call(
        gate_up_kernel,
        out_shape=jax.ShapeDtypeStruct((2 * x.shape[0], columns), jnp.float32),
        in_specs=[VMEM, HBM],
        out_specs=VMEM,
        scratch_shapes=[pltpu.VMEM(base.shape, base.dtype), pltpu.SemaphoreType.DMA((len(PIECES) + 1,))],
        compiler_params=pltpu.CompilerParams(vmem_limit_bytes=32 << 20),
        cost_estimate=pl.CostEstimate(
            flops=4 * x.shape[0] * depth * columns, bytes_accessed=2 * base.size, transcendentals=0
        ),
    )(x, in_hbm(base))


def part_kernel(bit, term, received, *refs):
    *outs, total = refs
    half = total.shape[0]
    size = half // 4
    me = lax.axis_index("tensor")
    core, flag = me % 2, (me // (2 * bit)) % 2
    total[...] = term[pl.ds(pl.multiple_of(core * half, half), half), :].astype(jnp.float32) + received[
        ...
    ].astype(jnp.float32)
    by_x = 1 - core
    sent = (core + by_x * 2 * (1 - flag), 3 - by_x * 2 * flag)
    kept = (by_x * 2 * flag, 2 * core + by_x * (2 * flag + 1))
    for blocks, out in zip((sent, kept), outs):
        rows = [total[pl.ds(pl.multiple_of(block * size, size), size), :] for block in blocks]
        out[...] = jnp.concatenate(rows).astype(out.dtype)


def add_and_part(term, received, bit):
    half, width = received.shape
    return pl.pallas_call(
        functools.partial(part_kernel, bit),
        out_shape=[jax.ShapeDtypeStruct((half // 2, width), term.dtype)] * 2,
        in_specs=[VMEM, VMEM],
        out_specs=[VMEM] * 2,
        scratch_shapes=[pltpu.VMEM((half, width), jnp.float32)],
        compiler_params=pltpu.CompilerParams(vmem_limit_bytes=16 << 20),
        cost_estimate=pl.CostEstimate(flops=0, bytes_accessed=6 * received.size, transcendentals=0),
    )(term, received)


def local(
    tokens,
    routes,
    numerators,
    place,
    base_in,
    base_down,
    delta_in,
    delta_mid,
    delta_down,
    delta_back,
):
    clusters = lax.axis_size("expert")
    members = lax.axis_size("tensor")
    me = lax.axis_index("tensor")
    cluster = lax.axis_index("expert")
    core = me % 2
    count, width = tokens.shape[1:]

    along, across = halves(clusters), halves(members // 2)
    shared, paired = along[: len(along) - len(across)], along[len(along) - len(across) :]

    packed = pack(tokens[0], routes[0], numerators[0], place)
    chips = members // 2
    pieces = {(0, 0): packed}
    for z in range(clusters - 1, 0, -1):
        pieces[0, z] = trade(packed, (z, 0), (z, 0))
    for x in range(1, chips):
        pieces[x, 0] = trade(packed, (0, 2 * x), (0, 2 * x))
    places = [(0, 0)]
    for mask in shared:
        places += [(x, z | mask) for x, z in places]
    for zbit, xbit in zip(paired, across):
        places += [(x, z | zbit) for x, z in places]
        places += [(x | xbit, z) for x, z in places]
    later = [z for x, z in places if x == 0 and z]
    rest = jnp.concatenate([pieces[0, z] for z in later])
    rest, *firsts = lax.optimization_barrier((rest, *(pieces[x, 0] for x in range(1, chips))))
    pieces.update({(x, 0): first for x, first in enumerate(firsts, 1)})
    for x in range(chips):
        received = trade(rest, (0, 2 * x), (0, 2 * x)) if x else rest
        for i, z in enumerate(later):
            pieces[x, z] = received[i * count : (i + 1) * count]
    segments = [(x, tuple(z for _, z in run)) for x, run in itertools.groupby(places, lambda place: place[0])]
    runs = {(x, zs): jnp.concatenate([pieces[x, z] for z in zs]) for x, zs in segments}
    for bit in across:
        flag = (me // (2 * bit)) % 2 == 1
        for x, zs in runs:
            if not x & bit:
                runs[x, zs], runs[x | bit, zs] = ordered(flag, runs[x, zs], runs[x | bit, zs])
    held = by_rows(jnp.concatenate([runs[segment] for segment in segments]))
    held = by_rows(jnp.concatenate(ordered(core == 1, held, trade(held, (0, 1), (0, 1)))))
    rows, code_table = lax.optimization_barrier((held, delta_in[0]))

    codes = jnp.dot(rows[:, :width], code_table, preferred_element_type=jnp.float32).astype(jnp.bfloat16)
    projected = gate_up_product(held, base_in[0])

    scale = lax.dynamic_slice_in_dim(rows[:, width:], cluster * members, members, axis=1)
    scale = scale.astype(jnp.float32).T

    codes = jnp.stack([codes if m == 0 else trade(codes, (0, m), (0, m)) for m in range(members)])
    by_slot = jnp.stack([lax.dynamic_index_in_dim(codes, s ^ me, 0, keepdims=False) for s in range(members)])

    lifted = jnp.einsum("srk,skgf->srgf", by_slot, delta_mid[0], preferred_element_type=jnp.float32)
    total = held.shape[0]
    hidden = jax.nn.silu(projected[None, :total] + lifted[:, :, 0]) * (projected[None, total:] + lifted[:, :, 1])
    hidden_sum = jnp.sum(scale[:, :, None] * hidden, axis=0).astype(jnp.bfloat16)
    partial_codes = jnp.einsum(
        "srf,sfk->srk", hidden.astype(jnp.bfloat16), delta_down[0], preferred_element_type=jnp.float32
    ).astype(jnp.bfloat16)
    by_core = partial_codes.reshape(chips, 2, *partial_codes.shape[1:])
    kept, sent = (lax.dynamic_index_in_dim(by_core, c, 1, keepdims=False) for c in (core, 1 - core))
    by_chip = add(kept, trade(sent, (0, 1), (0, 1)))
    chip = me // 2
    lowrank = lax.dynamic_index_in_dim(by_chip, chip, 0, keepdims=False).astype(jnp.float32)
    for m in range(1, chips):
        sent = lax.dynamic_index_in_dim(by_chip, chip ^ m, 0, keepdims=False)
        lowrank = lowrank + trade(sent, (0, 2 * m), (0, 2 * m)).astype(jnp.float32)
    own_scale = lax.dynamic_index_in_dim(scale, me, 0, keepdims=False)
    scaled = (own_scale[:, None] * lowrank).astype(jnp.bfloat16)

    base = jnp.dot(hidden_sum, base_down[0], preferred_element_type=jnp.float32)

    half, step = base.shape[0] // 2, width // CHUNKS
    outputs = []
    for c in range(CHUNKS):
        columns = slice(c * step, (c + 1) * step)
        term = jnp.dot(scaled, delta_back[0, :, columns], preferred_element_type=jnp.float32)
        term = (base[:, columns] + term).astype(jnp.bfloat16)
        sent = ordered(core == 1, term[half:], term[:half])[0]
        sent, kept = add_and_part(term, trade(sent, (0, 1), (0, 1)), across[-1])
        for i, (z, x) in enumerate(reversed(list(zip(paired, across)))):
            flag = (me // (2 * x)) % 2 == 1
            if i:
                size = total.shape[0] // 4
                blocks = [total[j * size : (j + 1) * size] for j in range(4)]
                inner = ordered(core == 1, blocks[1], blocks[2])
                kept, sent = ordered(
                    (core == 0) & flag,
                    jnp.concatenate([blocks[0], inner[0]]),
                    jnp.concatenate([inner[1], blocks[3]]),
                )
            total = add(kept, trade(sent, (0, 2 * x), (z, 0)))
            size = total.shape[0] // 2
            kept, sent = ordered((core == 1) & flag, total[:size], total[size:])
            total = add(kept, trade(sent, (z, 0), (0, 2 * x)))
        for mask in reversed(shared):
            size = total.shape[0] // 2
            total = add(total[:size], trade(total[size:], (mask, 0), (mask, 0)))
        outputs.append(total)
    return jnp.concatenate(outputs, axis=1)[None]


def solution(mesh):
    placed = (
        P(None, ("parts", "expert", "tensor"), None),
        P(None, ("parts", "expert", "tensor"), None),
        P(None, ("parts", "expert", "tensor"), None),
        P("parts"),
        P("expert", None, None, "tensor"),
        P("expert", "tensor", None),
        P(("expert", "tensor"), None, None),
        P("expert", None, None, None, "tensor"),
        P("expert", None, "tensor", None),
        P(("expert", "tensor"), None, None),
    )
    return jax.shard_map(
        local,
        mesh=mesh,
        in_specs=placed,
        out_specs=P(None, ("parts", "expert", "tensor"), None),
        check_vma=False,
    )
```

```python
import functools
import itertools

import jax
import jax.numpy as jnp
from jax import lax
from jax.experimental import pallas as pl
from jax.experimental.pallas import tpu as pltpu
from jax.experimental.layout import Layout, with_layout_constraint
from jax.sharding import PartitionSpec as P

CHUNKS = 2
PIECES = (1, 2, 4, 4)
DOWN_PIECES = (1, 3)
VMEM = pl.BlockSpec(memory_space=pltpu.VMEM)
HBM = pl.BlockSpec(memory_space=pltpu.HBM)


def in_hbm(value):
    return pltpu.with_memory_space_constraint(value, pltpu.HBM)


def by_rows(value):
    return with_layout_constraint(value, Layout((0, 1)))


def trade(value, even, odd):
    members = lax.axis_size("tensor")
    pairs = []
    for e in range(lax.axis_size("expert")):
        for t in range(members):
            along, across = odd if t % 2 else even
            pairs.append((e * members + t, (e ^ along) * members + (t ^ across)))
    return lax.ppermute(value, ("expert", "tensor"), pairs)


def halves(size):
    masks = []
    while size > 1:
        size //= 2
        masks.append(size)
    return masks


def ordered(flip, first, second):
    return jnp.where(flip, second, first), jnp.where(flip, first, second)


def add(kept, received):
    return (kept.astype(jnp.float32) + received.astype(jnp.float32)).astype(jnp.bfloat16)


def pack_kernel(tokens, routes, numerators, place, packed, routes_in, numerators_in, place_in, sems):
    width, top = tokens.shape[1], routes.shape[1]
    copies = [
        pltpu.make_async_copy(tokens, packed.at[:, pl.ds(0, width)], sems.at[0]),
        pltpu.make_async_copy(routes, routes_in, sems.at[1]),
        pltpu.make_async_copy(numerators, numerators_in, sems.at[2]),
        pltpu.make_async_copy(place, place_in, sems.at[3]),
    ]
    for copy in copies:
        copy.start()
    for copy in copies[1:]:
        copy.wait()
    named = routes_in[...]
    position = jnp.zeros(named.shape, jnp.int32)
    for expert in range(place.shape[0]):
        position = jnp.where(named == expert, place_in[expert], position)
    numerator = numerators_in[...].astype(jnp.float32)
    weight = 2.5 * numerator / jnp.sum(numerator, axis=1, keepdims=True)
    column = lax.broadcasted_iota(jnp.int32, (packed.shape[0], packed.shape[1] - width), 1)
    table = jnp.zeros(column.shape, jnp.float32)
    for k in range(top):
        table += jnp.where(column == position[:, k : k + 1], weight[:, k : k + 1], 0.0)
    packed[:, width:] = table.astype(packed.dtype)
    copies[0].wait()


def pack(tokens, routes, numerators, place):
    count, width = tokens.shape
    return pl.pallas_call(
        pack_kernel,
        out_shape=jax.ShapeDtypeStruct((count, width + 128), tokens.dtype),
        in_specs=[HBM] * 4,
        out_specs=VMEM,
        scratch_shapes=[
            pltpu.VMEM(routes.shape, routes.dtype),
            pltpu.VMEM(numerators.shape, numerators.dtype),
            pltpu.SMEM(place.shape, place.dtype),
            pltpu.SemaphoreType.DMA((4,)),
        ],
        compiler_params=pltpu.CompilerParams(vmem_limit_bytes=4 << 20),
        cost_estimate=pl.CostEstimate(flops=20 * 10**9, bytes_accessed=4 * tokens.size, transcendentals=0),
    )(in_hbm(tokens), in_hbm(routes), in_hbm(numerators), in_hbm(place))


def piece_bounds(size, step, pieces):
    ends = [0]
    for piece in pieces:
        ends.append(ends[-1] + piece * step)
    return list(zip(ends, [*ends[1:], size]))


def gate_up_kernel(x, base, out, weights, sems):
    depth, _, columns = weights.shape
    step = 512
    bounds = piece_bounds(depth, step, PIECES)
    copies = {
        low: pltpu.make_async_copy(base.at[pl.ds(low, high - low)], weights.at[pl.ds(low, high - low)], sems.at[i])
        for i, (low, high) in enumerate(bounds)
    }
    for copy in copies.values():
        copy.start()
    row = lax.broadcasted_iota(jnp.int32, (128, 256), 0)
    column = lax.broadcasted_iota(jnp.int32, (128, 256), 1)
    spread = jnp.where(column // 2 == row, 1.0, 0.0).astype(jnp.bfloat16)
    is_odd = (lax.broadcasted_iota(jnp.int32, (1, 2 * step), 1) % 2).astype(jnp.float32)
    odd_mask, even_mask = is_odd.astype(jnp.bfloat16), (1.0 - is_odd).astype(jnp.bfloat16)
    count = x.shape[0]
    flat = weights.reshape(2 * depth, columns)
    total = jnp.zeros(out.shape, jnp.float32)
    for k in range(0, depth, step):
        stacked = jnp.concatenate([x[:, i : i + 128] for i in range(k, k + step, 128)])
        wide = jnp.dot(stacked, spread, preferred_element_type=jnp.float32).astype(jnp.bfloat16)
        wide = jnp.concatenate([wide[i : i + count] for i in range(0, stacked.shape[0], count)], axis=1)
        if k in copies:
            copies[k].wait()
        total += jnp.dot(
            jnp.concatenate([wide * even_mask, wide * odd_mask]), flat[2 * k : 2 * (k + step), :], preferred_element_type=jnp.float32
        )
    out[...] = total


def gate_up_product(x, base):
    depth, _, columns = base.shape
    return pl.pallas_call(
        gate_up_kernel,
        out_shape=jax.ShapeDtypeStruct((2 * x.shape[0], columns), jnp.float32),
        in_specs=[VMEM, HBM],
        out_specs=VMEM,
        scratch_shapes=[pltpu.VMEM(base.shape, base.dtype), pltpu.SemaphoreType.DMA((len(PIECES) + 1,))],
        compiler_params=pltpu.CompilerParams(vmem_limit_bytes=32 << 20),
        cost_estimate=pl.CostEstimate(
            flops=4 * x.shape[0] * depth * columns, bytes_accessed=2 * base.size, transcendentals=0
        ),
    )(x, in_hbm(base))


def down_kernel(hidden, base, out, weights, sems):
    step = 1024
    copies = {
        low: pltpu.make_async_copy(
            base.at[:, pl.ds(low, high - low)], weights.at[:, pl.ds(low, high - low)], sems.at[i]
        )
        for i, (low, high) in enumerate(piece_bounds(base.shape[1], step, DOWN_PIECES))
    }
    for copy in copies.values():
        copy.start()
    for k in range(0, base.shape[1], step):
        if k in copies:
            copies[k].wait()
        part = pl.ds(k, step)
        out[:, part] = jnp.dot(hidden[...], weights[:, part], preferred_element_type=jnp.float32)


def down_product(hidden, base):
    rows, width = hidden.shape[0], base.shape[1]
    return pl.pallas_call(
        down_kernel,
        out_shape=jax.ShapeDtypeStruct((rows, width), jnp.float32),
        in_specs=[VMEM, HBM],
        out_specs=VMEM,
        scratch_shapes=[pltpu.VMEM(base.shape, base.dtype), pltpu.SemaphoreType.DMA((len(DOWN_PIECES) + 1,))],
        compiler_params=pltpu.CompilerParams(vmem_limit_bytes=16 << 20),
        cost_estimate=pl.CostEstimate(flops=2 * rows * base.size, bytes_accessed=2 * base.size, transcendentals=0),
    )(hidden, in_hbm(base))


def part_kernel(bit, term, received, *refs):
    *outs, total = refs
    half = total.shape[0]
    size = half // 4
    me = lax.axis_index("tensor")
    core, flag = me % 2, (me // (2 * bit)) % 2
    total[...] = term[pl.ds(pl.multiple_of(core * half, half), half), :].astype(jnp.float32) + received[
        ...
    ].astype(jnp.float32)
    by_x = 1 - core
    sent = (core + by_x * 2 * (1 - flag), 3 - by_x * 2 * flag)
    kept = (by_x * 2 * flag, 2 * core + by_x * (2 * flag + 1))
    for blocks, out in zip((sent, kept), outs):
        rows = [total[pl.ds(pl.multiple_of(block * size, size), size), :] for block in blocks]
        out[...] = jnp.concatenate(rows).astype(out.dtype)


def add_and_part(term, received, bit):
    half, width = received.shape
    return pl.pallas_call(
        functools.partial(part_kernel, bit),
        out_shape=[jax.ShapeDtypeStruct((half // 2, width), term.dtype)] * 2,
        in_specs=[VMEM, VMEM],
        out_specs=[VMEM] * 2,
        scratch_shapes=[pltpu.VMEM((half, width), jnp.float32)],
        compiler_params=pltpu.CompilerParams(vmem_limit_bytes=16 << 20),
        cost_estimate=pl.CostEstimate(flops=0, bytes_accessed=6 * received.size, transcendentals=0),
    )(term, received)


def local(
    tokens,
    routes,
    numerators,
    place,
    base_in,
    base_down,
    delta_in,
    delta_mid,
    delta_down,
    delta_back,
):
    clusters = lax.axis_size("expert")
    members = lax.axis_size("tensor")
    me = lax.axis_index("tensor")
    cluster = lax.axis_index("expert")
    core = me % 2
    count, width = tokens.shape[1:]

    along, across = halves(clusters), halves(members // 2)
    shared, paired = along[: len(along) - len(across)], along[len(along) - len(across) :]

    packed = pack(tokens[0], routes[0], numerators[0], place)
    chips = members // 2
    pieces = {(0, 0): packed}
    for z in range(clusters - 1, 0, -1):
        pieces[0, z] = trade(packed, (z, 0), (z, 0))
    for x in range(1, chips):
        pieces[x, 0] = trade(packed, (0, 2 * x), (0, 2 * x))
    places = [(0, 0)]
    for mask in shared:
        places += [(x, z | mask) for x, z in places]
    for zbit, xbit in zip(paired, across):
        places += [(x, z | zbit) for x, z in places]
        places += [(x | xbit, z) for x, z in places]
    later = [z for x, z in places if x == 0 and z]
    rest = jnp.concatenate([pieces[0, z] for z in later])
    rest, *firsts = lax.optimization_barrier((rest, *(pieces[x, 0] for x in range(1, chips))))
    pieces.update({(x, 0): first for x, first in enumerate(firsts, 1)})
    for x in range(chips):
        received = trade(rest, (0, 2 * x), (0, 2 * x)) if x else rest
        for i, z in enumerate(later):
            pieces[x, z] = received[i * count : (i + 1) * count]
    segments = [(x, tuple(z for _, z in run)) for x, run in itertools.groupby(places, lambda place: place[0])]
    runs = {(x, zs): jnp.concatenate([pieces[x, z] for z in zs]) for x, zs in segments}
    for bit in across:
        flag = (me // (2 * bit)) % 2 == 1
        for x, zs in runs:
            if not x & bit:
                runs[x, zs], runs[x | bit, zs] = ordered(flag, runs[x, zs], runs[x | bit, zs])
    held = by_rows(jnp.concatenate([runs[segment] for segment in segments]))
    held = by_rows(jnp.concatenate(ordered(core == 1, held, trade(held, (0, 1), (0, 1)))))
    rows, code_table = lax.optimization_barrier((held, delta_in[0]))

    codes = jnp.dot(rows[:, :width], code_table, preferred_element_type=jnp.float32).astype(jnp.bfloat16)
    projected = gate_up_product(held, base_in[0])

    scale = lax.dynamic_slice_in_dim(rows[:, width:], cluster * members, members, axis=1)
    scale = scale.astype(jnp.float32).T

    codes = jnp.stack([codes if m == 0 else trade(codes, (0, m), (0, m)) for m in range(members)])
    by_slot = jnp.stack([lax.dynamic_index_in_dim(codes, s ^ me, 0, keepdims=False) for s in range(members)])

    lifted = jnp.einsum("srk,skgf->srgf", by_slot, delta_mid[0], preferred_element_type=jnp.float32)
    total = held.shape[0]
    hidden = jax.nn.silu(projected[None, :total] + lifted[:, :, 0]) * (projected[None, total:] + lifted[:, :, 1])
    hidden_sum = jnp.sum(scale[:, :, None] * hidden, axis=0).astype(jnp.bfloat16)
    partial_codes = jnp.einsum(
        "srf,sfk->srk", hidden.astype(jnp.bfloat16), delta_down[0], preferred_element_type=jnp.float32
    ).astype(jnp.bfloat16)
    by_core = partial_codes.reshape(chips, 2, *partial_codes.shape[1:])
    kept, sent = (lax.dynamic_index_in_dim(by_core, c, 1, keepdims=False) for c in (core, 1 - core))
    by_chip = add(kept, trade(sent, (0, 1), (0, 1)))
    chip = me // 2
    lowrank = lax.dynamic_index_in_dim(by_chip, chip, 0, keepdims=False).astype(jnp.float32)
    for m in range(1, chips):
        sent = lax.dynamic_index_in_dim(by_chip, chip ^ m, 0, keepdims=False)
        lowrank = lowrank + trade(sent, (0, 2 * m), (0, 2 * m)).astype(jnp.float32)
    own_scale = lax.dynamic_index_in_dim(scale, me, 0, keepdims=False)
    scaled = (own_scale[:, None] * lowrank).astype(jnp.bfloat16)

    base = down_product(hidden_sum, base_down[0])

    half, step = base.shape[0] // 2, width // CHUNKS
    outputs = []
    for c in range(CHUNKS):
        columns = slice(c * step, (c + 1) * step)
        term = jnp.dot(scaled, delta_back[0, :, columns], preferred_element_type=jnp.float32)
        term = (base[:, columns] + term).astype(jnp.bfloat16)
        sent = ordered(core == 1, term[half:], term[:half])[0]
        sent, kept = add_and_part(term, trade(sent, (0, 1), (0, 1)), across[-1])
        for i, (z, x) in enumerate(reversed(list(zip(paired, across)))):
            flag = (me // (2 * x)) % 2 == 1
            if i:
                size = total.shape[0] // 4
                blocks = [total[j * size : (j + 1) * size] for j in range(4)]
                inner = ordered(core == 1, blocks[1], blocks[2])
                kept, sent = ordered(
                    (core == 0) & flag,
                    jnp.concatenate([blocks[0], inner[0]]),
                    jnp.concatenate([inner[1], blocks[3]]),
                )
            total = add(kept, trade(sent, (0, 2 * x), (z, 0)))
            size = total.shape[0] // 2
            kept, sent = ordered((core == 1) & flag, total[:size], total[size:])
            total = add(kept, trade(sent, (z, 0), (0, 2 * x)))
        for mask in reversed(shared):
            size = total.shape[0] // 2
            total = add(total[:size], trade(total[size:], (mask, 0), (mask, 0)))
        outputs.append(total)
    return jnp.concatenate(outputs, axis=1)[None]


def solution(mesh):
    placed = (
        P(None, ("parts", "expert", "tensor"), None),
        P(None, ("parts", "expert", "tensor"), None),
        P(None, ("parts", "expert", "tensor"), None),
        P("parts"),
        P("expert", None, None, "tensor"),
        P("expert", "tensor", None),
        P(("expert", "tensor"), None, None),
        P("expert", None, None, None, "tensor"),
        P("expert", None, "tensor", None),
        P(("expert", "tensor"), None, None),
    )
    return jax.shard_map(
        local,
        mesh=mesh,
        in_specs=placed,
        out_specs=P(None, ("parts", "expert", "tensor"), None),
        check_vma=False,
    )
```

```python
import functools
import itertools

import jax
import jax.numpy as jnp
from jax import lax
from jax.experimental import pallas as pl
from jax.experimental.pallas import tpu as pltpu
from jax.experimental.layout import Layout, with_layout_constraint
from jax.sharding import PartitionSpec as P

CHUNKS = 2
PIECES = (1, 3, 5)
DOWN_PIECES = (2,)
VMEM = pl.BlockSpec(memory_space=pltpu.VMEM)
HBM = pl.BlockSpec(memory_space=pltpu.HBM)


def in_hbm(value):
    return pltpu.with_memory_space_constraint(value, pltpu.HBM)


def by_rows(value):
    return with_layout_constraint(value, Layout((0, 1)))


def trade(value, even, odd):
    members = lax.axis_size("tensor")
    pairs = []
    for e in range(lax.axis_size("expert")):
        for t in range(members):
            along, across = odd if t % 2 else even
            pairs.append((e * members + t, (e ^ along) * members + (t ^ across)))
    return lax.ppermute(value, ("expert", "tensor"), pairs)


def halves(size):
    masks = []
    while size > 1:
        size //= 2
        masks.append(size)
    return masks


def ordered(flip, first, second):
    return jnp.where(flip, second, first), jnp.where(flip, first, second)


def add(kept, received):
    return (kept.astype(jnp.float32) + received.astype(jnp.float32)).astype(jnp.bfloat16)


def pack_kernel(tokens, routes, numerators, place, packed, routes_in, numerators_in, place_in, sems):
    width, top = tokens.shape[1], routes.shape[1]
    copies = [
        pltpu.make_async_copy(tokens, packed.at[:, pl.ds(0, width)], sems.at[0]),
        pltpu.make_async_copy(routes, routes_in, sems.at[1]),
        pltpu.make_async_copy(numerators, numerators_in, sems.at[2]),
        pltpu.make_async_copy(place, place_in, sems.at[3]),
    ]
    for copy in copies:
        copy.start()
    for copy in copies[1:]:
        copy.wait()
    named = routes_in[...]
    position = jnp.zeros(named.shape, jnp.int32)
    for expert in range(place.shape[0]):
        position = jnp.where(named == expert, place_in[expert], position)
    numerator = numerators_in[...].astype(jnp.float32)
    weight = 2.5 * numerator / jnp.sum(numerator, axis=1, keepdims=True)
    column = lax.broadcasted_iota(jnp.int32, (packed.shape[0], packed.shape[1] - width), 1)
    table = jnp.zeros(column.shape, jnp.float32)
    for k in range(top):
        table += jnp.where(column == position[:, k : k + 1], weight[:, k : k + 1], 0.0)
    packed[:, width:] = table.astype(packed.dtype)
    copies[0].wait()


def pack(tokens, routes, numerators, place):
    count, width = tokens.shape
    return pl.pallas_call(
        pack_kernel,
        out_shape=jax.ShapeDtypeStruct((count, width + 128), tokens.dtype),
        in_specs=[HBM] * 4,
        out_specs=VMEM,
        scratch_shapes=[
            pltpu.VMEM(routes.shape, routes.dtype),
            pltpu.VMEM(numerators.shape, numerators.dtype),
            pltpu.SMEM(place.shape, place.dtype),
            pltpu.SemaphoreType.DMA((4,)),
        ],
        compiler_params=pltpu.CompilerParams(vmem_limit_bytes=4 << 20),
        cost_estimate=pl.CostEstimate(flops=20 * 10**9, bytes_accessed=4 * tokens.size, transcendentals=0),
    )(in_hbm(tokens), in_hbm(routes), in_hbm(numerators), in_hbm(place))


def piece_bounds(size, step, pieces):
    ends = [0]
    for piece in pieces:
        ends.append(ends[-1] + piece * step)
    return list(zip(ends, [*ends[1:], size]))


def gate_up_kernel(x, base, out, weights, sems):
    depth, _, columns = weights.shape
    step = 512
    bounds = piece_bounds(depth, step, PIECES)
    copies = {
        low: pltpu.make_async_copy(base.at[pl.ds(low, high - low)], weights.at[pl.ds(low, high - low)], sems.at[i])
        for i, (low, high) in enumerate(bounds)
    }
    for copy in copies.values():
        copy.start()
    row = lax.broadcasted_iota(jnp.int32, (128, 256), 0)
    column = lax.broadcasted_iota(jnp.int32, (128, 256), 1)
    spread = jnp.where(column // 2 == row, 1.0, 0.0).astype(jnp.bfloat16)
    is_odd = (lax.broadcasted_iota(jnp.int32, (1, 2 * step), 1) % 2).astype(jnp.float32)
    odd_mask, even_mask = is_odd.astype(jnp.bfloat16), (1.0 - is_odd).astype(jnp.bfloat16)
    count = x.shape[0]
    flat = weights.reshape(2 * depth, columns)
    total = jnp.zeros(out.shape, jnp.float32)
    for k in range(0, depth, step):
        stacked = jnp.concatenate([x[:, i : i + 128] for i in range(k, k + step, 128)])
        wide = jnp.dot(stacked, spread, preferred_element_type=jnp.float32).astype(jnp.bfloat16)
        wide = jnp.concatenate([wide[i : i + count] for i in range(0, stacked.shape[0], count)], axis=1)
        if k in copies:
            copies[k].wait()
        total += jnp.dot(
            jnp.concatenate([wide * even_mask, wide * odd_mask]), flat[2 * k : 2 * (k + step), :], preferred_element_type=jnp.float32
        )
    out[...] = total


def gate_up_product(x, base):
    depth, _, columns = base.shape
    return pl.pallas_call(
        gate_up_kernel,
        out_shape=jax.ShapeDtypeStruct((2 * x.shape[0], columns), jnp.float32),
        in_specs=[VMEM, HBM],
        out_specs=VMEM,
        scratch_shapes=[pltpu.VMEM(base.shape, base.dtype), pltpu.SemaphoreType.DMA((len(PIECES) + 1,))],
        compiler_params=pltpu.CompilerParams(vmem_limit_bytes=32 << 20),
        cost_estimate=pl.CostEstimate(
            flops=4 * x.shape[0] * depth * columns, bytes_accessed=2 * base.size, transcendentals=0
        ),
    )(x, in_hbm(base))


def down_kernel(hidden, base, out, weights, sems):
    step = 1024
    copies = {
        low: pltpu.make_async_copy(
            base.at[:, pl.ds(low, high - low)], weights.at[:, pl.ds(low, high - low)], sems.at[i]
        )
        for i, (low, high) in enumerate(piece_bounds(base.shape[1], step, DOWN_PIECES))
    }
    for copy in copies.values():
        copy.start()
    for k in range(0, base.shape[1], step):
        if k in copies:
            copies[k].wait()
        part = pl.ds(k, step)
        out[:, part] = jnp.dot(hidden[...], weights[:, part], preferred_element_type=jnp.float32)


def down_product(hidden, base):
    rows, width = hidden.shape[0], base.shape[1]
    return pl.pallas_call(
        down_kernel,
        out_shape=jax.ShapeDtypeStruct((rows, width), jnp.float32),
        in_specs=[VMEM, HBM],
        out_specs=VMEM,
        scratch_shapes=[pltpu.VMEM(base.shape, base.dtype), pltpu.SemaphoreType.DMA((len(DOWN_PIECES) + 1,))],
        compiler_params=pltpu.CompilerParams(vmem_limit_bytes=16 << 20),
        cost_estimate=pl.CostEstimate(flops=2 * rows * base.size, bytes_accessed=2 * base.size, transcendentals=0),
    )(hidden, in_hbm(base))


def part_kernel(bit, term, received, *refs):
    *outs, total = refs
    half = total.shape[0]
    size = half // 4
    me = lax.axis_index("tensor")
    core, flag = me % 2, (me // (2 * bit)) % 2
    total[...] = term[pl.ds(pl.multiple_of(core * half, half), half), :].astype(jnp.float32) + received[
        ...
    ].astype(jnp.float32)
    by_x = 1 - core
    sent = (core + by_x * 2 * (1 - flag), 3 - by_x * 2 * flag)
    kept = (by_x * 2 * flag, 2 * core + by_x * (2 * flag + 1))
    for blocks, out in zip((sent, kept), outs):
        rows = [total[pl.ds(pl.multiple_of(block * size, size), size), :] for block in blocks]
        out[...] = jnp.concatenate(rows).astype(out.dtype)


def add_and_part(term, received, bit):
    half, width = received.shape
    return pl.pallas_call(
        functools.partial(part_kernel, bit),
        out_shape=[jax.ShapeDtypeStruct((half // 2, width), term.dtype)] * 2,
        in_specs=[VMEM, VMEM],
        out_specs=[VMEM] * 2,
        scratch_shapes=[pltpu.VMEM((half, width), jnp.float32)],
        compiler_params=pltpu.CompilerParams(vmem_limit_bytes=16 << 20),
        cost_estimate=pl.CostEstimate(flops=0, bytes_accessed=6 * received.size, transcendentals=0),
    )(term, received)


def local(
    tokens,
    routes,
    numerators,
    place,
    base_in,
    base_down,
    delta_in,
    delta_mid,
    delta_down,
    delta_back,
):
    clusters = lax.axis_size("expert")
    members = lax.axis_size("tensor")
    me = lax.axis_index("tensor")
    cluster = lax.axis_index("expert")
    core = me % 2
    count, width = tokens.shape[1:]

    along, across = halves(clusters), halves(members // 2)
    shared, paired = along[: len(along) - len(across)], along[len(along) - len(across) :]

    packed = pack(tokens[0], routes[0], numerators[0], place)
    chips = members // 2
    pieces = {(0, 0): packed}
    for z in range(clusters - 1, 0, -1):
        pieces[0, z] = trade(packed, (z, 0), (z, 0))
    for x in range(1, chips):
        pieces[x, 0] = trade(packed, (0, 2 * x), (0, 2 * x))
    places = [(0, 0)]
    for mask in shared:
        places += [(x, z | mask) for x, z in places]
    for zbit, xbit in zip(paired, across):
        places += [(x, z | zbit) for x, z in places]
        places += [(x | xbit, z) for x, z in places]
    later = [z for x, z in places if x == 0 and z]
    rest = jnp.concatenate([pieces[0, z] for z in later])
    rest, *firsts = lax.optimization_barrier((rest, *(pieces[x, 0] for x in range(1, chips))))
    pieces.update({(x, 0): first for x, first in enumerate(firsts, 1)})
    for x in range(chips):
        received = trade(rest, (0, 2 * x), (0, 2 * x)) if x else rest
        for i, z in enumerate(later):
            pieces[x, z] = received[i * count : (i + 1) * count]
    segments = [(x, tuple(z for _, z in run)) for x, run in itertools.groupby(places, lambda place: place[0])]
    runs = {(x, zs): jnp.concatenate([pieces[x, z] for z in zs]) for x, zs in segments}
    for bit in across:
        flag = (me // (2 * bit)) % 2 == 1
        for x, zs in runs:
            if not x & bit:
                runs[x, zs], runs[x | bit, zs] = ordered(flag, runs[x, zs], runs[x | bit, zs])
    held = by_rows(jnp.concatenate([runs[segment] for segment in segments]))
    held = by_rows(jnp.concatenate(ordered(core == 1, held, trade(held, (0, 1), (0, 1)))))
    rows, code_table = lax.optimization_barrier((held, delta_in[0]))

    codes = jnp.dot(rows[:, :width], code_table, preferred_element_type=jnp.float32).astype(jnp.bfloat16)
    projected = gate_up_product(held, base_in[0])

    scale = lax.dynamic_slice_in_dim(rows[:, width:], cluster * members, members, axis=1)
    scale = scale.astype(jnp.float32).T

    codes = jnp.stack([codes if m == 0 else trade(codes, (0, m), (0, m)) for m in range(members)])
    by_slot = jnp.stack([lax.dynamic_index_in_dim(codes, s ^ me, 0, keepdims=False) for s in range(members)])

    lifted = jnp.einsum("srk,skgf->srgf", by_slot, delta_mid[0], preferred_element_type=jnp.float32)
    total = held.shape[0]
    hidden = jax.nn.silu(projected[None, :total] + lifted[:, :, 0]) * (projected[None, total:] + lifted[:, :, 1])
    hidden_sum = jnp.sum(scale[:, :, None] * hidden, axis=0).astype(jnp.bfloat16)
    partial_codes = jnp.einsum(
        "srf,sfk->srk", hidden.astype(jnp.bfloat16), delta_down[0], preferred_element_type=jnp.float32
    ).astype(jnp.bfloat16)
    by_core = partial_codes.reshape(chips, 2, *partial_codes.shape[1:])
    kept, sent = (lax.dynamic_index_in_dim(by_core, c, 1, keepdims=False) for c in (core, 1 - core))
    by_chip = add(kept, trade(sent, (0, 1), (0, 1)))
    chip = me // 2
    lowrank = lax.dynamic_index_in_dim(by_chip, chip, 0, keepdims=False).astype(jnp.float32)
    for m in range(1, chips):
        sent = lax.dynamic_index_in_dim(by_chip, chip ^ m, 0, keepdims=False)
        lowrank = lowrank + trade(sent, (0, 2 * m), (0, 2 * m)).astype(jnp.float32)
    own_scale = lax.dynamic_index_in_dim(scale, me, 0, keepdims=False)
    scaled = (own_scale[:, None] * lowrank).astype(jnp.bfloat16)

    base = down_product(hidden_sum, base_down[0])

    half, step = base.shape[0] // 2, width // CHUNKS
    outputs = []
    for c in range(CHUNKS):
        columns = slice(c * step, (c + 1) * step)
        term = jnp.dot(scaled, delta_back[0, :, columns], preferred_element_type=jnp.float32)
        term = (base[:, columns] + term).astype(jnp.bfloat16)
        sent = ordered(core == 1, term[half:], term[:half])[0]
        sent, kept = add_and_part(term, trade(sent, (0, 1), (0, 1)), across[-1])
        for i, (z, x) in enumerate(reversed(list(zip(paired, across)))):
            flag = (me // (2 * x)) % 2 == 1
            if i:
                size = total.shape[0] // 4
                blocks = [total[j * size : (j + 1) * size] for j in range(4)]
                inner = ordered(core == 1, blocks[1], blocks[2])
                kept, sent = ordered(
                    (core == 0) & flag,
                    jnp.concatenate([blocks[0], inner[0]]),
                    jnp.concatenate([inner[1], blocks[3]]),
                )
            total = add(kept, trade(sent, (0, 2 * x), (z, 0)))
            size = total.shape[0] // 2
            kept, sent = ordered((core == 1) & flag, total[:size], total[size:])
            total = add(kept, trade(sent, (z, 0), (0, 2 * x)))
        for mask in reversed(shared):
            size = total.shape[0] // 2
            total = add(total[:size], trade(total[size:], (mask, 0), (mask, 0)))
        outputs.append(total)
    return jnp.concatenate(outputs, axis=1)[None]


def solution(mesh):
    placed = (
        P(None, ("parts", "expert", "tensor"), None),
        P(None, ("parts", "expert", "tensor"), None),
        P(None, ("parts", "expert", "tensor"), None),
        P("parts"),
        P("expert", None, None, "tensor"),
        P("expert", "tensor", None),
        P(("expert", "tensor"), None, None),
        P("expert", None, None, None, "tensor"),
        P("expert", None, "tensor", None),
        P(("expert", "tensor"), None, None),
    )
    return jax.shard_map(
        local,
        mesh=mesh,
        in_specs=placed,
        out_specs=P(None, ("parts", "expert", "tensor"), None),
        check_vma=False,
    )
```
